32 devices in a mesh: gz: 4 (over y, x), xy: 8 (over z, core).
Axes of the slice: x: 2, y: 2, z: 4, core: 2. Of those that a mesh axis runs over, the one named last changes fastest.
Arguments:
- velocity: float32 [3, 64, 256, 128], P(None, 'gz', 'xy'), may hold values from -6 to 6
- viscosity: float32 [64, 256, 128], P('gz', 'xy'), may hold values from 0.4 to 2
- frac: float32 [256, 3, 128], P(('gz', 'xy')), may hold values from 0 to 1
- force: float32 [256, 3, 128], P(('gz', 'xy')), may hold values from -24 to 24
- target: int32 [256, 1], P(('gz', 'xy')), may hold values from 0 to 7; in each aligned block of 8 rows (0 to 7, 8 to 15, ...) at most 2 rows name the same one
- z_offset: int32 [256], P(('gz', 'xy')), may hold values from -4 to 12
- y_offset: int32 [256], P(('gz', 'xy')), may hold values from -4 to 28
Outputs:
- new_velocity: float32 [3, 64, 256, 128], P(None, 'gz', 'xy')
- point_velocity: float32 [256, 3, 128], P(('gz', 'xy'))
The draws below stay inside these ranges and needn't reach their ends.
Inputs may be any that keep to these rules, and one draw needn't show every extreme that they name: Among the 8 blocks stored on one device, no value of target occurs more than 2 times, and some device's blocks hold one value exactly 2 times.
All inputs are finite; a program needn't handle non-finite values.
Results may differ from the reference program's by a relative error of at most 0.0003.
Values sent between devices are 32-bit elements; how exact they have to be, the bound alone decides.
A program may use at most 64 MiB of HBM per device.

```python
import math
import jax
import jax.numpy as jnp
import numpy as np
from jax import lax

CZ = 16
CY = 32
NX = 128
NB_DEV = 8
PB = 128
BOX = 8
CAP = 2
COLUMNS = 8
NZ = 64
NY = 256
NB = 256


def place_ends(entries, key, low, largest):
    spot = [jax.random.randint(jax.random.fold_in(key, axis), (), 0, length) for axis, length in enumerate(entries.shape)]
    widest = entries.shape.index(max(entries.shape))
    beside = spot[:widest] + [(spot[widest] + 1) % entries.shape[widest]] + spot[widest + 1:]
    return entries.at[tuple(spot)].set(low).at[tuple(beside)].set(largest)


def levels(stream_key, extent, shards, low, high):
    factor_of = 1.0
    for dim, parts in shards:
        draws = jax.random.uniform(jax.random.fold_in(jax.random.fold_in(stream_key, 6), dim), (parts,), jnp.float32, low / len(shards), high / len(shards))
        factor_of = factor_of * jnp.repeat(jnp.exp(draws), extent[dim] // parts).reshape((-1,) + (1,) * (len(extent) - 1 - dim))
    return factor_of


def assign_block(key, own, number, rows, number_of, top, most, skew):
    order = jax.random.permutation(key, number_of)
    crowded, usual = shares(number_of, rows * top, most, skew, True), shares(number_of, rows * top, most, skew, False)
    places = jnp.arange(number_of)

    def named(tallies, rotation):
        used = int((tallies > 0).sum())
        fixed = max(1, used // 4)
        moved = fixed + (places - fixed + rotation * (used - fixed)) % max(1, number_of - fixed)
        return jnp.zeros((number_of,), jnp.int32).at[order[jnp.where(places < fixed, places, moved)]].set(jnp.asarray(tallies, jnp.int32))

    tallies = jnp.where(number % 4 == 0, named(crowded, number // 4), named(usual, number - number // 4 - 1))
    mixed = jax.random.permutation(jax.random.fold_in(own, 3), number_of)
    giver, sink = mixed[0:number_of // 2 * 2:2], mixed[1:number_of // 2 * 2:2]
    room = jnp.minimum(tallies[giver] - 1, most - tallies[sink]) // 2
    room = jnp.where((giver == order[0]) | (sink == order[0]) | (tallies[sink] == 0), 0, jnp.maximum(room, 0))
    moved = jax.random.randint(jax.random.fold_in(own, 4), (number_of // 2,), 0, 1 << 20) % (room + 1)
    tallies = tallies.at[giver].add(-moved).at[sink].add(moved)
    members = jnp.searchsorted(jnp.cumsum(tallies), jnp.arange(rows * top), side="right").astype(jnp.int32)
    listing = members.reshape(top, rows).T
    listing = listing[jax.random.permutation(jax.random.fold_in(own, 1), rows)]
    rotation = jax.random.randint(jax.random.fold_in(own, 2), (rows, 1), 0, top)
    return jnp.take_along_axis(listing, (jnp.arange(top)[None, :] + rotation) % top, axis=1)


def shares(number_of, total, most, skew, full):
    portions = [(1 << 20) // math.isqrt(standing ** skew) + 1 for standing in range(1, number_of + 1)]
    largest = most if full else min(most, max(-(-total // number_of), total * portions[0] // sum(portions)))
    least = 1 if total - largest >= number_of - 1 else 0
    counts, spare = [largest] + [least] * (number_of - 1), total - largest - least * (number_of - 1)
    while spare > 0:
        free = [i for i in range(1, number_of) if counts[i] < largest] or [i for i in range(1, number_of) if counts[i] < most]
        whole, left = sum([portions[i] for i in free]), spare
        for i in free:
            extra = min(most - counts[i], max(1, left * portions[i] // whole), spare)
            counts[i] = counts[i] + extra
            spare = spare - extra
    return np.array(counts)


def gaussian(own_key, extent, spread, most, cuts=(), kind=jnp.bfloat16):
    values = jax.random.normal(own_key, extent, jnp.float32) * spread
    if len(cuts) > 0:
        values = levels(own_key, extent, cuts, -0.22, 0.18) * values
    return jnp.clip(values, min=-most, max=most).astype(kind)


def setup_inputs(seed: int = 0) -> dict:
    keys = jax.random.split(jax.random.key(seed), 8)
    velocity = gaussian(keys[0], (3, NZ, NY, NX), 1.0, 6.0, ((1, 4), (2, 8)), jnp.float32)
    viscosity = jnp.clip(jnp.exp(math.log(2.0) - 1.609438 * jax.random.uniform(keys[1], (NZ, NY, NX), jnp.float32) ** levels(keys[1], (NZ, NY, NX), ((0, 4), (1, 8)), -0.2, 0.2)), 0.4, 2.0)
    frac = jnp.clip(1.0 * jax.random.uniform(keys[2], (NB, 3, PB), jnp.float32) ** levels(keys[2], (NB, 3, PB), ((0, 32),), -0.2, 0.2), 0.0, 1.0)
    force = gaussian(keys[3], (NB, 3, PB), 4.0, 24.0, ((0, 32),), jnp.float32)
    target_keys = jax.random.split(jax.random.fold_in(keys[4], 1), NB // NB_DEV)
    target_turns = jax.random.permutation(jax.random.fold_in(keys[4], 3), NB // NB_DEV)
    target = jax.vmap(lambda own, number: assign_block(jax.random.fold_in(keys[4], 2), own, number, NB_DEV, COLUMNS, 1, CAP, 2))(target_keys, target_turns).reshape((NB, 1))
    z_offset = place_ends(jax.random.randint(keys[5], (NB,), -4, CZ - BOX + 5), jax.random.fold_in(keys[5], 1), -4, (CZ - BOX + 5) - 1).astype(jnp.int32)
    y_offset = place_ends(jax.random.randint(keys[6], (NB,), -4, CY - BOX + 5), jax.random.fold_in(keys[6], 1), -4, (CY - BOX + 5) - 1).astype(jnp.int32)
    return dict(velocity=velocity, viscosity=viscosity, frac=frac, force=force, target=target, z_offset=z_offset, y_offset=y_offset)


NEIGHBOURS = ((1, 0, 0), (-1, 0, 0), (0, 1, 0), (0, -1, 0), (0, 0, 1), (0, 0, -1))
rim_width = 4


def shifted(array, offset, depth, breadth, length):
    return array[:, 1 + offset[0]:1 + offset[0] + depth, 1 + offset[1]:1 + offset[1] + breadth, 1 + offset[2]:1 + offset[2] + length]


def sweep(vel_pad, visc_pad):
    vel_pad = jnp.pad(vel_pad, ((0, 0), (0, 0), (0, 0), (1, 1)))
    visc_pad = jnp.pad(visc_pad, ((0, 0), (0, 0), (0, 0), (1, 1)))
    depth = vel_pad.shape[1] - 2
    breadth = vel_pad.shape[2] - 2
    length = vel_pad.shape[3] - 2
    centre = shifted(vel_pad, (0, 0, 0), depth, breadth, length)
    visc_centre = shifted(visc_pad, (0, 0, 0), depth, breadth, length)
    total = jnp.zeros_like(centre)
    for offset in NEIGHBOURS:
        coeff = 0.5 * (visc_centre + shifted(visc_pad, offset, depth, breadth, length))
        total = total + coeff * (shifted(vel_pad, offset, depth, breadth, length) - centre)
    return centre + 0.08 * total


def peskin(radius):
    return jnp.where(jnp.abs(radius) < 2.0, 0.25 * (1.0 + jnp.cos(0.5 * jnp.pi * radius)), 0.0 * radius)


def kernel_weights(frac, cells):
    span = jnp.arange(BOX).astype(frac.dtype)
    line = jnp.arange(cells).astype(frac.dtype)
    pos_z = 2.0 + (BOX - 5) * frac[:, 0, :]
    pos_y = 2.0 + (BOX - 5) * frac[:, 1, :]
    pos_x = 2.0 + (cells - 5) * frac[:, 2, :]
    return peskin(pos_z[:, :, None] - span), peskin(pos_y[:, :, None] - span), peskin(pos_x[:, :, None] - line)


def box_index(z_base, y_base):
    steps = jnp.arange(BOX).astype(jnp.int32)
    z_index = (z_base.astype(jnp.int32)[:, None] + steps)[:, :, None]
    y_index = (y_base.astype(jnp.int32)[:, None] + steps)[:, None, :]
    return z_index, y_index


def spread_group(field, frac, force, z_base, y_base):
    weight_z, weight_y, weight_x = kernel_weights(frac, field.shape[3])
    coeff = force[:, :, None, None, :] * jnp.transpose(weight_z, (0, 2, 1))[:, None, :, None, :] * jnp.transpose(weight_y, (0, 2, 1))[:, None, None, :, :]
    boxes = jnp.einsum("kcabp,kpi->ckabi", coeff, weight_x, precision=lax.Precision.HIGHEST)
    z_index, y_index = box_index(z_base, y_base)
    return field.at[:, z_index, y_index, :].add(boxes)


def sample_group(field, frac, z_base, y_base):
    weight_z, weight_y, weight_x = kernel_weights(frac, field.shape[3])
    z_index, y_index = box_index(z_base, y_base)
    boxes = field[:, z_index, y_index, :]
    partial_sum = jnp.einsum("ckabi,kpi->kcabp", boxes, weight_x, precision=lax.Precision.HIGHEST)
    return jnp.einsum("kcabp,kpa,kpb->kcp", partial_sum, weight_z, weight_y, precision=lax.Precision.HIGHEST)


def grouped(array, group):
    return array.reshape((array.shape[0] // group, group) + array.shape[1:])


def spread_all(field, frac, force, z_base, y_base):
    group = math.gcd(frac.shape[0], 32)
    def step_fn(carry, items):
        return spread_group(carry, items[0], items[1], items[2], items[3]), None
    result, unused = lax.scan(step_fn, field, (grouped(frac, group), grouped(force, group), grouped(z_base, group), grouped(y_base, group)))
    return result


def sample_all(field, frac, z_base, y_base):
    group = math.gcd(frac.shape[0], 32)
    values = lax.map(lambda items: sample_group(field, items[0], items[1], items[2]), (grouped(frac, group), grouped(z_base, group), grouped(y_base, group)))
    return values.reshape((frac.shape[0],) + values.shape[2:])


def reference(velocity, viscosity, frac, force, target, z_offset, y_offset):
    padding = ((0, 0), (1, 1), (1, 1), (0, 0))
    visc_pad = jnp.pad(viscosity[None], padding)

    def both_sweeps(component):
        once = sweep(jnp.pad(component[None], padding), visc_pad)
        return sweep(jnp.pad(once, padding), visc_pad)[0]

    moved = lax.map(both_sweeps, velocity)
    owner = jnp.arange(NB).astype(jnp.int32) // NB_DEV
    slab = owner // COLUMNS
    z_base = slab * CZ + z_offset + rim_width
    y_base = target[:, 0] * CY + y_offset + rim_width
    rim = ((0, 0), (rim_width, rim_width), (rim_width, rim_width), (0, 0))
    empty = jnp.zeros((3, NZ + 2 * rim_width, NY + 2 * rim_width, NX), velocity.dtype)
    forcing = spread_all(empty, frac, force, z_base, y_base)[:, rim_width:-rim_width, rim_width:-rim_width, :]
    new_velocity = moved + forcing
    point_velocity = sample_all(jnp.pad(new_velocity, rim), frac, z_base, y_base)
    return new_velocity, point_velocity
```

```python
import functools

import jax
import jax.numpy as jnp
from jax import lax
from jax.experimental import pallas as pl
from jax.experimental.pallas import tpu as pltpu
from jax.sharding import PartitionSpec as P

BOX = 8
CAP = 2
FAR = 4096.0
ZP = 7
YP = 8
GROUP = 8
TOGETHER = 4
MESH = pl.DeviceIdType.MESH
VMEM_LIMIT = 24 * 1024 * 1024


def peers(gz, xy, rows, columns):
    def each(body):
        for dr in (-1, 0, 1):
            inside = jnp.logical_and(gz + dr >= 0, gz + dr < rows)

            @pl.when(inside)
            def _(dr=dr):
                for k in range(1 if dr == 0 else 0, columns):
                    column = xy + k
                    body(dr, jnp.where(column >= columns, column - columns, column))

    return each


def each_row(gz, rows, body):
    for dr in (-1, 0, 1):
        inside = jnp.logical_and(gz + dr >= 0, gz + dr < rows)
        pl.when(inside)(functools.partial(body, dr))


def greet(gz, xy, rows, columns):
    barrier = pltpu.get_barrier_semaphore()

    def signal(dr, column):
        pl.semaphore_signal(barrier, inc=1, device_id=(gz + dr, column), device_id_type=MESH)

    peers(gz, xy, rows, columns)(signal)
    near = (
        1 + (gz > 0).astype(jnp.int32) + (gz < rows - 1).astype(jnp.int32)
    )
    return lambda: pl.semaphore_wait(barrier, near * columns - 1)


def matches(target_ref, count, column):
    first, second = jnp.int32(-1), jnp.int32(-1)
    for j in range(count):
        hit = target_ref[j] == column
        second = jnp.where(jnp.logical_and(hit, jnp.logical_and(first >= 0, second < 0)), j, second)
        first = jnp.where(jnp.logical_and(hit, first < 0), j, first)
    return first, second


def laplace(centre, visc, z_low, z_high, y_low, y_high, coeffs, lane):
    length = centre.shape[-1]
    x_high = jnp.where(lane == length - 1, 0.0, pltpu.roll(centre, length - 1, 1))
    x_low = jnp.where(lane == 0, 0.0, pltpu.roll(centre, 1, 1))
    total = coeffs[0] * (z_high - centre) + coeffs[1] * (z_low - centre)
    total = total + coeffs[2] * (y_high - centre) + coeffs[3] * (y_low - centre)
    total = total + coeffs[4] * (x_high - centre) + coeffs[5] * (x_low - centre)
    return centre + 0.08 * total


def x_coeffs(visc, lane):
    length = visc.shape[-1]
    high = jnp.where(lane == length - 1, 0.0, pltpu.roll(visc, length - 1, 1))
    low = jnp.where(lane == 0, 0.0, pltpu.roll(visc, 1, 1))
    return 0.5 * (visc + high), 0.5 * (visc + low)


def exchange_kernel(
    rows, columns, target_ref, zoff_ref, yoff_ref, velocity_ref, viscosity_ref, frac_ref, force_ref,
    moved_ref, slots_ref, meta_ref,
    pad, once, staging, layers_out, layers_in, corner_out, corner_in,
    load_sem, ab_send, ab_recv, halo_send, halo_recv, corner_send, corner_recv, c_send, c_recv,
):
    gz, xy = lax.axis_index("gz"), lax.axis_index("xy")
    depth, breadth = velocity_ref.shape[1], velocity_ref.shape[2]
    length = velocity_ref.shape[3]
    wait_greeting = greet(gz, xy, rows, columns)
    loads = (
        pltpu.make_async_copy(
            velocity_ref, pad.at[0:3, 2 : 2 + depth, 8 : 8 + breadth], load_sem.at[0]
        ),
        pltpu.make_async_copy(
            viscosity_ref, pad.at[3, 2 : 2 + depth, 8 : 8 + breadth], load_sem.at[1]
        ),
    )
    for load in loads:
        load.start()

    lanes = lax.broadcasted_iota(jnp.int32, (1, length), 1)
    count = frac_ref.shape[1]

    def stage(column, unused):
        for rank, block in enumerate(matches(target_ref, count, column)):
            at = jnp.maximum(block, 0)
            there = block >= 0
            z = jnp.where(there, zoff_ref[at].astype(jnp.float32), FAR)
            y = jnp.where(there, yoff_ref[at].astype(jnp.float32), FAR)
            staging[column, rank, 0:3, :] = frac_ref[:, at, :]
            staging[column, rank, 3:6, :] = force_ref[:, at, :]
            staging[column, rank, 6:7, :] = jnp.where(lanes == 0, z, y)
            staging[column, rank, 7:8, :] = jnp.zeros((1, length), jnp.float32)
        return unused

    lax.fori_loop(0, columns, stage, 0)
    each_peer = peers(gz, xy, rows, columns)

    def block_copy(dr, column):
        return pltpu.make_async_remote_copy(
            src_ref=staging.at[column],
            dst_ref=slots_ref.at[0, 1 - dr, xy],
            send_sem=ab_send.at[dr + 1],
            recv_sem=ab_recv.at[1 - dr],
            device_id=(gz + dr, column),
            device_id_type=MESH,
        )

    def whole_row(dr):
        span = pl.ds(0, columns - (1 if dr == 0 else 0))
        return pltpu.make_async_remote_copy(
            src_ref=staging.at[span],
            dst_ref=slots_ref.at[0, dr + 1, span],
            send_sem=ab_send.at[dr + 1],
            recv_sem=ab_recv.at[dr + 1],
            device_id=(gz, xy),
            device_id_type=MESH,
        )

    wait_greeting()
    each_peer(lambda dr, column: block_copy(dr, column).start())
    slots_ref[0, 1, xy] = staging[xy]

    has = (gz > 0, gz < rows - 1, xy > 0, xy < columns - 1)
    device = ((gz - 1, xy), (gz + 1, xy), (gz, xy - 1), (gz, xy + 1))
    own_y = slice(8, 8 + breadth)
    own_z = slice(2, 2 + depth)

    def halo_copies(side):
        if side == 0:
            cut, land = slice(0, 2), (slice(2 + depth, 4 + depth), own_y)
        elif side == 1:
            cut, land = slice(depth - 2, depth), (slice(0, 2), own_y)
        if side < 2:
            sources = (velocity_ref.at[:, cut], viscosity_ref.at[cut])
            lands = (pad.at[(slice(0, 3),) + land], pad.at[(3,) + land])
        else:
            sources, lands = (layers_out.at[side - 2],), (layers_in.at[3 - side],)
        return [
            pltpu.make_async_remote_copy(
                src_ref=source,
                dst_ref=spot,
                send_sem=halo_send.at[side, number],
                recv_sem=halo_recv.at[side, number],
                device_id=device[side],
                device_id_type=MESH,
            )
            for number, (source, spot) in enumerate(zip(sources, lands))
        ]

    def on_side(side, action):
        @pl.when(has[side])
        def _():
            for copy in halo_copies(side):
                action(copy)

    for side in (0, 1):
        on_side(side, lambda copy: copy.start())

    zeros_z = jnp.zeros((4, 2, breadth, length), jnp.float32)
    zeros_y = jnp.zeros((4, depth, 8, length), jnp.float32)

    @pl.when(gz == 0)
    def _():
        pad[:, 0:2, 8 : 8 + breadth, :] = zeros_z
        slots_ref[0, 0] = jnp.full(slots_ref.shape[2:], FAR, jnp.float32)

    @pl.when(gz == rows - 1)
    def _():
        pad[:, 2 + depth : 4 + depth, 8 : 8 + breadth, :] = zeros_z
        slots_ref[0, 2] = jnp.full(slots_ref.shape[2:], FAR, jnp.float32)

    @pl.when(xy == 0)
    def _():
        pad[:, 2 : 2 + depth, 0:8, :] = zeros_y
        slots_ref[1] = jnp.full(slots_ref.shape[1:], FAR, jnp.float32)

    @pl.when(xy == columns - 1)
    def _():
        pad[:, 2 : 2 + depth, 8 + breadth : 16 + breadth, :] = zeros_y
        slots_ref[2] = jnp.full(slots_ref.shape[1:], FAR, jnp.float32)

    for load in loads:
        load.wait()
    for side, start in ((2, 8), (3, 6 + breadth)):
        for part in range(4):
            for layer in range(2):
                layers_out[side - 2, part, layer * depth : (layer + 1) * depth, :] = pad[
                    part, 2 : 2 + depth, start + layer, :
                ]
        on_side(side, lambda copy: copy.start())

    corners = []
    for number, (dz, dy) in enumerate(((-1, -1), (-1, 1), (1, -1), (1, 1))):
        z_in = 2 if dz < 0 else 1 + depth
        y_in = 8 if dy < 0 else 7 + breadth
        z_out = 1 if dz < 0 else 2 + depth
        y_out = 7 if dy < 0 else 8 + breadth
        present = jnp.logical_and(has[0 if dz < 0 else 1], has[2 if dy < 0 else 3])
        for part in range(4):
            corner_out[number, part : part + 1, :] = pad[part, z_in, y_in : y_in + 1, :]
        copy = pltpu.make_async_remote_copy(
            src_ref=corner_out.at[number],
            dst_ref=corner_in.at[3 - number],
            send_sem=corner_send.at[number],
            recv_sem=corner_recv.at[3 - number],
            device_id=(gz + dz, xy + dy),
            device_id_type=MESH,
        )
        arrival = pltpu.make_async_remote_copy(
            src_ref=corner_out.at[number],
            dst_ref=corner_in.at[number],
            send_sem=corner_send.at[number],
            recv_sem=corner_recv.at[number],
            device_id=(gz + dz, xy + dy),
            device_id_type=MESH,
        )
        corners.append((present, copy, arrival, number, z_out, y_out))
    for present, copy, arrival, number, z_out, y_out in corners:
        pl.when(present)(lambda copy=copy: copy.start())

    lane = lax.broadcasted_iota(jnp.int32, (breadth + 16, length), 1)
    line = lax.broadcasted_iota(jnp.int32, (breadth + 16, length), 0)
    low_y = jnp.where(xy > 0, 0, 8)
    high_y = jnp.where(xy < columns - 1, breadth + 16, breadth + 8)
    in_grid = jnp.logical_and(line >= low_y, line < high_y)
    first_z = jnp.where(gz > 0, 0, 2)
    last_z = jnp.where(gz < rows - 1, depth + 3, depth + 1)

    def first_sweep(z):
        visc = pad[3, z]
        size = visc.shape[0]
        cx_high, cx_low = x_coeffs(visc, lane)
        coeffs = (
            0.5 * (visc + pad[3, z + 1]),
            0.5 * (visc + pad[3, z - 1]),
            0.5 * (visc + pltpu.roll(visc, size - 1, 0)),
            0.5 * (visc + pltpu.roll(visc, 1, 0)),
            cx_high,
            cx_low,
        )
        z_inside = jnp.logical_and(z >= first_z, z <= last_z)
        keep = jnp.logical_and(in_grid, z_inside)
        for part in range(3):
            centre = pad[part, z]
            new = laplace(
                centre, visc, pad[part, z - 1], pad[part, z + 1],
                pltpu.roll(centre, 1, 0), pltpu.roll(centre, size - 1, 0), coeffs, lane,
            )
            once[part, z - 1] = jnp.where(keep, new, 0.0)

    own_lane = lane[:breadth]

    def second_sweep(z):
        visc = pad[3, z, 8 : 8 + breadth, :]
        cx_high, cx_low = x_coeffs(visc, own_lane)
        coeffs = (
            0.5 * (visc + pad[3, z + 1, 8 : 8 + breadth, :]),
            0.5 * (visc + pad[3, z - 1, 8 : 8 + breadth, :]),
            0.5 * (visc + pad[3, z, 9 : 9 + breadth, :]),
            0.5 * (visc + pad[3, z, 7 : 7 + breadth, :]),
            cx_high,
            cx_low,
        )
        for part in range(3):
            moved_ref[part, z - 2] = laplace(
                once[part, z - 1, 8 : 8 + breadth, :], visc,
                once[part, z - 2, 8 : 8 + breadth, :], once[part, z, 8 : 8 + breadth, :],
                once[part, z - 1, 7 : 7 + breadth, :], once[part, z - 1, 9 : 9 + breadth, :],
                coeffs, own_lane,
            )

    def loop(low, high, body):
        def step(z, unused):
            body(z)
            return unused

        lax.fori_loop(low, high, step, 0)

    arrives = ((1, 0), (0, 1), (3, 2), (2, 3))

    def wait_side(side, neighbour):
        @pl.when(has[neighbour])
        def _():
            for copy in halo_copies(side):
                copy.wait_recv()
            if side >= 2:
                start = 6 if side == 3 else 8 + breadth
                for part in range(4):
                    for layer in range(2):
                        pad[part, 2 : 2 + depth, start + layer, :] = layers_in[
                            3 - side, part, layer * depth : (layer + 1) * depth, :
                        ]

    forwards = []
    for number, (there, column, side) in enumerate(((has[3], xy + 1, 1), (has[2], xy - 1, 2))):
        for dr in (-1, 0, 1):
            copy = pltpu.make_async_remote_copy(
                src_ref=slots_ref.at[0, dr + 1],
                dst_ref=slots_ref.at[side, dr + 1],
                send_sem=c_send.at[number, dr + 1],
                recv_sem=c_recv.at[number, dr + 1],
                device_id=(gz, column),
                device_id_type=MESH,
            )
            forwards.append((there, copy, dr, has[2 + number]))

    def forward(row):
        for there, copy, dr, unused in forwards:
            if dr == row:
                pl.when(there)(lambda copy=copy: copy.start())

    whole_row(0).wait_recv()
    forward(0)
    wait_side(2, 3)
    wait_side(3, 2)
    loop(3, 3 + depth // 4, first_sweep)
    for dr in (-1, 1):
        pl.when(has[0 if dr < 0 else 1])(lambda dr=dr: whole_row(dr).wait_recv())
        forward(dr)
    loop(3 + depth // 4, 1 + depth, first_sweep)

    wait_side(0, 1)
    wait_side(1, 0)
    for present, copy, arrival, number, z_out, y_out in corners:

        @pl.when(present)
        def _(arrival=arrival, number=number, z_out=z_out, y_out=y_out):
            arrival.wait_recv()
            for part in range(4):
                pad[part, z_out, y_out : y_out + 1, :] = corner_in[number, part : part + 1, :]

        @pl.when(jnp.logical_not(present))
        def _(z_out=z_out, y_out=y_out):
            for part in range(4):
                pad[part, z_out, y_out : y_out + 1, :] = jnp.zeros((1, length), jnp.float32)

    for z in (1, 2, 1 + depth, 2 + depth):
        first_sweep(z)
    loop(2, 2 + depth, second_sweep)

    for unused, copy, dr, comes in forwards:
        pl.when(comes)(lambda copy=copy: copy.wait_recv())
    for side in range(3):
        for dr in range(3):
            shift = jnp.where(lanes == 0, (dr - 1) * depth, (0, -breadth, breadth)[side])
            for column in range(columns):
                at = ((side * 3 + dr) * columns + column) * CAP
                for rank in range(CAP):
                    row = slots_ref[side, dr, column, rank, 6:7, :].astype(jnp.int32)
                    meta_ref[at + rank : at + rank + 1, :] = row + shift

    each_row(gz, rows, lambda dr: whole_row(dr).wait_send())
    for side in range(4):
        on_side(side, lambda copy: copy.wait_send())
    for present, copy, arrival, number, z_out, y_out in corners:
        pl.when(present)(lambda copy=copy: copy.wait_send())
    for there, copy, unused, comes in forwards:
        pl.when(there)(lambda copy=copy: copy.wait_send())


def phi(radius):
    x2 = radius * radius * 0.6168502750680849
    c = 1.0 / 479001600.0
    for factor in (-1.0 / 3628800.0, 1.0 / 40320.0, -1.0 / 720.0, 1.0 / 24.0, -0.5, 1.0):
        c = c * x2 + factor
    return jnp.where(jnp.abs(radius) < 2.0, 0.5 * c * c, 0.0)


def split(value):
    high = value.astype(jnp.bfloat16)
    return high, (value - high.astype(jnp.float32)).astype(jnp.bfloat16)


def product(left, right, contract):
    dims = (((1,), (contract,)), ((), ()))
    dot = functools.partial(
        lax.dot_general, dimension_numbers=dims, preferred_element_type=jnp.float32
    )
    (left_high, left_low), (right_high, right_low) = left, right
    return dot(left_high, right_high) + dot(left_high, right_low) + dot(left_low, right_high)


def points_kernel(
    columns, meta_ref, slots_ref, moved_ref, new_ref, partial_ref, field, wx_high, wx_low, listed, load_sem, store_sem
):
    depth, breadth, length = moved_ref.shape[1:]
    inner = field.at[:, ZP : ZP + depth, YP : YP + breadth]
    load = pltpu.make_async_copy(moved_ref, inner, load_sem)
    load.start()
    total_z = field.shape[1]
    field[:, 0:ZP] = jnp.zeros((3, ZP) + field.shape[2:], jnp.float32)
    field[:, ZP + depth :] = jnp.zeros((3, total_z - ZP - depth) + field.shape[2:], jnp.float32)
    field[:, ZP : ZP + depth, 0:YP] = jnp.zeros((3, depth, YP, length), jnp.float32)
    field[:, ZP : ZP + depth, YP + breadth :] = jnp.zeros(
        (3, depth, field.shape[2] - YP - breadth, length), jnp.float32
    )
    partial_ref[...] = jnp.zeros_like(partial_ref)
    slot_count = meta_ref.shape[0]

    def list_some(group, found):
        for number in range(GROUP):
            slot = group * GROUP + number
            z, y = meta_ref[slot, 0], meta_ref[slot, 1]
            meets = (z > -BOX) & (z < depth) & (y > -BOX) & (y < breadth)
            listed[found] = slot
            found = found + meets.astype(jnp.int32)
        return found

    found = lax.fori_loop(0, slot_count // GROUP, list_some, jnp.int32(0))
    rounds = (found + TOGETHER - 1) // TOGETHER
    load.wait()

    line = lax.broadcasted_iota(jnp.int32, (BOX, length), 0)
    rel = line.astype(jnp.float32)
    far = lax.broadcasted_iota(jnp.int32, (length, length), 0).astype(jnp.float32)

    def members(number):
        for other in range(TOGETHER):
            at = number * TOGETHER + other
            slot = listed[jnp.minimum(at, found - 1)]
            yield at, at < found, slot, meta_ref[slot, 0], meta_ref[slot, 1]

    def near_weights(tile, z, y):
        wz = phi(2.0 + (BOX - 5) * tile[0:1] - rel)
        wy = phi(2.0 + (BOX - 5) * tile[1:2] - rel)
        wz = jnp.where((z + line >= 0) & (z + line < depth), wz, 0.0)
        wy = jnp.where((y + line >= 0) & (y + line < breadth), wy, 0.0)
        return wz, wy

    def box_of(z, y):
        return (slice(None), pl.ds(z + ZP, BOX), pl.ds(y + YP, BOX), slice(None))

    def spread(number, unused):
        adds = []
        for at, counts, slot, z, y in members(number):
            tile = slots_ref[slot]
            wz, wy = near_weights(tile, z, y)
            wy = jnp.where(counts, wy, 0.0)
            wx = split(phi(2.0 + (length - 5) * tile[2:3] - far))
            wx_high[at], wx_low[at] = wx
            pulled = tile[3:6][:, None, :] * wz[None]
            coeff = pulled[:, :, None, :] * wy[None, None]
            boxes = product(split(coeff.reshape(3 * BOX * BOX, length)), wx, 1)
            adds.append((box_of(z, y), boxes.reshape(3, BOX, BOX, length)))
        for box, boxes in adds:
            field[box] = field[box] + boxes
        return unused

    lax.fori_loop(0, rounds, spread, 0)
    store = pltpu.make_async_copy(inner, new_ref, store_sem)
    store.start()

    def sample(number, unused):
        results = []
        for at, counts, slot, z, y in members(number):
            wz, wy = near_weights(slots_ref[slot], z, y)
            cells = field[box_of(z, y)].reshape(3 * BOX * BOX, length)
            taken = product(split(cells), (wx_high[at], wx_low[at]), 0)
            taken = taken.reshape(3, BOX, BOX, length)
            summed = jnp.sum(taken * wz[None, :, None, :], axis=1)
            results.append((slot, jnp.sum(summed * wy[None], axis=1)))
        for slot, values in results:
            partial_ref[slot // CAP, pl.ds(3 * lax.rem(slot, CAP), 3), :] = values
        return unused

    lax.fori_loop(0, rounds, sample, 0)
    store.wait()


def return_kernel(
    rows, columns, target_ref, partial_ref, out_ref,
    side_in, summed, gathered, c_send, c_recv, ab_send, ab_recv,
):
    gz, xy = lax.axis_index("gz"), lax.axis_index("xy")
    wait_greeting = greet(gz, xy, rows, columns)
    wait_greeting()
    has_low, has_high = xy > 0, xy < columns - 1
    copies = []
    for number, (there, column) in enumerate(((has_low, xy - 1), (has_high, xy + 1))):
        copy = pltpu.make_async_remote_copy(
            src_ref=partial_ref.at[number + 1],
            dst_ref=side_in.at[1 - number],
            send_sem=c_send.at[number],
            recv_sem=c_recv.at[1 - number],
            device_id=(gz, column),
            device_id_type=MESH,
        )
        arrival = pltpu.make_async_remote_copy(
            src_ref=partial_ref.at[number + 1],
            dst_ref=side_in.at[number],
            send_sem=c_send.at[number],
            recv_sem=c_recv.at[number],
            device_id=(gz, column),
            device_id_type=MESH,
        )
        copies.append((there, copy))
        pl.when(there)(lambda copy=copy: copy.start())

        @pl.when(jnp.logical_not(there))
        def _(number=number):
            side_in[number] = jnp.zeros(side_in.shape[1:], jnp.float32)

        copies[-1] = (there, copy, arrival)
    for there, copy, arrival in copies:
        pl.when(there)(lambda arrival=arrival: arrival.wait_recv())
    summed[...] = partial_ref[0] + side_in[0] + side_in[1]

    each_peer = peers(gz, xy, rows, columns)

    def block_copy(dr, column):
        return pltpu.make_async_remote_copy(
            src_ref=summed.at[dr + 1, column],
            dst_ref=gathered.at[1 - dr, xy],
            send_sem=ab_send.at[dr + 1],
            recv_sem=ab_recv.at[1 - dr],
            device_id=(gz + dr, column),
            device_id_type=MESH,
        )

    def whole_row(dr):
        span = pl.ds(0, columns - (1 if dr == 0 else 0))
        return pltpu.make_async_remote_copy(
            src_ref=summed.at[dr + 1, span],
            dst_ref=gathered.at[dr + 1, span],
            send_sem=ab_send.at[dr + 1],
            recv_sem=ab_recv.at[dr + 1],
            device_id=(gz, xy),
            device_id_type=MESH,
        )

    each_peer(lambda dr, column: block_copy(dr, column).start())
    gathered[1, xy] = summed[1, xy]

    @pl.when(gz == 0)
    def _():
        gathered[0] = jnp.zeros(gathered.shape[1:], jnp.float32)

    @pl.when(gz == rows - 1)
    def _():
        gathered[2] = jnp.zeros(gathered.shape[1:], jnp.float32)

    each_row(gz, rows, lambda dr: whole_row(dr).wait_recv())
    count = out_ref.shape[1]
    for j in range(count):
        column = target_ref[j]
        rank = jnp.int32(0)
        for earlier in range(j):
            rank = rank + (target_ref[earlier] == column).astype(jnp.int32)
        tile = gathered[0, column] + gathered[1, column] + gathered[2, column]
        out_ref[:, j, :] = jnp.where(rank == 0, tile[0:3], tile[3:6])
    each_row(gz, rows, lambda dr: whole_row(dr).wait_send())
    for there, copy, arrival in copies:
        pl.when(there)(lambda copy=copy: copy.wait_send())


def shards(rows, columns, velocity, viscosity, frac, force, target, z_offset, y_offset):
    parts, depth, breadth, length = velocity.shape
    target = target.reshape(target.shape[0])
    frac, force = jnp.transpose(frac, (1, 0, 2)), jnp.transpose(force, (1, 0, 2))
    held = lambda array: pltpu.with_memory_space_constraint(array, pltpu.HBM)
    velocity, viscosity, frac, force = held(velocity), held(viscosity), held(frac), held(force)
    target, z_offset, y_offset = held(target), held(z_offset), held(y_offset)
    f32 = jnp.float32
    vmem = pl.BlockSpec(memory_space=pltpu.VMEM)
    smem = pl.BlockSpec(memory_space=pltpu.SMEM)
    hbm = pl.BlockSpec(memory_space=pltpu.HBM)
    anyw = pl.BlockSpec(memory_space=pl.ANY)
    dma = pltpu.SemaphoreType.DMA
    slot_count = 9 * columns * CAP
    moved, slots, meta = pl.pallas_call(
        functools.partial(exchange_kernel, rows, columns),
        out_shape=(
            jax.ShapeDtypeStruct(velocity.shape, f32),
            jax.ShapeDtypeStruct((3, 3, columns, CAP, 8, length), f32),
            jax.ShapeDtypeStruct((slot_count, length), jnp.int32),
        ),
        in_specs=[smem, smem, smem, hbm, hbm, vmem, vmem],
        out_specs=(vmem, vmem, vmem),
        scratch_shapes=[
            pltpu.VMEM((4, depth + 4, breadth + 16, length), f32),
            pltpu.VMEM((3, depth + 2, breadth + 16, length), f32),
            pltpu.VMEM((columns, CAP, 8, length), f32),
            pltpu.VMEM((2, 4, 2 * depth, length), f32),
            pltpu.VMEM((2, 4, 2 * depth, length), f32),
            pltpu.VMEM((4, 8, length), f32),
            pltpu.VMEM((4, 8, length), f32),
            dma((2,)), dma((3,)), dma((3,)), dma((4, 2)), dma((4, 2)),
            dma((4,)), dma((4,)), dma((2, 3)), dma((2, 3)),
        ],
        compiler_params=pltpu.CompilerParams(
            collective_id=0, has_side_effects=True, vmem_limit_bytes=VMEM_LIMIT
        ),
    )(target, z_offset, y_offset, velocity, viscosity, frac, force)

    new_velocity, partial = pl.pallas_call(
        functools.partial(points_kernel, columns),
        out_shape=(
            jax.ShapeDtypeStruct(velocity.shape, f32),
            jax.ShapeDtypeStruct((slot_count // CAP, 8, length), f32),
        ),
        in_specs=[smem, vmem, anyw],
        out_specs=(anyw, vmem),
        scratch_shapes=[
            pltpu.VMEM((3, depth + 2 * ZP, breadth + 2 * YP, length), f32),
            pltpu.VMEM((slot_count + TOGETHER, length, length), jnp.bfloat16),
            pltpu.VMEM((slot_count + TOGETHER, length, length), jnp.bfloat16),
            pltpu.SMEM((slot_count + 1,), jnp.int32),
            dma(()), dma(()),
        ],
        compiler_params=pltpu.CompilerParams(vmem_limit_bytes=VMEM_LIMIT),
    )(meta, slots.reshape(slot_count, 8, length), moved)

    point_velocity = pl.pallas_call(
        functools.partial(return_kernel, rows, columns),
        out_shape=jax.ShapeDtypeStruct(frac.shape, f32),
        in_specs=[smem, vmem],
        out_specs=vmem,
        scratch_shapes=[
            pltpu.VMEM((2, 3, columns, 8, length), f32),
            pltpu.VMEM((3, columns, 8, length), f32),
            pltpu.VMEM((3, columns, 8, length), f32),
            dma((2,)), dma((2,)), dma((3,)), dma((3,)),
        ],
        compiler_params=pltpu.CompilerParams(
            collective_id=1, has_side_effects=True, vmem_limit_bytes=VMEM_LIMIT
        ),
    )(target, partial.reshape(3, 3, columns, 8, length))
    return new_velocity, jnp.transpose(point_velocity, (1, 0, 2))


def solution(mesh):
    placed = (
        P(None, "gz", "xy", None),
        P("gz", "xy", None),
        P(("gz", "xy"), None, None),
        P(("gz", "xy"), None, None),
        P(("gz", "xy"), None),
        P(("gz", "xy")),
        P(("gz", "xy")),
    )
    return jax.shard_map(
        functools.partial(shards, mesh.shape["gz"], mesh.shape["xy"]),
        mesh=mesh,
        in_specs=placed,
        out_specs=(P(None, "gz", "xy", None), P(("gz", "xy"), None, None)),
        check_vma=False,
    )
```

```python
import functools

import jax
import jax.numpy as jnp
from jax import lax
from jax.experimental import pallas as pl
from jax.experimental.pallas import tpu as pltpu
from jax.sharding import PartitionSpec as P

BOX = 8
CAP = 2
FAR = 4096.0
ZP = 7
YP = 8
PAIR = 16
USED = 13
TOGETHER = 4
MESH = pl.DeviceIdType.MESH
VMEM_LIMIT = 24 * 1024 * 1024


def peers(gz, xy, rows, columns):
    def each(body):
        for dr in (-1, 0, 1):
            inside = jnp.logical_and(gz + dr >= 0, gz + dr < rows)

            @pl.when(inside)
            def _(dr=dr):
                for k in range(1 if dr == 0 else 0, columns):
                    column = xy + k
                    body(dr, jnp.where(column >= columns, column - columns, column))

    return each


def each_row(gz, rows, body):
    for dr in (-1, 0, 1):
        inside = jnp.logical_and(gz + dr >= 0, gz + dr < rows)
        pl.when(inside)(functools.partial(body, dr))


def greet(gz, xy, rows, columns):
    barrier = pltpu.get_barrier_semaphore()

    def signal(dr, column):
        pl.semaphore_signal(barrier, inc=1, device_id=(gz + dr, column), device_id_type=MESH)

    peers(gz, xy, rows, columns)(signal)
    near = (
        1 + (gz > 0).astype(jnp.int32) + (gz < rows - 1).astype(jnp.int32)
    )
    return lambda: pl.semaphore_wait(barrier, near * columns - 1)


def matches(target_ref, count, column):
    first, second = jnp.int32(-1), jnp.int32(-1)
    for j in range(count):
        hit = target_ref[j] == column
        second = jnp.where(jnp.logical_and(hit, jnp.logical_and(first >= 0, second < 0)), j, second)
        first = jnp.where(jnp.logical_and(hit, first < 0), j, first)
    return first, second


def laplace(centre, visc, z_low, z_high, y_low, y_high, coeffs, lane):
    length = centre.shape[-1]
    x_high = jnp.where(lane == length - 1, 0.0, pltpu.roll(centre, length - 1, 1))
    x_low = jnp.where(lane == 0, 0.0, pltpu.roll(centre, 1, 1))
    total = coeffs[0] * (z_high - centre) + coeffs[1] * (z_low - centre)
    total = total + coeffs[2] * (y_high - centre) + coeffs[3] * (y_low - centre)
    total = total + coeffs[4] * (x_high - centre) + coeffs[5] * (x_low - centre)
    return centre + 0.08 * total


def x_coeffs(visc, lane):
    length = visc.shape[-1]
    high = jnp.where(lane == length - 1, 0.0, pltpu.roll(visc, length - 1, 1))
    low = jnp.where(lane == 0, 0.0, pltpu.roll(visc, 1, 1))
    return 0.5 * (visc + high), 0.5 * (visc + low)


def make_list(depth, breadth, slots_ref, list_ref):
    columns, length = slots_ref.shape[2], slots_ref.shape[4]
    pairs, listed = 9 * columns, list_ref.shape[1]
    rows = slots_ref[:, :, :, USED - 1 : USED, :].reshape(pairs, length)
    number = lax.broadcasted_iota(jnp.int32, (pairs, length), 0)
    lane = lax.broadcasted_iota(jnp.int32, (pairs, length), 1)
    side, dr = number // (3 * columns), number // columns % 3
    shift_z = ((dr - 1) * depth).astype(jnp.float32)
    shift_y = jnp.where(side == 0, 0, jnp.where(side == 1, -breadth, breadth)).astype(jnp.float32)
    earlier = lax.broadcasted_iota(jnp.int32, (pairs, pairs), 0) > lax.broadcasted_iota(
        jnp.int32, (pairs, pairs), 1
    )
    earlier = earlier.astype(jnp.float32).astype(jnp.bfloat16)
    place = lax.broadcasted_iota(jnp.int32, (pairs, listed), 1)
    before = jnp.zeros((1, 1), jnp.float32)
    listing = jnp.zeros((length, listed), jnp.float32)
    for rank in range(CAP):
        z = rows[:, 2 * rank : 2 * rank + 1] + shift_z
        y = rows[:, 2 * rank + 1 : 2 * rank + 2] + shift_y
        meets = (z > -BOX) & (z < depth) & (y > -BOX) & (y < breadth)
        one = jnp.where(meets, 1.0, 0.0)
        rank_of = jnp.dot(earlier, one.astype(jnp.bfloat16), preferred_element_type=jnp.float32) + before
        spot = jnp.where(meets, rank_of, -1.0).astype(jnp.int32)
        chosen = jnp.where(place == spot[:, 0:1], 1.0, 0.0).astype(jnp.bfloat16)
        facts = jnp.where(lane == 0, z, jnp.where(lane == 1, y, jnp.where(lane == 2, number, 0).astype(jnp.float32)))
        facts = jnp.where(meets, jnp.where(lane == 3, float(rank), facts), 0.0).astype(jnp.bfloat16)
        listing = listing + lax.dot_general(
            facts, chosen, (((0,), (0,)), ((), ())), preferred_element_type=jnp.float32
        )
        before = before + jnp.sum(one[:, 0:1], axis=0, keepdims=True)
    list_ref[0:4, :] = listing[0:4].astype(jnp.int32)
    list_ref[4:8, :] = jnp.broadcast_to(before, (4, listed)).astype(jnp.int32)


def exchange_kernel(
    rows, columns, target_ref, zoff_ref, yoff_ref, velocity_ref, viscosity_ref, frac_ref, force_ref,
    field_ref, slots_ref, list_ref,
    pad, once, staging, layers_out, layers_in, corner_out, corner_in,
    load_sem, ab_send, ab_recv, halo_send, halo_recv, corner_send, corner_recv, c_send, c_recv,
):
    gz, xy = lax.axis_index("gz"), lax.axis_index("xy")
    depth, breadth = velocity_ref.shape[1], velocity_ref.shape[2]
    length = velocity_ref.shape[3]
    wait_greeting = greet(gz, xy, rows, columns)
    loads = (
        pltpu.make_async_copy(
            velocity_ref, pad.at[0:3, 2 : 2 + depth, 8 : 8 + breadth], load_sem.at[0]
        ),
        pltpu.make_async_copy(
            viscosity_ref, pad.at[3, 2 : 2 + depth, 8 : 8 + breadth], load_sem.at[1]
        ),
    )
    for load in loads:
        load.start()

    lanes = lax.broadcasted_iota(jnp.int32, (1, length), 1)
    count = frac_ref.shape[1]

    def stage(column, unused):
        row = jnp.full((1, length), FAR, jnp.float32)
        for rank, block in enumerate(matches(target_ref, count, column)):
            at = jnp.maximum(block, 0)
            there = block >= 0
            z = jnp.where(there, zoff_ref[at].astype(jnp.float32), FAR)
            y = jnp.where(there, yoff_ref[at].astype(jnp.float32), FAR)
            staging[column, 6 * rank : 6 * rank + 3, :] = frac_ref[:, at, :]
            staging[column, 6 * rank + 3 : 6 * rank + 6, :] = force_ref[:, at, :]
            row = jnp.where(lanes == 2 * rank, z, row)
            row = jnp.where(lanes == 2 * rank + 1, y, row)
        staging[column, 12:13, :] = row
        return unused

    lax.fori_loop(0, columns, stage, 0)
    each_peer = peers(gz, xy, rows, columns)

    def block_copy(dr, column):
        return pltpu.make_async_remote_copy(
            src_ref=staging.at[column, 0:USED],
            dst_ref=slots_ref.at[0, 1 - dr, xy, 0:USED],
            send_sem=ab_send.at[dr + 1],
            recv_sem=ab_recv.at[1 - dr],
            device_id=(gz + dr, column),
            device_id_type=MESH,
        )

    def whole_row(dr):
        span = pl.ds(0, columns - (1 if dr == 0 else 0))
        return pltpu.make_async_remote_copy(
            src_ref=staging.at[span, 0:USED],
            dst_ref=slots_ref.at[0, dr + 1, span, 0:USED],
            send_sem=ab_send.at[dr + 1],
            recv_sem=ab_recv.at[dr + 1],
            device_id=(gz, xy),
            device_id_type=MESH,
        )

    wait_greeting()
    each_peer(lambda dr, column: block_copy(dr, column).start())
    slots_ref[0, 1, xy, 0:USED] = staging[xy, 0:USED]

    has = (gz > 0, gz < rows - 1, xy > 0, xy < columns - 1)
    device = ((gz - 1, xy), (gz + 1, xy), (gz, xy - 1), (gz, xy + 1))
    own_y = slice(8, 8 + breadth)
    own_z = slice(2, 2 + depth)

    def halo_copies(side):
        if side == 0:
            cut, land = slice(0, 2), (slice(2 + depth, 4 + depth), own_y)
        elif side == 1:
            cut, land = slice(depth - 2, depth), (slice(0, 2), own_y)
        if side < 2:
            sources = (velocity_ref.at[:, cut], viscosity_ref.at[cut])
            lands = (pad.at[(slice(0, 3),) + land], pad.at[(3,) + land])
        else:
            sources, lands = (layers_out.at[side - 2],), (layers_in.at[3 - side],)
        return [
            pltpu.make_async_remote_copy(
                src_ref=source,
                dst_ref=spot,
                send_sem=halo_send.at[side, number],
                recv_sem=halo_recv.at[side, number],
                device_id=device[side],
                device_id_type=MESH,
            )
            for number, (source, spot) in enumerate(zip(sources, lands))
        ]

    def on_side(side, action):
        @pl.when(has[side])
        def _():
            for copy in halo_copies(side):
                action(copy)

    for side in (0, 1):
        on_side(side, lambda copy: copy.start())

    wide, high = field_ref.shape[2], field_ref.shape[1]
    field_ref[:, 0:ZP] = jnp.zeros((3, ZP, wide, length), jnp.float32)
    field_ref[:, ZP + depth :] = jnp.zeros((3, high - ZP - depth, wide, length), jnp.float32)
    field_ref[:, ZP : ZP + depth, 0:YP] = jnp.zeros((3, depth, YP, length), jnp.float32)
    field_ref[:, ZP : ZP + depth, YP + breadth :] = jnp.zeros(
        (3, depth, wide - YP - breadth, length), jnp.float32
    )
    zeros_z = jnp.zeros((4, 2, breadth, length), jnp.float32)
    zeros_y = jnp.zeros((4, depth, 8, length), jnp.float32)

    @pl.when(gz == 0)
    def _():
        pad[:, 0:2, 8 : 8 + breadth, :] = zeros_z
        slots_ref[0, 0] = jnp.full(slots_ref.shape[2:], FAR, jnp.float32)

    @pl.when(gz == rows - 1)
    def _():
        pad[:, 2 + depth : 4 + depth, 8 : 8 + breadth, :] = zeros_z
        slots_ref[0, 2] = jnp.full(slots_ref.shape[2:], FAR, jnp.float32)

    @pl.when(xy == 0)
    def _():
        pad[:, 2 : 2 + depth, 0:8, :] = zeros_y
        slots_ref[1] = jnp.full(slots_ref.shape[1:], FAR, jnp.float32)

    @pl.when(xy == columns - 1)
    def _():
        pad[:, 2 : 2 + depth, 8 + breadth : 16 + breadth, :] = zeros_y
        slots_ref[2] = jnp.full(slots_ref.shape[1:], FAR, jnp.float32)

    for load in loads:
        load.wait()
    for side, start in ((2, 8), (3, 6 + breadth)):
        for part in range(4):
            for layer in range(2):
                layers_out[side - 2, part, layer * depth : (layer + 1) * depth, :] = pad[
                    part, 2 : 2 + depth, start + layer, :
                ]
        on_side(side, lambda copy: copy.start())

    corners = []
    for number, (dz, dy) in enumerate(((-1, -1), (-1, 1), (1, -1), (1, 1))):
        z_in = 2 if dz < 0 else 1 + depth
        y_in = 8 if dy < 0 else 7 + breadth
        z_out = 1 if dz < 0 else 2 + depth
        y_out = 7 if dy < 0 else 8 + breadth
        present = jnp.logical_and(has[0 if dz < 0 else 1], has[2 if dy < 0 else 3])
        for part in range(4):
            corner_out[number, part : part + 1, :] = pad[part, z_in, y_in : y_in + 1, :]
        copy = pltpu.make_async_remote_copy(
            src_ref=corner_out.at[number],
            dst_ref=corner_in.at[3 - number],
            send_sem=corner_send.at[number],
            recv_sem=corner_recv.at[3 - number],
            device_id=(gz + dz, xy + dy),
            device_id_type=MESH,
        )
        arrival = pltpu.make_async_remote_copy(
            src_ref=corner_out.at[number],
            dst_ref=corner_in.at[number],
            send_sem=corner_send.at[number],
            recv_sem=corner_recv.at[number],
            device_id=(gz + dz, xy + dy),
            device_id_type=MESH,
        )
        corners.append((present, copy, arrival, number, z_out, y_out))
    for present, copy, arrival, number, z_out, y_out in corners:
        pl.when(present)(lambda copy=copy: copy.start())

    lane = lax.broadcasted_iota(jnp.int32, (breadth + 16, length), 1)
    line = lax.broadcasted_iota(jnp.int32, (breadth + 16, length), 0)
    low_y = jnp.where(xy > 0, 0, 8)
    high_y = jnp.where(xy < columns - 1, breadth + 16, breadth + 8)
    in_grid = jnp.logical_and(line >= low_y, line < high_y)
    first_z = jnp.where(gz > 0, 0, 2)
    last_z = jnp.where(gz < rows - 1, depth + 3, depth + 1)

    def first_sweep(z):
        visc = pad[3, z]
        size = visc.shape[0]
        cx_high, cx_low = x_coeffs(visc, lane)
        coeffs = (
            0.5 * (visc + pad[3, z + 1]),
            0.5 * (visc + pad[3, z - 1]),
            0.5 * (visc + pltpu.roll(visc, size - 1, 0)),
            0.5 * (visc + pltpu.roll(visc, 1, 0)),
            cx_high,
            cx_low,
        )
        z_inside = jnp.logical_and(z >= first_z, z <= last_z)
        keep = jnp.logical_and(in_grid, z_inside)
        for part in range(3):
            centre = pad[part, z]
            new = laplace(
                centre, visc, pad[part, z - 1], pad[part, z + 1],
                pltpu.roll(centre, 1, 0), pltpu.roll(centre, size - 1, 0), coeffs, lane,
            )
            once[part, z - 1] = jnp.where(keep, new, 0.0)

    own_lane = lane[:breadth]

    def second_sweep(z):
        visc = pad[3, z, 8 : 8 + breadth, :]
        cx_high, cx_low = x_coeffs(visc, own_lane)
        coeffs = (
            0.5 * (visc + pad[3, z + 1, 8 : 8 + breadth, :]),
            0.5 * (visc + pad[3, z - 1, 8 : 8 + breadth, :]),
            0.5 * (visc + pad[3, z, 9 : 9 + breadth, :]),
            0.5 * (visc + pad[3, z, 7 : 7 + breadth, :]),
            cx_high,
            cx_low,
        )
        for part in range(3):
            field_ref[part, z - 2 + ZP, YP : YP + breadth, :] = laplace(
                once[part, z - 1, 8 : 8 + breadth, :], visc,
                once[part, z - 2, 8 : 8 + breadth, :], once[part, z, 8 : 8 + breadth, :],
                once[part, z - 1, 7 : 7 + breadth, :], once[part, z - 1, 9 : 9 + breadth, :],
                coeffs, own_lane,
            )

    def loop(low, high, body):
        def step(z, unused):
            body(z)
            return unused

        lax.fori_loop(low, high, step, 0)

    arrives = ((1, 0), (0, 1), (3, 2), (2, 3))

    def wait_side(side, neighbour):
        @pl.when(has[neighbour])
        def _():
            for copy in halo_copies(side):
                copy.wait_recv()
            if side >= 2:
                start = 6 if side == 3 else 8 + breadth
                for part in range(4):
                    for layer in range(2):
                        pad[part, 2 : 2 + depth, start + layer, :] = layers_in[
                            3 - side, part, layer * depth : (layer + 1) * depth, :
                        ]

    forwards = []
    for number, (there, column, side) in enumerate(((has[3], xy + 1, 1), (has[2], xy - 1, 2))):
        for dr in (-1, 0, 1):
            copy = pltpu.make_async_remote_copy(
                src_ref=slots_ref.at[0, dr + 1, :, 0:USED],
                dst_ref=slots_ref.at[side, dr + 1, :, 0:USED],
                send_sem=c_send.at[number, dr + 1],
                recv_sem=c_recv.at[number, dr + 1],
                device_id=(gz, column),
                device_id_type=MESH,
            )
            forwards.append((there, copy, dr, has[2 + number]))

    def forward(row):
        for there, copy, dr, unused in forwards:
            if dr == row:
                pl.when(there)(lambda copy=copy: copy.start())

    whole_row(0).wait_recv()
    forward(0)
    wait_side(2, 3)
    wait_side(3, 2)
    loop(3, 3 + depth // 4, first_sweep)
    for dr in (-1, 1):
        pl.when(has[0 if dr < 0 else 1])(lambda dr=dr: whole_row(dr).wait_recv())
        forward(dr)
    loop(3 + depth // 4, 1 + depth, first_sweep)

    wait_side(0, 1)
    wait_side(1, 0)
    for present, copy, arrival, number, z_out, y_out in corners:

        @pl.when(present)
        def _(arrival=arrival, number=number, z_out=z_out, y_out=y_out):
            arrival.wait_recv()
            for part in range(4):
                pad[part, z_out, y_out : y_out + 1, :] = corner_in[number, part : part + 1, :]

        @pl.when(jnp.logical_not(present))
        def _(z_out=z_out, y_out=y_out):
            for part in range(4):
                pad[part, z_out, y_out : y_out + 1, :] = jnp.zeros((1, length), jnp.float32)

    for z in (1, 2, 1 + depth, 2 + depth):
        first_sweep(z)
    loop(2, 2 + depth, second_sweep)

    for unused, copy, dr, comes in forwards:
        pl.when(comes)(lambda copy=copy: copy.wait_recv())
    make_list(depth, breadth, slots_ref, list_ref)
    each_row(gz, rows, lambda dr: whole_row(dr).wait_send())
    for side in range(4):
        on_side(side, lambda copy: copy.wait_send())
    for present, copy, arrival, number, z_out, y_out in corners:
        pl.when(present)(lambda copy=copy: copy.wait_send())
    for there, copy, unused, comes in forwards:
        pl.when(there)(lambda copy=copy: copy.wait_send())


def phi(radius):
    x2 = radius * radius * 0.6168502750680849
    c = 1.0 / 479001600.0
    for factor in (-1.0 / 3628800.0, 1.0 / 40320.0, -1.0 / 720.0, 1.0 / 24.0, -0.5, 1.0):
        c = c * x2 + factor
    return jnp.where(jnp.abs(radius) < 2.0, 0.5 * c * c, 0.0)


def split(value):
    high = value.astype(jnp.bfloat16)
    return high, (value - high.astype(jnp.float32)).astype(jnp.bfloat16)


def product(left, right, contract):
    (left_high, left_low), (right_high, right_low) = left, right
    return lax.dot_general(
        jnp.concatenate([left_high, left_low, left_high], axis=1),
        jnp.concatenate([right_high, right_high, right_low], axis=contract),
        (((1,), (contract,)), ((), ())),
        preferred_element_type=jnp.float32,
    )


def points_kernel(
    depth, breadth, list_ref, slots_ref, field_in, new_ref, partial_ref, field, wx_high, wx_low, store_sem
):
    length = field.shape[3]
    partial_ref[...] = jnp.zeros_like(partial_ref)
    found = list_ref[4, 0]
    rounds = (found + TOGETHER - 1) // TOGETHER

    line = lax.broadcasted_iota(jnp.int32, (BOX, length), 0)
    rel = line.astype(jnp.float32)
    far = lax.broadcasted_iota(jnp.int32, (length, length), 0).astype(jnp.float32)

    def members(number):
        for other in range(TOGETHER):
            at = number * TOGETHER + other
            spot = jnp.minimum(at, found - 1)
            z, y, pair, rank = (list_ref[row, spot] for row in range(4))
            yield at, at < found, pair, rank, z, y

    def near_weights(frac, z, y):
        wz = phi(2.0 + (BOX - 5) * frac[0:1] - rel)
        wy = phi(2.0 + (BOX - 5) * frac[1:2] - rel)
        wz = jnp.where((z + line >= 0) & (z + line < depth), wz, 0.0)
        wy = jnp.where((y + line >= 0) & (y + line < breadth), wy, 0.0)
        return wz, wy

    def far_weights(frac):
        at = 2.0 + (length - 5) * frac
        near = at - rel
        base = phi(near - 4.0 * jnp.floor(0.25 * near + 0.5))
        high = base.astype(jnp.bfloat16).astype(jnp.float32)
        low = base - high
        inside = jnp.abs(at - far) < 2.0

        def spread_out(part):
            whole = jnp.broadcast_to(part[None], (length // BOX, BOX, length)).reshape(length, length)
            return jnp.where(inside, whole, 0.0).astype(jnp.bfloat16)

        return spread_out(high), spread_out(low)

    def box_of(z, y):
        return (slice(None), pl.ds(z + ZP, BOX), pl.ds(y + YP, BOX), slice(None))

    def spread(number, unused):
        adds = []
        for at, counts, pair, rank, z, y in members(number):
            tile = slots_ref[pair, pl.ds(6 * rank, 6), :]
            wz, wy = near_weights(tile, z, y)
            wy = jnp.where(counts, wy, 0.0)
            wx = far_weights(tile[2:3])
            wx_high[at], wx_low[at] = wx
            pulled = tile[3:6][:, None, :] * wz[None]
            coeff = pulled[:, :, None, :] * wy[None, None]
            boxes = product(split(coeff.reshape(3 * BOX * BOX, length)), wx, 1)
            adds.append((box_of(z, y), boxes.reshape(3, BOX, BOX, length)))
        for box, boxes in adds:
            field[box] = field[box] + boxes
        return unused

    lax.fori_loop(0, rounds, spread, 0)
    store = pltpu.make_async_copy(
        field.at[:, ZP : ZP + depth, YP : YP + breadth], new_ref, store_sem
    )
    store.start()

    def sample(number, unused):
        results = []
        for at, counts, pair, rank, z, y in members(number):
            wz, wy = near_weights(slots_ref[pair, pl.ds(6 * rank, 6), :], z, y)
            cells = field[box_of(z, y)].reshape(3 * BOX * BOX, length)
            taken = product(split(cells), (wx_high[at], wx_low[at]), 0)
            taken = taken.reshape(3, BOX, BOX, length)
            summed = jnp.sum(taken * wz[None, :, None, :], axis=1)
            results.append((pair, rank, jnp.sum(summed * wy[None], axis=1)))
        for pair, rank, values in results:
            partial_ref[pair, pl.ds(3 * rank, 3), :] = values
        return unused

    lax.fori_loop(0, rounds, sample, 0)
    store.wait()


def return_kernel(
    rows, columns, target_ref, partial_ref, out_ref,
    side_in, summed, gathered, c_send, c_recv, ab_send, ab_recv,
):
    gz, xy = lax.axis_index("gz"), lax.axis_index("xy")
    wait_greeting = greet(gz, xy, rows, columns)
    wait_greeting()
    has_low, has_high = xy > 0, xy < columns - 1
    copies = []
    for number, (there, column) in enumerate(((has_low, xy - 1), (has_high, xy + 1))):
        copy = pltpu.make_async_remote_copy(
            src_ref=partial_ref.at[number + 1],
            dst_ref=side_in.at[1 - number],
            send_sem=c_send.at[number],
            recv_sem=c_recv.at[1 - number],
            device_id=(gz, column),
            device_id_type=MESH,
        )
        arrival = pltpu.make_async_remote_copy(
            src_ref=partial_ref.at[number + 1],
            dst_ref=side_in.at[number],
            send_sem=c_send.at[number],
            recv_sem=c_recv.at[number],
            device_id=(gz, column),
            device_id_type=MESH,
        )
        copies.append((there, copy))
        pl.when(there)(lambda copy=copy: copy.start())

        @pl.when(jnp.logical_not(there))
        def _(number=number):
            side_in[number] = jnp.zeros(side_in.shape[1:], jnp.float32)

        copies[-1] = (there, copy, arrival)
    for there, copy, arrival in copies:
        pl.when(there)(lambda arrival=arrival: arrival.wait_recv())
    summed[...] = partial_ref[0] + side_in[0] + side_in[1]

    each_peer = peers(gz, xy, rows, columns)

    def block_copy(dr, column):
        return pltpu.make_async_remote_copy(
            src_ref=summed.at[dr + 1, column],
            dst_ref=gathered.at[1 - dr, xy],
            send_sem=ab_send.at[dr + 1],
            recv_sem=ab_recv.at[1 - dr],
            device_id=(gz + dr, column),
            device_id_type=MESH,
        )

    def whole_row(dr):
        span = pl.ds(0, columns - (1 if dr == 0 else 0))
        return pltpu.make_async_remote_copy(
            src_ref=summed.at[dr + 1, span],
            dst_ref=gathered.at[dr + 1, span],
            send_sem=ab_send.at[dr + 1],
            recv_sem=ab_recv.at[dr + 1],
            device_id=(gz, xy),
            device_id_type=MESH,
        )

    each_peer(lambda dr, column: block_copy(dr, column).start())
    gathered[1, xy] = summed[1, xy]

    @pl.when(gz == 0)
    def _():
        gathered[0] = jnp.zeros(gathered.shape[1:], jnp.float32)

    @pl.when(gz == rows - 1)
    def _():
        gathered[2] = jnp.zeros(gathered.shape[1:], jnp.float32)

    each_row(gz, rows, lambda dr: whole_row(dr).wait_recv())
    count = out_ref.shape[1]
    for j in range(count):
        column = target_ref[j]
        rank = jnp.int32(0)
        for earlier in range(j):
            rank = rank + (target_ref[earlier] == column).astype(jnp.int32)
        tile = gathered[0, column] + gathered[1, column] + gathered[2, column]
        out_ref[:, j, :] = jnp.where(rank == 0, tile[0:3], tile[3:6])
    each_row(gz, rows, lambda dr: whole_row(dr).wait_send())
    for there, copy, arrival in copies:
        pl.when(there)(lambda copy=copy: copy.wait_send())


def shards(rows, columns, velocity, viscosity, frac, force, target, z_offset, y_offset):
    parts, depth, breadth, length = velocity.shape
    target = target.reshape(target.shape[0])
    frac, force = jnp.transpose(frac, (1, 0, 2)), jnp.transpose(force, (1, 0, 2))
    held = lambda array: pltpu.with_memory_space_constraint(array, pltpu.HBM)
    velocity, viscosity, frac, force = held(velocity), held(viscosity), held(frac), held(force)
    target, z_offset, y_offset = held(target), held(z_offset), held(y_offset)
    f32 = jnp.float32
    vmem = pl.BlockSpec(memory_space=pltpu.VMEM)
    smem = pl.BlockSpec(memory_space=pltpu.SMEM)
    hbm = pl.BlockSpec(memory_space=pltpu.HBM)
    anyw = pl.BlockSpec(memory_space=pl.ANY)
    dma = pltpu.SemaphoreType.DMA
    pairs = 9 * columns
    listed = pl.cdiv(CAP * pairs, length) * length
    field_shape = (3, depth + 2 * ZP, breadth + 2 * YP, length)
    field, slots, listing = pl.pallas_call(
        functools.partial(exchange_kernel, rows, columns),
        out_shape=(
            jax.ShapeDtypeStruct(field_shape, f32),
            jax.ShapeDtypeStruct((3, 3, columns, PAIR, length), f32),
            jax.ShapeDtypeStruct((8, listed), jnp.int32),
        ),
        in_specs=[smem, smem, smem, hbm, hbm, vmem, vmem],
        out_specs=(vmem, vmem, vmem),
        scratch_shapes=[
            pltpu.VMEM((4, depth + 4, breadth + 16, length), f32),
            pltpu.VMEM((3, depth + 2, breadth + 16, length), f32),
            pltpu.VMEM((columns, PAIR, length), f32),
            pltpu.VMEM((2, 4, 2 * depth, length), f32),
            pltpu.VMEM((2, 4, 2 * depth, length), f32),
            pltpu.VMEM((4, 8, length), f32),
            pltpu.VMEM((4, 8, length), f32),
            dma((2,)), dma((3,)), dma((3,)), dma((4, 2)), dma((4, 2)),
            dma((4,)), dma((4,)), dma((2, 3)), dma((2, 3)),
        ],
        compiler_params=pltpu.CompilerParams(
            collective_id=0, has_side_effects=True, vmem_limit_bytes=VMEM_LIMIT
        ),
    )(target, z_offset, y_offset, velocity, viscosity, frac, force)

    new_velocity, partial, unused = pl.pallas_call(
        functools.partial(points_kernel, depth, breadth),
        out_shape=(
            jax.ShapeDtypeStruct(velocity.shape, f32),
            jax.ShapeDtypeStruct((pairs, 8, length), f32),
            jax.ShapeDtypeStruct(field_shape, f32),
        ),
        in_specs=[smem, vmem, vmem],
        out_specs=(anyw, vmem, vmem),
        scratch_shapes=[
            pltpu.VMEM((CAP * pairs + TOGETHER, length, length), jnp.bfloat16),
            pltpu.VMEM((CAP * pairs + TOGETHER, length, length), jnp.bfloat16),
            dma(()),
        ],
        input_output_aliases={2: 2},
        compiler_params=pltpu.CompilerParams(vmem_limit_bytes=VMEM_LIMIT),
    )(listing, slots.reshape(pairs, PAIR, length), field)

    point_velocity = pl.pallas_call(
        functools.partial(return_kernel, rows, columns),
        out_shape=jax.ShapeDtypeStruct(frac.shape, f32),
        in_specs=[smem, vmem],
        out_specs=vmem,
        scratch_shapes=[
            pltpu.VMEM((2, 3, columns, 8, length), f32),
            pltpu.VMEM((3, columns, 8, length), f32),
            pltpu.VMEM((3, columns, 8, length), f32),
            dma((2,)), dma((2,)), dma((3,)), dma((3,)),
        ],
        compiler_params=pltpu.CompilerParams(
            collective_id=1, has_side_effects=True, vmem_limit_bytes=VMEM_LIMIT
        ),
    )(target, partial.reshape(3, 3, columns, 8, length))
    return new_velocity, jnp.transpose(point_velocity, (1, 0, 2))


def solution(mesh):
    placed = (
        P(None, "gz", "xy", None),
        P("gz", "xy", None),
        P(("gz", "xy"), None, None),
        P(("gz", "xy"), None, None),
        P(("gz", "xy"), None),
        P(("gz", "xy")),
        P(("gz", "xy")),
    )
    return jax.shard_map(
        functools.partial(shards, mesh.shape["gz"], mesh.shape["xy"]),
        mesh=mesh,
        in_specs=placed,
        out_specs=(P(None, "gz", "xy", None), P(("gz", "xy"), None, None)),
        check_vma=False,
    )
```

```python
import functools

import jax
import jax.numpy as jnp
from jax import lax
from jax.experimental import pallas as pl
from jax.experimental.pallas import tpu as pltpu
from jax.sharding import PartitionSpec as P

BOX = 8
CAP = 2
FAR = 4096.0
ZP = 7
YP = 8
PAIR = 16
USED = 13
TOGETHER = 4
CORES = 2
MESH = pl.DeviceIdType.MESH
VMEM_LIMIT = 24 * 1024 * 1024


def peers(gz, xy, rows, columns):
    def each(body):
        for dr in (-1, 0, 1):
            inside = jnp.logical_and(gz + dr >= 0, gz + dr < rows)

            @pl.when(inside)
            def _(dr=dr):
                for k in range(1 if dr == 0 else 0, columns):
                    column = xy + k
                    body(dr, jnp.where(column >= columns, column - columns, column))

    return each


def each_row(gz, rows, body):
    for dr in (-1, 0, 1):
        inside = jnp.logical_and(gz + dr >= 0, gz + dr < rows)
        pl.when(inside)(functools.partial(body, dr))


def greet(gz, xy, rows, columns):
    barrier = pltpu.get_barrier_semaphore()

    def signal(dr, column):
        pl.semaphore_signal(barrier, inc=1, device_id=(gz + dr, column), device_id_type=MESH)

    peers(gz, xy, rows, columns)(signal)
    near = (
        1 + (gz > 0).astype(jnp.int32) + (gz < rows - 1).astype(jnp.int32)
    )
    return lambda: pl.semaphore_wait(barrier, near * columns - 1)


def chip_peers(gz, xy, rows, columns, steps):
    chip, core = xy // CORES, xy % CORES
    chips = columns // CORES

    def each(body):
        for step in steps:
            for dr in (0, -1, 1):
                there = (gz + dr >= 0) & (gz + dr < rows) & (chip + step >= 0) & (chip + step < chips)
                for turn in range(CORES):
                    if step == 0 and dr == 0 and turn == 0:
                        continue
                    other = core + turn
                    column = (chip + step) * CORES + jnp.where(other >= CORES, other - CORES, other)
                    pl.when(there)(functools.partial(body, dr, column))

    return each


def matches(target_ref, count, column):
    first, second = jnp.int32(-1), jnp.int32(-1)
    for j in range(count):
        hit = target_ref[j] == column
        second = jnp.where(jnp.logical_and(hit, jnp.logical_and(first >= 0, second < 0)), j, second)
        first = jnp.where(jnp.logical_and(hit, first < 0), j, first)
    return first, second


def laplace(centre, visc, z_low, z_high, y_low, y_high, coeffs, lane):
    length = centre.shape[-1]
    x_high = jnp.where(lane == length - 1, 0.0, pltpu.roll(centre, length - 1, 1))
    x_low = jnp.where(lane == 0, 0.0, pltpu.roll(centre, 1, 1))
    total = coeffs[0] * (z_high - centre) + coeffs[1] * (z_low - centre)
    total = total + coeffs[2] * (y_high - centre) + coeffs[3] * (y_low - centre)
    total = total + coeffs[4] * (x_high - centre) + coeffs[5] * (x_low - centre)
    return centre + 0.08 * total


def x_coeffs(visc, lane):
    length = visc.shape[-1]
    high = jnp.where(lane == length - 1, 0.0, pltpu.roll(visc, length - 1, 1))
    low = jnp.where(lane == 0, 0.0, pltpu.roll(visc, 1, 1))
    return 0.5 * (visc + high), 0.5 * (visc + low)


def make_list(depth, breadth, slots_ref, list_ref):
    columns, length = slots_ref.shape[2], slots_ref.shape[4]
    pairs, listed = 9 * columns, list_ref.shape[1]
    rows = slots_ref[:, :, :, USED - 1 : USED, :].reshape(pairs, length)
    number = lax.broadcasted_iota(jnp.int32, (pairs, length), 0)
    lane = lax.broadcasted_iota(jnp.int32, (pairs, length), 1)
    side, dr = number // (3 * columns), number // columns % 3
    shift_z = ((dr - 1) * depth).astype(jnp.float32)
    shift_y = jnp.where(side == 0, 0, jnp.where(side == 1, -breadth, breadth)).astype(jnp.float32)
    earlier = lax.broadcasted_iota(jnp.int32, (pairs, pairs), 0) > lax.broadcasted_iota(
        jnp.int32, (pairs, pairs), 1
    )
    earlier = earlier.astype(jnp.float32).astype(jnp.bfloat16)
    place = lax.broadcasted_iota(jnp.int32, (pairs, listed), 1)
    before = jnp.zeros((1, 1), jnp.float32)
    listing = jnp.zeros((length, listed), jnp.float32)
    for rank in range(CAP):
        z = rows[:, 2 * rank : 2 * rank + 1] + shift_z
        y = rows[:, 2 * rank + 1 : 2 * rank + 2] + shift_y
        meets = (z > -BOX) & (z < depth) & (y > -BOX) & (y < breadth)
        one = jnp.where(meets, 1.0, 0.0)
        rank_of = jnp.dot(earlier, one.astype(jnp.bfloat16), preferred_element_type=jnp.float32) + before
        spot = jnp.where(meets, rank_of, -1.0).astype(jnp.int32)
        chosen = jnp.where(place == spot[:, 0:1], 1.0, 0.0).astype(jnp.bfloat16)
        facts = jnp.where(lane == 0, z, jnp.where(lane == 1, y, jnp.where(lane == 2, number, 0).astype(jnp.float32)))
        facts = jnp.where(meets, jnp.where(lane == 3, float(rank), facts), 0.0).astype(jnp.bfloat16)
        listing = listing + lax.dot_general(
            facts, chosen, (((0,), (0,)), ((), ())), preferred_element_type=jnp.float32
        )
        before = before + jnp.sum(one[:, 0:1], axis=0, keepdims=True)
    list_ref[0:4, :] = listing[0:4].astype(jnp.int32)
    list_ref[4:8, :] = jnp.broadcast_to(before, (4, listed)).astype(jnp.int32)


def exchange_kernel(
    rows, columns, target_ref, zoff_ref, yoff_ref, velocity_ref, viscosity_ref, frac_ref, force_ref,
    field_ref, slots_ref, list_ref,
    pad, once, staging, layers_out, layers_in, corner_out, corner_in,
    load_sem, ab_send, ab_recv, halo_send, halo_recv, corner_send, corner_recv, c_send, c_recv, known,
):
    gz, xy = lax.axis_index("gz"), lax.axis_index("xy")
    depth, breadth = velocity_ref.shape[1], velocity_ref.shape[2]
    length = velocity_ref.shape[3]
    chip, chips = xy // CORES, columns // CORES
    barrier = pltpu.get_barrier_semaphore()
    near_peers = chip_peers(gz, xy, rows, columns, (0, -1, 1))

    def signal_near(dr, column):
        pl.semaphore_signal(barrier, inc=1, device_id=(gz + dr, column), device_id_type=MESH)

    near_peers(signal_near)
    near_rows = 1 + (gz > 0).astype(jnp.int32) + (gz < rows - 1).astype(jnp.int32)
    near_chips = 1 + (chip > 0).astype(jnp.int32) + (chip < chips - 1).astype(jnp.int32)
    loads = (
        pltpu.make_async_copy(
            velocity_ref, pad.at[0:3, 2 : 2 + depth, 8 : 8 + breadth], load_sem.at[0]
        ),
        pltpu.make_async_copy(
            viscosity_ref, pad.at[3, 2 : 2 + depth, 8 : 8 + breadth], load_sem.at[1]
        ),
    )
    for load in loads:
        load.start()

    lanes = lax.broadcasted_iota(jnp.int32, (1, length), 1)
    count = frac_ref.shape[1]

    def stage(column, unused):
        row = jnp.full((1, length), FAR, jnp.float32)
        for rank, block in enumerate(matches(target_ref, count, column)):
            at = jnp.maximum(block, 0)
            there = block >= 0
            z = jnp.where(there, zoff_ref[at].astype(jnp.float32), FAR)
            y = jnp.where(there, yoff_ref[at].astype(jnp.float32), FAR)
            staging[column, 6 * rank : 6 * rank + 3, :] = frac_ref[:, at, :]
            staging[column, 6 * rank + 3 : 6 * rank + 6, :] = force_ref[:, at, :]
            row = jnp.where(lanes == 2 * rank, z, row)
            row = jnp.where(lanes == 2 * rank + 1, y, row)
        staging[column, 12:13, :] = row
        return unused

    lax.fori_loop(0, columns, stage, 0)
    def block_copy(dr, column):
        return pltpu.make_async_remote_copy(
            src_ref=staging.at[column, 0:USED],
            dst_ref=slots_ref.at[0, 1 - dr, xy, 0:USED],
            send_sem=ab_send.at[dr + 1],
            recv_sem=ab_recv.at[1 - dr],
            device_id=(gz + dr, column),
            device_id_type=MESH,
        )

    def whole_row(dr):
        span = pl.ds(0, columns - (1 if dr == 0 else 0))
        return pltpu.make_async_remote_copy(
            src_ref=staging.at[span, 0:USED],
            dst_ref=slots_ref.at[0, dr + 1, span, 0:USED],
            send_sem=ab_send.at[dr + 1],
            recv_sem=ab_recv.at[dr + 1],
            device_id=(gz, xy),
            device_id_type=MESH,
        )

    def tell(stage):
        for number, (there, column) in enumerate(chain):
            pl.when(there)(
                lambda number=number, column=column: pl.semaphore_signal(
                    known.at[stage, number], inc=1, device_id=(gz, column), device_id_type=MESH
                )
            )

    def hear(stage):
        for number, (there, column) in enumerate(chain):
            pl.when(there)(lambda number=number: pl.semaphore_wait(known.at[stage, 1 - number], 1))

    chain = ((chip < chips - 1, xy + CORES), (chip > 0, xy - CORES))
    pl.semaphore_wait(barrier, near_rows * near_chips * CORES - 1)
    tell(0)
    near_peers(lambda dr, column: block_copy(dr, column).start())
    slots_ref[0, 1, xy, 0:USED] = staging[xy, 0:USED]

    has = (gz > 0, gz < rows - 1, xy > 0, xy < columns - 1)
    device = ((gz - 1, xy), (gz + 1, xy), (gz, xy - 1), (gz, xy + 1))
    own_y = slice(8, 8 + breadth)
    own_z = slice(2, 2 + depth)

    def halo_copies(side):
        if side == 0:
            cut, land = slice(0, 2), (slice(2 + depth, 4 + depth), own_y)
        elif side == 1:
            cut, land = slice(depth - 2, depth), (slice(0, 2), own_y)
        if side < 2:
            sources = (velocity_ref.at[:, cut], viscosity_ref.at[cut])
            lands = (pad.at[(slice(0, 3),) + land], pad.at[(3,) + land])
        else:
            sources, lands = (layers_out.at[side - 2],), (layers_in.at[3 - side],)
        return [
            pltpu.make_async_remote_copy(
                src_ref=source,
                dst_ref=spot,
                send_sem=halo_send.at[side, number],
                recv_sem=halo_recv.at[side, number],
                device_id=device[side],
                device_id_type=MESH,
            )
            for number, (source, spot) in enumerate(zip(sources, lands))
        ]

    def on_side(side, action):
        @pl.when(has[side])
        def _():
            for copy in halo_copies(side):
                action(copy)

    for side in (0, 1):
        on_side(side, lambda copy: copy.start())

    for stage in range(chips - 2):
        hear(stage)
        if stage < chips - 3:
            tell(stage + 1)
        far_peers = chip_peers(gz, xy, rows, columns, (-2 - stage, 2 + stage))
        far_peers(lambda dr, column: block_copy(dr, column).start())

    wide, high = field_ref.shape[2], field_ref.shape[1]
    field_ref[:, 0:ZP] = jnp.zeros((3, ZP, wide, length), jnp.float32)
    field_ref[:, ZP + depth :] = jnp.zeros((3, high - ZP - depth, wide, length), jnp.float32)
    field_ref[:, ZP : ZP + depth, 0:YP] = jnp.zeros((3, depth, YP, length), jnp.float32)
    field_ref[:, ZP : ZP + depth, YP + breadth :] = jnp.zeros(
        (3, depth, wide - YP - breadth, length), jnp.float32
    )
    zeros_z = jnp.zeros((4, 2, breadth, length), jnp.float32)
    zeros_y = jnp.zeros((4, depth, 8, length), jnp.float32)

    @pl.when(gz == 0)
    def _():
        pad[:, 0:2, 8 : 8 + breadth, :] = zeros_z
        slots_ref[0, 0] = jnp.full(slots_ref.shape[2:], FAR, jnp.float32)

    @pl.when(gz == rows - 1)
    def _():
        pad[:, 2 + depth : 4 + depth, 8 : 8 + breadth, :] = zeros_z
        slots_ref[0, 2] = jnp.full(slots_ref.shape[2:], FAR, jnp.float32)

    @pl.when(xy == 0)
    def _():
        pad[:, 2 : 2 + depth, 0:8, :] = zeros_y
        slots_ref[1] = jnp.full(slots_ref.shape[1:], FAR, jnp.float32)

    @pl.when(xy == columns - 1)
    def _():
        pad[:, 2 : 2 + depth, 8 + breadth : 16 + breadth, :] = zeros_y
        slots_ref[2] = jnp.full(slots_ref.shape[1:], FAR, jnp.float32)

    for load in loads:
        load.wait()
    for side, start in ((2, 8), (3, 6 + breadth)):
        for part in range(4):
            for layer in range(2):
                layers_out[side - 2, part, layer * depth : (layer + 1) * depth, :] = pad[
                    part, 2 : 2 + depth, start + layer, :
                ]
        on_side(side, lambda copy: copy.start())

    corners = []
    for number, (dz, dy) in enumerate(((-1, -1), (-1, 1), (1, -1), (1, 1))):
        z_in = 2 if dz < 0 else 1 + depth
        y_in = 8 if dy < 0 else 7 + breadth
        z_out = 1 if dz < 0 else 2 + depth
        y_out = 7 if dy < 0 else 8 + breadth
        present = jnp.logical_and(has[0 if dz < 0 else 1], has[2 if dy < 0 else 3])
        for part in range(4):
            corner_out[number, part : part + 1, :] = pad[part, z_in, y_in : y_in + 1, :]
        copy = pltpu.make_async_remote_copy(
            src_ref=corner_out.at[number],
            dst_ref=corner_in.at[3 - number],
            send_sem=corner_send.at[number],
            recv_sem=corner_recv.at[3 - number],
            device_id=(gz + dz, xy + dy),
            device_id_type=MESH,
        )
        arrival = pltpu.make_async_remote_copy(
            src_ref=corner_out.at[number],
            dst_ref=corner_in.at[number],
            send_sem=corner_send.at[number],
            recv_sem=corner_recv.at[number],
            device_id=(gz + dz, xy + dy),
            device_id_type=MESH,
        )
        corners.append((present, copy, arrival, number, z_out, y_out))
    for present, copy, arrival, number, z_out, y_out in corners:
        pl.when(present)(lambda copy=copy: copy.start())

    lane = lax.broadcasted_iota(jnp.int32, (breadth + 16, length), 1)
    line = lax.broadcasted_iota(jnp.int32, (breadth + 16, length), 0)
    low_y = jnp.where(xy > 0, 0, 8)
    high_y = jnp.where(xy < columns - 1, breadth + 16, breadth + 8)
    in_grid = jnp.logical_and(line >= low_y, line < high_y)
    first_z = jnp.where(gz > 0, 0, 2)
    last_z = jnp.where(gz < rows - 1, depth + 3, depth + 1)

    def first_sweep(z):
        visc = pad[3, z]
        size = visc.shape[0]
        cx_high, cx_low = x_coeffs(visc, lane)
        coeffs = (
            0.5 * (visc + pad[3, z + 1]),
            0.5 * (visc + pad[3, z - 1]),
            0.5 * (visc + pltpu.roll(visc, size - 1, 0)),
            0.5 * (visc + pltpu.roll(visc, 1, 0)),
            cx_high,
            cx_low,
        )
        z_inside = jnp.logical_and(z >= first_z, z <= last_z)
        keep = jnp.logical_and(in_grid, z_inside)
        for part in range(3):
            centre = pad[part, z]
            new = laplace(
                centre, visc, pad[part, z - 1], pad[part, z + 1],
                pltpu.roll(centre, 1, 0), pltpu.roll(centre, size - 1, 0), coeffs, lane,
            )
            once[part, z - 1] = jnp.where(keep, new, 0.0)

    own_lane = lane[:breadth]

    def second_sweep(z):
        visc = pad[3, z, 8 : 8 + breadth, :]
        cx_high, cx_low = x_coeffs(visc, own_lane)
        coeffs = (
            0.5 * (visc + pad[3, z + 1, 8 : 8 + breadth, :]),
            0.5 * (visc + pad[3, z - 1, 8 : 8 + breadth, :]),
            0.5 * (visc + pad[3, z, 9 : 9 + breadth, :]),
            0.5 * (visc + pad[3, z, 7 : 7 + breadth, :]),
            cx_high,
            cx_low,
        )
        for part in range(3):
            field_ref[part, z - 2 + ZP, YP : YP + breadth, :] = laplace(
                once[part, z - 1, 8 : 8 + breadth, :], visc,
                once[part, z - 2, 8 : 8 + breadth, :], once[part, z, 8 : 8 + breadth, :],
                once[part, z - 1, 7 : 7 + breadth, :], once[part, z - 1, 9 : 9 + breadth, :],
                coeffs, own_lane,
            )

    def loop(low, high, body):
        def step(z, unused):
            body(z)
            return unused

        lax.fori_loop(low, high, step, 0)

    arrives = ((1, 0), (0, 1), (3, 2), (2, 3))

    def wait_side(side, neighbour):
        @pl.when(has[neighbour])
        def _():
            for copy in halo_copies(side):
                copy.wait_recv()
            if side >= 2:
                start = 6 if side == 3 else 8 + breadth
                for part in range(4):
                    for layer in range(2):
                        pad[part, 2 : 2 + depth, start + layer, :] = layers_in[
                            3 - side, part, layer * depth : (layer + 1) * depth, :
                        ]

    forwards = []
    for number, (there, column, side) in enumerate(((has[3], xy + 1, 1), (has[2], xy - 1, 2))):
        for dr in (-1, 0, 1):
            copy = pltpu.make_async_remote_copy(
                src_ref=slots_ref.at[0, dr + 1, :, 0:USED],
                dst_ref=slots_ref.at[side, dr + 1, :, 0:USED],
                send_sem=c_send.at[number, dr + 1],
                recv_sem=c_recv.at[number, dr + 1],
                device_id=(gz, column),
                device_id_type=MESH,
            )
            forwards.append((there, copy, dr, has[2 + number]))

    def forward(row):
        for there, copy, dr, unused in forwards:
            if dr == row:
                pl.when(there)(lambda copy=copy: copy.start())

    wait_side(2, 3)
    wait_side(3, 2)
    loop(3, 1 + depth, first_sweep)
    whole_row(0).wait_recv()
    forward(0)
    middle = 4 + (depth - 4) // 2
    loop(4, middle, second_sweep)
    for dr in (-1, 1):
        pl.when(has[0 if dr < 0 else 1])(lambda dr=dr: whole_row(dr).wait_recv())
        forward(dr)
    loop(middle, depth, second_sweep)

    wait_side(0, 1)
    wait_side(1, 0)
    for present, copy, arrival, number, z_out, y_out in corners:

        @pl.when(present)
        def _(arrival=arrival, number=number, z_out=z_out, y_out=y_out):
            arrival.wait_recv()
            for part in range(4):
                pad[part, z_out, y_out : y_out + 1, :] = corner_in[number, part : part + 1, :]

        @pl.when(jnp.logical_not(present))
        def _(z_out=z_out, y_out=y_out):
            for part in range(4):
                pad[part, z_out, y_out : y_out + 1, :] = jnp.zeros((1, length), jnp.float32)

    for z in (1, 2, 1 + depth, 2 + depth):
        first_sweep(z)
    for z in (2, 3, depth, 1 + depth):
        second_sweep(z)

    for unused, copy, dr, comes in forwards:
        pl.when(comes)(lambda copy=copy: copy.wait_recv())
    make_list(depth, breadth, slots_ref, list_ref)
    each_row(gz, rows, lambda dr: whole_row(dr).wait_send())
    for side in range(4):
        on_side(side, lambda copy: copy.wait_send())
    for present, copy, arrival, number, z_out, y_out in corners:
        pl.when(present)(lambda copy=copy: copy.wait_send())
    for there, copy, unused, comes in forwards:
        pl.when(there)(lambda copy=copy: copy.wait_send())


def phi(radius):
    x2 = radius * radius * 0.6168502750680849
    c = 1.0 / 479001600.0
    for factor in (-1.0 / 3628800.0, 1.0 / 40320.0, -1.0 / 720.0, 1.0 / 24.0, -0.5, 1.0):
        c = c * x2 + factor
    return jnp.where(jnp.abs(radius) < 2.0, 0.5 * c * c, 0.0)


def split(value):
    high = value.astype(jnp.bfloat16)
    return high, (value - high.astype(jnp.float32)).astype(jnp.bfloat16)


def product(left, right, contract):
    (left_high, left_low), (right_high, right_low) = left, right
    return lax.dot_general(
        jnp.concatenate([left_high, left_low, left_high], axis=1),
        jnp.concatenate([right_high, right_high, right_low], axis=contract),
        (((1,), (contract,)), ((), ())),
        preferred_element_type=jnp.float32,
    )


def points_kernel(
    depth, breadth, list_ref, slots_ref, field_in, new_ref, partial_ref, field, wx_high, wx_low, store_sem
):
    length = field.shape[3]
    partial_ref[...] = jnp.zeros_like(partial_ref)
    found = list_ref[4, 0]
    rounds = (found + TOGETHER - 1) // TOGETHER

    line = lax.broadcasted_iota(jnp.int32, (BOX, length), 0)
    rel = line.astype(jnp.float32)
    far = lax.broadcasted_iota(jnp.int32, (length, length), 0).astype(jnp.float32)

    def members(number):
        for other in range(TOGETHER):
            at = number * TOGETHER + other
            spot = jnp.minimum(at, found - 1)
            z, y, pair, rank = (list_ref[row, spot] for row in range(4))
            yield at, at < found, pair, rank, z, y

    def near_weights(frac, z, y):
        wz = phi(2.0 + (BOX - 5) * frac[0:1] - rel)
        wy = phi(2.0 + (BOX - 5) * frac[1:2] - rel)
        wz = jnp.where((z + line >= 0) & (z + line < depth), wz, 0.0)
        wy = jnp.where((y + line >= 0) & (y + line < breadth), wy, 0.0)
        return wz, wy

    def far_weights(frac):
        at = 2.0 + (length - 5) * frac
        near = at - rel
        base = phi(near - 4.0 * jnp.floor(0.25 * near + 0.5))
        high = base.astype(jnp.bfloat16).astype(jnp.float32)
        low = base - high
        inside = jnp.abs(at - far) < 2.0

        def spread_out(part):
            whole = jnp.broadcast_to(part[None], (length // BOX, BOX, length)).reshape(length, length)
            return jnp.where(inside, whole, 0.0).astype(jnp.bfloat16)

        return spread_out(high), spread_out(low)

    def box_of(z, y):
        return (slice(None), pl.ds(z + ZP, BOX), pl.ds(y + YP, BOX), slice(None))

    def spread(number, unused):
        adds = []
        for at, counts, pair, rank, z, y in members(number):
            tile = slots_ref[pair, pl.ds(6 * rank, 6), :]
            wz, wy = near_weights(tile, z, y)
            wy = jnp.where(counts, wy, 0.0)
            wx = far_weights(tile[2:3])
            wx_high[at], wx_low[at] = wx
            pulled = tile[3:6][:, None, :] * wz[None]
            coeff = pulled[:, :, None, :] * wy[None, None]
            boxes = product(split(coeff.reshape(3 * BOX * BOX, length)), wx, 1)
            adds.append((box_of(z, y), boxes.reshape(3, BOX, BOX, length)))
        for box, boxes in adds:
            field[box] = field[box] + boxes
        return unused

    lax.fori_loop(0, rounds, spread, 0)
    store = pltpu.make_async_copy(
        field.at[:, ZP : ZP + depth, YP : YP + breadth], new_ref, store_sem
    )
    store.start()

    def sample(number, unused):
        results = []
        for at, counts, pair, rank, z, y in members(number):
            wz, wy = near_weights(slots_ref[pair, pl.ds(6 * rank, 6), :], z, y)
            cells = field[box_of(z, y)].reshape(3 * BOX * BOX, length)
            taken = product(split(cells), (wx_high[at], wx_low[at]), 0)
            taken = taken.reshape(3, BOX, BOX, length)
            summed = jnp.sum(taken * wz[None, :, None, :], axis=1)
            results.append((pair, rank, jnp.sum(summed * wy[None], axis=1)))
        for pair, rank, values in results:
            partial_ref[pair, pl.ds(3 * rank, 3), :] = values
        return unused

    lax.fori_loop(0, rounds, sample, 0)
    store.wait()


def return_kernel(
    rows, columns, target_ref, partial_ref, out_ref,
    side_in, summed, gathered, c_send, c_recv, ab_send, ab_recv,
):
    gz, xy = lax.axis_index("gz"), lax.axis_index("xy")
    wait_greeting = greet(gz, xy, rows, columns)
    wait_greeting()
    has_low, has_high = xy > 0, xy < columns - 1
    copies = []
    for number, (there, column) in enumerate(((has_low, xy - 1), (has_high, xy + 1))):
        copy = pltpu.make_async_remote_copy(
            src_ref=partial_ref.at[number + 1],
            dst_ref=side_in.at[1 - number],
            send_sem=c_send.at[number],
            recv_sem=c_recv.at[1 - number],
            device_id=(gz, column),
            device_id_type=MESH,
        )
        arrival = pltpu.make_async_remote_copy(
            src_ref=partial_ref.at[number + 1],
            dst_ref=side_in.at[number],
            send_sem=c_send.at[number],
            recv_sem=c_recv.at[number],
            device_id=(gz, column),
            device_id_type=MESH,
        )
        copies.append((there, copy))
        pl.when(there)(lambda copy=copy: copy.start())

        @pl.when(jnp.logical_not(there))
        def _(number=number):
            side_in[number] = jnp.zeros(side_in.shape[1:], jnp.float32)

        copies[-1] = (there, copy, arrival)
    for there, copy, arrival in copies:
        pl.when(there)(lambda arrival=arrival: arrival.wait_recv())
    summed[...] = partial_ref[0] + side_in[0] + side_in[1]

    each_peer = peers(gz, xy, rows, columns)

    def block_copy(dr, column):
        return pltpu.make_async_remote_copy(
            src_ref=summed.at[dr + 1, column],
            dst_ref=gathered.at[1 - dr, xy],
            send_sem=ab_send.at[dr + 1],
            recv_sem=ab_recv.at[1 - dr],
            device_id=(gz + dr, column),
            device_id_type=MESH,
        )

    def whole_row(dr):
        span = pl.ds(0, columns - (1 if dr == 0 else 0))
        return pltpu.make_async_remote_copy(
            src_ref=summed.at[dr + 1, span],
            dst_ref=gathered.at[dr + 1, span],
            send_sem=ab_send.at[dr + 1],
            recv_sem=ab_recv.at[dr + 1],
            device_id=(gz, xy),
            device_id_type=MESH,
        )

    each_peer(lambda dr, column: block_copy(dr, column).start())
    gathered[1, xy] = summed[1, xy]

    @pl.when(gz == 0)
    def _():
        gathered[0] = jnp.zeros(gathered.shape[1:], jnp.float32)

    @pl.when(gz == rows - 1)
    def _():
        gathered[2] = jnp.zeros(gathered.shape[1:], jnp.float32)

    each_row(gz, rows, lambda dr: whole_row(dr).wait_recv())
    count = out_ref.shape[1]
    for j in range(count):
        column = target_ref[j]
        rank = jnp.int32(0)
        for earlier in range(j):
            rank = rank + (target_ref[earlier] == column).astype(jnp.int32)
        tile = gathered[0, column] + gathered[1, column] + gathered[2, column]
        out_ref[:, j, :] = jnp.where(rank == 0, tile[0:3], tile[3:6])
    each_row(gz, rows, lambda dr: whole_row(dr).wait_send())
    for there, copy, arrival in copies:
        pl.when(there)(lambda copy=copy: copy.wait_send())


def shards(rows, columns, velocity, viscosity, frac, force, target, z_offset, y_offset):
    parts, depth, breadth, length = velocity.shape
    target = target.reshape(target.shape[0])
    frac, force = jnp.transpose(frac, (1, 0, 2)), jnp.transpose(force, (1, 0, 2))
    held = lambda array: pltpu.with_memory_space_constraint(array, pltpu.HBM)
    velocity, viscosity, frac, force = held(velocity), held(viscosity), held(frac), held(force)
    target, z_offset, y_offset = held(target), held(z_offset), held(y_offset)
    f32 = jnp.float32
    vmem = pl.BlockSpec(memory_space=pltpu.VMEM)
    smem = pl.BlockSpec(memory_space=pltpu.SMEM)
    hbm = pl.BlockSpec(memory_space=pltpu.HBM)
    anyw = pl.BlockSpec(memory_space=pl.ANY)
    dma = pltpu.SemaphoreType.DMA
    pairs = 9 * columns
    listed = pl.cdiv(CAP * pairs, length) * length
    field_shape = (3, depth + 2 * ZP, breadth + 2 * YP, length)
    field, slots, listing = pl.pallas_call(
        functools.partial(exchange_kernel, rows, columns),
        out_shape=(
            jax.ShapeDtypeStruct(field_shape, f32),
            jax.ShapeDtypeStruct((3, 3, columns, PAIR, length), f32),
            jax.ShapeDtypeStruct((8, listed), jnp.int32),
        ),
        in_specs=[smem, smem, smem, hbm, hbm, vmem, vmem],
        out_specs=(vmem, vmem, vmem),
        scratch_shapes=[
            pltpu.VMEM((4, depth + 4, breadth + 16, length), f32),
            pltpu.VMEM((3, depth + 2, breadth + 16, length), f32),
            pltpu.VMEM((columns, PAIR, length), f32),
            pltpu.VMEM((2, 4, 2 * depth, length), f32),
            pltpu.VMEM((2, 4, 2 * depth, length), f32),
            pltpu.VMEM((4, 8, length), f32),
            pltpu.VMEM((4, 8, length), f32),
            dma((2,)), dma((3,)), dma((3,)), dma((4, 2)), dma((4, 2)),
            dma((4,)), dma((4,)), dma((2, 3)), dma((2, 3)),
            pltpu.SemaphoreType.REGULAR((max(columns // CORES - 2, 1), 2)),
        ],
        compiler_params=pltpu.CompilerParams(
            collective_id=0, has_side_effects=True, vmem_limit_bytes=VMEM_LIMIT
        ),
    )(target, z_offset, y_offset, velocity, viscosity, frac, force)

    new_velocity, partial, unused = pl.pallas_call(
        functools.partial(points_kernel, depth, breadth),
        out_shape=(
            jax.ShapeDtypeStruct(velocity.shape, f32),
            jax.ShapeDtypeStruct((pairs, 8, length), f32),
            jax.ShapeDtypeStruct(field_shape, f32),
        ),
        in_specs=[smem, vmem, vmem],
        out_specs=(anyw, vmem, vmem),
        scratch_shapes=[
            pltpu.VMEM((CAP * pairs + TOGETHER, length, length), jnp.bfloat16),
            pltpu.VMEM((CAP * pairs + TOGETHER, length, length), jnp.bfloat16),
            dma(()),
        ],
        input_output_aliases={2: 2},
        compiler_params=pltpu.CompilerParams(vmem_limit_bytes=VMEM_LIMIT),
    )(listing, slots.reshape(pairs, PAIR, length), field)

    point_velocity = pl.pallas_call(
        functools.partial(return_kernel, rows, columns),
        out_shape=jax.ShapeDtypeStruct(frac.shape, f32),
        in_specs=[smem, vmem],
        out_specs=vmem,
        scratch_shapes=[
            pltpu.VMEM((2, 3, columns, 8, length), f32),
            pltpu.VMEM((3, columns, 8, length), f32),
            pltpu.VMEM((3, columns, 8, length), f32),
            dma((2,)), dma((2,)), dma((3,)), dma((3,)),
        ],
        compiler_params=pltpu.CompilerParams(
            collective_id=1, has_side_effects=True, vmem_limit_bytes=VMEM_LIMIT
        ),
    )(target, partial.reshape(3, 3, columns, 8, length))
    return new_velocity, jnp.transpose(point_velocity, (1, 0, 2))


def solution(mesh):
    placed = (
        P(None, "gz", "xy", None),
        P("gz", "xy", None),
        P(("gz", "xy"), None, None),
        P(("gz", "xy"), None, None),
        P(("gz", "xy"), None),
        P(("gz", "xy")),
        P(("gz", "xy")),
    )
    return jax.shard_map(
        functools.partial(shards, mesh.shape["gz"], mesh.shape["xy"]),
        mesh=mesh,
        in_specs=placed,
        out_specs=(P(None, "gz", "xy", None), P(("gz", "xy"), None, None)),
        check_vma=False,
    )
```

```python
import functools

import jax
import jax.numpy as jnp
from jax import lax
from jax.experimental import pallas as pl
from jax.experimental.pallas import tpu as pltpu
from jax.sharding import PartitionSpec as P

BOX = 8
CAP = 2
FAR = 4096.0
ZP = 7
YP = 8
PAIR = 16
USED = 13
KEPT = 6
TOGETHER = 4
CORES = 2
MESH = pl.DeviceIdType.MESH
VMEM_LIMIT = 24 * 1024 * 1024


def each_row(gz, rows, body):
    for dr in (-1, 0, 1):
        inside = jnp.logical_and(gz + dr >= 0, gz + dr < rows)
        pl.when(inside)(functools.partial(body, dr))


def chip_peers(gz, xy, rows, columns, steps):
    chip, core = xy // CORES, xy % CORES
    chips = columns // CORES

    def each(body):
        for step in steps:
            for dr in (0, -1, 1):
                there = (gz + dr >= 0) & (gz + dr < rows) & (chip + step >= 0) & (chip + step < chips)
                for turn in range(CORES):
                    if step == 0 and dr == 0 and turn == 0:
                        continue
                    other = core + turn
                    column = (chip + step) * CORES + jnp.where(other >= CORES, other - CORES, other)
                    pl.when(there)(functools.partial(body, dr, column))

    return each


def staged_greeting(gz, xy, rows, columns, known):
    chip, chips = xy // CORES, columns // CORES
    barrier = pltpu.get_barrier_semaphore()
    near_peers = chip_peers(gz, xy, rows, columns, (0, -1, 1))

    def signal_near(dr, column):
        pl.semaphore_signal(barrier, inc=1, device_id=(gz + dr, column), device_id_type=MESH)

    near_peers(signal_near)
    near_rows = 1 + (gz > 0).astype(jnp.int32) + (gz < rows - 1).astype(jnp.int32)
    near_chips = 1 + (chip > 0).astype(jnp.int32) + (chip < chips - 1).astype(jnp.int32)
    chain = ((chip < chips - 1, xy + CORES), (chip > 0, xy - CORES))

    def tell(reach):
        for number, (there, column) in enumerate(chain):
            pl.when(there)(
                lambda number=number, column=column: pl.semaphore_signal(
                    known.at[reach, number], inc=1, device_id=(gz, column), device_id_type=MESH
                )
            )

    def hear(reach):
        for number, (there, column) in enumerate(chain):
            pl.when(there)(lambda number=number: pl.semaphore_wait(known.at[reach, 1 - number], 1))

    def near():
        pl.semaphore_wait(barrier, near_rows * near_chips * CORES - 1)
        if chips > 2:
            tell(0)
        return near_peers

    def farther():
        for reach in range(chips - 2):
            hear(reach)
            if reach < chips - 3:
                tell(reach + 1)
            yield chip_peers(gz, xy, rows, columns, (-2 - reach, 2 + reach))

    return near, farther


def known_shape(columns):
    return pltpu.SemaphoreType.REGULAR((max(columns // CORES - 2, 1), 2))


def matches(target_ref, count, column):
    first, second = jnp.int32(-1), jnp.int32(-1)
    for j in range(count):
        hit = target_ref[j] == column
        second = jnp.where(jnp.logical_and(hit, jnp.logical_and(first >= 0, second < 0)), j, second)
        first = jnp.where(jnp.logical_and(hit, first < 0), j, first)
    return first, second


def laplace(centre, visc, z_low, z_high, y_low, y_high, coeffs, lane):
    length = centre.shape[-1]
    x_high = jnp.where(lane == length - 1, 0.0, pltpu.roll(centre, length - 1, 1))
    x_low = jnp.where(lane == 0, 0.0, pltpu.roll(centre, 1, 1))
    total = coeffs[0] * (z_high - centre) + coeffs[1] * (z_low - centre)
    total = total + coeffs[2] * (y_high - centre) + coeffs[3] * (y_low - centre)
    total = total + coeffs[4] * (x_high - centre) + coeffs[5] * (x_low - centre)
    return centre + 0.08 * total


def x_coeffs(visc, lane):
    length = visc.shape[-1]
    high = jnp.where(lane == length - 1, 0.0, pltpu.roll(visc, length - 1, 1))
    low = jnp.where(lane == 0, 0.0, pltpu.roll(visc, 1, 1))
    return 0.5 * (visc + high), 0.5 * (visc + low)


def make_list(depth, breadth, slots_ref, list_ref):
    columns, length = slots_ref.shape[2], slots_ref.shape[4]
    pairs, listed = 9 * columns, list_ref.shape[1]
    rows = slots_ref[:, :, :, USED - 1 : USED, :].reshape(pairs, length)
    facts = jnp.transpose(rows)[0:8]
    number = lax.broadcasted_iota(jnp.int32, (1, pairs), 1)
    above = (number >= 3 * columns).astype(jnp.int32)
    below = (number >= 6 * columns).astype(jnp.int32)
    place = number - 3 * columns * (above + below)
    level = (place >= columns).astype(jnp.int32) + (place >= 2 * columns).astype(jnp.int32)
    shift_z = ((level - 1) * depth).astype(jnp.float32)
    shift_y = ((2 * below - above) * breadth).astype(jnp.float32)
    earlier = lax.broadcasted_iota(jnp.int32, (pairs, pairs), 0) < lax.broadcasted_iota(
        jnp.int32, (pairs, pairs), 1
    )
    earlier = earlier.astype(jnp.float32).astype(jnp.bfloat16)
    found = []
    for rank in range(CAP):
        z = facts[2 * rank : 2 * rank + 1] + shift_z
        y = facts[2 * rank + 1 : 2 * rank + 2] + shift_y
        meets = (z > -BOX) & (z < depth) & (y > -BOX) & (y < breadth)
        found.append((z, y, meets, jnp.where(meets, 1.0, 0.0)))
    both = found[0][3] + found[1][3]
    spot = jnp.dot(
        jnp.broadcast_to(both, (BOX, pairs)).astype(jnp.bfloat16), earlier,
        preferred_element_type=jnp.float32,
    )[0:1]
    entry = lax.broadcasted_iota(jnp.int32, (listed, pairs), 0).astype(jnp.float32)
    fact = lax.broadcasted_iota(jnp.int32, (BOX, pairs), 0)
    listing = jnp.zeros((BOX, listed), jnp.float32)
    for rank, (z, y, meets, one) in enumerate(found):
        mine = jnp.where(meets, spot + (found[0][3] if rank else 0.0), -1.0)
        chosen = jnp.where(entry == mine, 1.0, 0.0).astype(jnp.bfloat16)
        told = jnp.where(fact == 0, z, jnp.where(fact == 1, y, number.astype(jnp.float32)))
        told = jnp.where(meets, jnp.where(fact == 3, float(rank), told), 0.0).astype(jnp.bfloat16)
        listing = listing + lax.dot_general(
            told, chosen, (((1,), (1,)), ((), ())), preferred_element_type=jnp.float32
        )
    list_ref[0:4, :] = listing[0:4].astype(jnp.int32)
    total = jnp.sum(both, axis=1, keepdims=True)
    list_ref[4:8, :] = jnp.broadcast_to(total, (4, listed)).astype(jnp.int32)


def exchange_kernel(
    rows, columns, target_hbm, zoff_hbm, yoff_hbm, velocity_ref, viscosity_ref, frac_hbm, force_hbm,
    field_ref, slots_ref, list_ref,
    pad, once, staging, layers_out, layers_in, corner_out, corner_in,
    load_sem, ab_send, ab_recv, halo_send, halo_recv, corner_send, corner_recv, c_send, c_recv, known,
    target_ref, zoff_ref, yoff_ref, frac_ref, force_ref, small_sem,
):
    gz, xy = lax.axis_index("gz"), lax.axis_index("xy")
    depth, breadth = velocity_ref.shape[1], velocity_ref.shape[2]
    length = velocity_ref.shape[3]
    near, farther = staged_greeting(gz, xy, rows, columns, known)
    loads = (
        pltpu.make_async_copy(
            velocity_ref, pad.at[0:3, 2 : 2 + depth, 8 : 8 + breadth], load_sem.at[0]
        ),
        pltpu.make_async_copy(
            viscosity_ref, pad.at[3, 2 : 2 + depth, 8 : 8 + breadth], load_sem.at[1]
        ),
    )
    small = [
        pltpu.make_async_copy(source, place, small_sem.at[number])
        for number, (source, place) in enumerate((
            (target_hbm, target_ref), (zoff_hbm, zoff_ref), (yoff_hbm, yoff_ref),
            (frac_hbm, frac_ref), (force_hbm, force_ref),
        ))
    ]
    for load in small:
        load.start()
    for load in loads:
        load.start()

    lanes = lax.broadcasted_iota(jnp.int32, (1, length), 1)
    count = frac_ref.shape[1]

    def stage(column, unused):
        row = jnp.full((1, length), FAR, jnp.float32)
        for rank, block in enumerate(matches(target_ref, count, column)):
            at = jnp.maximum(block, 0)
            there = block >= 0
            z = jnp.where(there, zoff_ref[at].astype(jnp.float32), FAR)
            y = jnp.where(there, yoff_ref[at].astype(jnp.float32), FAR)
            staging[column, 6 * rank : 6 * rank + 3, :] = frac_ref[:, at, :]
            staging[column, 6 * rank + 3 : 6 * rank + 6, :] = force_ref[:, at, :]
            row = jnp.where(lanes == 2 * rank, z, row)
            row = jnp.where(lanes == 2 * rank + 1, y, row)
        staging[column, 12:13, :] = row
        return unused

    def block_copy(dr, column):
        return pltpu.make_async_remote_copy(
            src_ref=staging.at[column, 0:USED],
            dst_ref=slots_ref.at[0, 1 - dr, xy, 0:USED],
            send_sem=ab_send.at[dr + 1],
            recv_sem=ab_recv.at[1 - dr],
            device_id=(gz + dr, column),
            device_id_type=MESH,
        )

    def whole_row(dr):
        span = pl.ds(0, columns - (1 if dr == 0 else 0))
        return pltpu.make_async_remote_copy(
            src_ref=staging.at[span, 0:USED],
            dst_ref=slots_ref.at[0, dr + 1, span, 0:USED],
            send_sem=ab_send.at[dr + 1],
            recv_sem=ab_recv.at[dr + 1],
            device_id=(gz, xy),
            device_id_type=MESH,
        )

    for load in small:
        load.wait()
    lax.fori_loop(0, columns, stage, 0)
    near_peers = near()

    has = (gz > 0, gz < rows - 1, xy > 0, xy < columns - 1)
    device = ((gz - 1, xy), (gz + 1, xy), (gz, xy - 1), (gz, xy + 1))
    own_y = slice(8, 8 + breadth)
    own_z = slice(2, 2 + depth)

    def halo_copies(side):
        if side == 0:
            cut, land = slice(0, 2), (slice(2 + depth, 4 + depth), own_y)
        elif side == 1:
            cut, land = slice(depth - 2, depth), (slice(0, 2), own_y)
        if side < 2:
            sources = (velocity_ref.at[:, cut], viscosity_ref.at[cut])
            lands = (pad.at[(slice(0, 3),) + land], pad.at[(3,) + land])
        else:
            sources, lands = (layers_out.at[side - 2],), (layers_in.at[3 - side],)
        return [
            pltpu.make_async_remote_copy(
                src_ref=source,
                dst_ref=spot,
                send_sem=halo_send.at[side, number],
                recv_sem=halo_recv.at[side, number],
                device_id=device[side],
                device_id_type=MESH,
            )
            for number, (source, spot) in enumerate(zip(sources, lands))
        ]

    def on_side(side, action):
        @pl.when(has[side])
        def _():
            for copy in halo_copies(side):
                action(copy)


    near_peers(lambda dr, column: block_copy(dr, column).start())
    slots_ref[0, 1, xy, 0:USED] = staging[xy, 0:USED]
    for side in (0, 1):
        on_side(side, lambda copy: copy.start())


    wide, high = field_ref.shape[2], field_ref.shape[1]
    field_ref[:, 0:ZP] = jnp.zeros((3, ZP, wide, length), jnp.float32)
    field_ref[:, ZP + depth :] = jnp.zeros((3, high - ZP - depth, wide, length), jnp.float32)
    field_ref[:, ZP : ZP + depth, 0:YP] = jnp.zeros((3, depth, YP, length), jnp.float32)
    field_ref[:, ZP : ZP + depth, YP + breadth :] = jnp.zeros(
        (3, depth, wide - YP - breadth, length), jnp.float32
    )
    zeros_z = jnp.zeros((4, 2, breadth, length), jnp.float32)
    zeros_y = jnp.zeros((4, depth, 8, length), jnp.float32)

    @pl.when(gz == 0)
    def _():
        pad[:, 0:2, 8 : 8 + breadth, :] = zeros_z
        slots_ref[0, 0] = jnp.full(slots_ref.shape[2:], FAR, jnp.float32)

    @pl.when(gz == rows - 1)
    def _():
        pad[:, 2 + depth : 4 + depth, 8 : 8 + breadth, :] = zeros_z
        slots_ref[0, 2] = jnp.full(slots_ref.shape[2:], FAR, jnp.float32)

    @pl.when(xy == 0)
    def _():
        pad[:, 2 : 2 + depth, 0:8, :] = zeros_y
        slots_ref[1] = jnp.full(slots_ref.shape[1:], FAR, jnp.float32)

    @pl.when(xy == columns - 1)
    def _():
        pad[:, 2 : 2 + depth, 8 + breadth : 16 + breadth, :] = zeros_y
        slots_ref[2] = jnp.full(slots_ref.shape[1:], FAR, jnp.float32)

    for load in loads:
        load.wait()
    for side, start in ((2, 8), (3, 6 + breadth)):
        for part in range(4):
            for layer in range(2):
                layers_out[side - 2, part, layer * depth : (layer + 1) * depth, :] = pad[
                    part, 2 : 2 + depth, start + layer, :
                ]
        on_side(side, lambda copy: copy.start())

    corners = []
    for number, (dz, dy) in enumerate(((-1, -1), (-1, 1), (1, -1), (1, 1))):
        z_in = 2 if dz < 0 else 1 + depth
        y_in = 8 if dy < 0 else 7 + breadth
        z_out = 1 if dz < 0 else 2 + depth
        y_out = 7 if dy < 0 else 8 + breadth
        present = jnp.logical_and(has[0 if dz < 0 else 1], has[2 if dy < 0 else 3])
        for part in range(4):
            corner_out[number, part : part + 1, :] = pad[part, z_in, y_in : y_in + 1, :]
        copy = pltpu.make_async_remote_copy(
            src_ref=corner_out.at[number],
            dst_ref=corner_in.at[3 - number],
            send_sem=corner_send.at[number],
            recv_sem=corner_recv.at[3 - number],
            device_id=(gz + dz, xy + dy),
            device_id_type=MESH,
        )
        arrival = pltpu.make_async_remote_copy(
            src_ref=corner_out.at[number],
            dst_ref=corner_in.at[number],
            send_sem=corner_send.at[number],
            recv_sem=corner_recv.at[number],
            device_id=(gz + dz, xy + dy),
            device_id_type=MESH,
        )
        corners.append((present, copy, arrival, number, z_out, y_out))
    for present, copy, arrival, number, z_out, y_out in corners:
        pl.when(present)(lambda copy=copy: copy.start())

    for far_peers in farther():
        far_peers(lambda dr, column: block_copy(dr, column).start())

    lane = lax.broadcasted_iota(jnp.int32, (breadth + 16, length), 1)
    line = lax.broadcasted_iota(jnp.int32, (breadth + 16, length), 0)
    low_y = jnp.where(xy > 0, 0, 8)
    high_y = jnp.where(xy < columns - 1, breadth + 16, breadth + 8)
    in_grid = jnp.logical_and(line >= low_y, line < high_y)
    first_z = jnp.where(gz > 0, 0, 2)
    last_z = jnp.where(gz < rows - 1, depth + 3, depth + 1)

    def first_sweep(z):
        visc = pad[3, z]
        size = visc.shape[0]
        cx_high, cx_low = x_coeffs(visc, lane)
        coeffs = (
            0.5 * (visc + pad[3, z + 1]),
            0.5 * (visc + pad[3, z - 1]),
            0.5 * (visc + pltpu.roll(visc, size - 1, 0)),
            0.5 * (visc + pltpu.roll(visc, 1, 0)),
            cx_high,
            cx_low,
        )
        z_inside = jnp.logical_and(z >= first_z, z <= last_z)
        keep = jnp.logical_and(in_grid, z_inside)
        for part in range(3):
            centre = pad[part, z]
            new = laplace(
                centre, visc, pad[part, z - 1], pad[part, z + 1],
                pltpu.roll(centre, 1, 0), pltpu.roll(centre, size - 1, 0), coeffs, lane,
            )
            once[part, z - 1] = jnp.where(keep, new, 0.0)

    own_lane = lane[:breadth]

    def second_sweep(z):
        visc = pad[3, z, 8 : 8 + breadth, :]
        cx_high, cx_low = x_coeffs(visc, own_lane)
        coeffs = (
            0.5 * (visc + pad[3, z + 1, 8 : 8 + breadth, :]),
            0.5 * (visc + pad[3, z - 1, 8 : 8 + breadth, :]),
            0.5 * (visc + pad[3, z, 9 : 9 + breadth, :]),
            0.5 * (visc + pad[3, z, 7 : 7 + breadth, :]),
            cx_high,
            cx_low,
        )
        for part in range(3):
            field_ref[part, z - 2 + ZP, YP : YP + breadth, :] = laplace(
                once[part, z - 1, 8 : 8 + breadth, :], visc,
                once[part, z - 2, 8 : 8 + breadth, :], once[part, z, 8 : 8 + breadth, :],
                once[part, z - 1, 7 : 7 + breadth, :], once[part, z - 1, 9 : 9 + breadth, :],
                coeffs, own_lane,
            )

    def loop(low, high, body):
        def step(z, unused):
            body(z)
            return unused

        lax.fori_loop(low, high, step, 0)

    arrives = ((1, 0), (0, 1), (3, 2), (2, 3))

    def wait_side(side, neighbour):
        @pl.when(has[neighbour])
        def _():
            for copy in halo_copies(side):
                copy.wait_recv()
            if side >= 2:
                start = 6 if side == 3 else 8 + breadth
                for part in range(4):
                    for layer in range(2):
                        pad[part, 2 : 2 + depth, start + layer, :] = layers_in[
                            3 - side, part, layer * depth : (layer + 1) * depth, :
                        ]

    forwards = []
    for number, (there, column, side) in enumerate(((has[3], xy + 1, 1), (has[2], xy - 1, 2))):
        for dr in (-1, 0, 1):
            copy = pltpu.make_async_remote_copy(
                src_ref=slots_ref.at[0, dr + 1, :, 0:USED],
                dst_ref=slots_ref.at[side, dr + 1, :, 0:USED],
                send_sem=c_send.at[number, dr + 1],
                recv_sem=c_recv.at[number, dr + 1],
                device_id=(gz, column),
                device_id_type=MESH,
            )
            forwards.append((there, copy, dr, has[2 + number]))

    def forward(row):
        for there, copy, dr, unused in forwards:
            if dr == row:
                pl.when(there)(lambda copy=copy: copy.start())

    wait_side(2, 3)
    wait_side(3, 2)
    loop(3, 1 + depth, first_sweep)
    whole_row(0).wait_recv()
    forward(0)
    middle = 4 + (depth - 4) // 2
    loop(4, middle, second_sweep)
    for dr in (-1, 1):
        pl.when(has[0 if dr < 0 else 1])(lambda dr=dr: whole_row(dr).wait_recv())
        forward(dr)
    loop(middle, depth, second_sweep)

    wait_side(0, 1)
    wait_side(1, 0)
    for present, copy, arrival, number, z_out, y_out in corners:

        @pl.when(present)
        def _(arrival=arrival, number=number, z_out=z_out, y_out=y_out):
            arrival.wait_recv()
            for part in range(4):
                pad[part, z_out, y_out : y_out + 1, :] = corner_in[number, part : part + 1, :]

        @pl.when(jnp.logical_not(present))
        def _(z_out=z_out, y_out=y_out):
            for part in range(4):
                pad[part, z_out, y_out : y_out + 1, :] = jnp.zeros((1, length), jnp.float32)

    for z in (1, 2, 1 + depth, 2 + depth):
        first_sweep(z)
    for z in (2, 3, depth, 1 + depth):
        second_sweep(z)

    for unused, copy, dr, comes in forwards:
        pl.when(comes)(lambda copy=copy: copy.wait_recv())
    make_list(depth, breadth, slots_ref, list_ref)
    each_row(gz, rows, lambda dr: whole_row(dr).wait_send())
    for side in range(4):
        on_side(side, lambda copy: copy.wait_send())
    for present, copy, arrival, number, z_out, y_out in corners:
        pl.when(present)(lambda copy=copy: copy.wait_send())
    for there, copy, unused, comes in forwards:
        pl.when(there)(lambda copy=copy: copy.wait_send())


def phi(radius):
    x2 = radius * radius * 0.6168502750680849
    c = 1.0 / 479001600.0
    for factor in (-1.0 / 3628800.0, 1.0 / 40320.0, -1.0 / 720.0, 1.0 / 24.0, -0.5, 1.0):
        c = c * x2 + factor
    return jnp.where(jnp.abs(radius) < 2.0, 0.5 * c * c, 0.0)


def split(value):
    high = value.astype(jnp.bfloat16)
    return high, (value - high.astype(jnp.float32)).astype(jnp.bfloat16)


def product(left, right, contract):
    (left_high, left_low), (right_high, right_low) = left, right
    return lax.dot_general(
        jnp.concatenate([left_high, left_low, left_high], axis=1),
        jnp.concatenate([right_high, right_high, right_low], axis=contract),
        (((1,), (contract,)), ((), ())),
        preferred_element_type=jnp.float32,
    )


def points_kernel(
    depth, breadth, list_ref, slots_ref, field_in, new_ref, partial_ref, field, wx_high, wx_low, store_sem
):
    length = field.shape[3]
    partial_ref[...] = jnp.zeros_like(partial_ref)
    found = list_ref[4, 0]
    rounds = (found + TOGETHER - 1) // TOGETHER

    line = lax.broadcasted_iota(jnp.int32, (BOX, length), 0)
    rel = line.astype(jnp.float32)
    far = lax.broadcasted_iota(jnp.int32, (length, length), 0).astype(jnp.float32)

    def members(number):
        for other in range(TOGETHER):
            at = number * TOGETHER + other
            spot = jnp.minimum(at, found - 1)
            z, y, pair, rank = (list_ref[row, spot] for row in range(4))
            yield at, at < found, pair, rank, z, y

    def near_weights(frac, z, y):
        wz = phi(2.0 + (BOX - 5) * frac[0:1] - rel)
        wy = phi(2.0 + (BOX - 5) * frac[1:2] - rel)
        wz = jnp.where((z + line >= 0) & (z + line < depth), wz, 0.0)
        wy = jnp.where((y + line >= 0) & (y + line < breadth), wy, 0.0)
        return wz, wy

    def far_weights(frac):
        at = 2.0 + (length - 5) * frac
        near = at - rel
        base = phi(near - 4.0 * jnp.floor(0.25 * near + 0.5))
        high = base.astype(jnp.bfloat16).astype(jnp.float32)
        low = base - high
        inside = jnp.abs(at - far) < 2.0

        def spread_out(part):
            whole = jnp.broadcast_to(part[None], (length // BOX, BOX, length)).reshape(length, length)
            return jnp.where(inside, whole, 0.0).astype(jnp.bfloat16)

        return spread_out(high), spread_out(low)

    def box_of(z, y):
        return (slice(None), pl.ds(z + ZP, BOX), pl.ds(y + YP, BOX), slice(None))

    def spread(number, unused):
        adds = []
        for at, counts, pair, rank, z, y in members(number):
            tile = slots_ref[pair, pl.ds(6 * rank, 6), :]
            wz, wy = near_weights(tile, z, y)
            wy = jnp.where(counts, wy, 0.0)
            wx = far_weights(tile[2:3])
            wx_high[at], wx_low[at] = wx
            pulled = tile[3:6][:, None, :] * wz[None]
            coeff = pulled[:, :, None, :] * wy[None, None]
            boxes = product(split(coeff.reshape(3 * BOX * BOX, length)), wx, 1)
            adds.append((box_of(z, y), boxes.reshape(3, BOX, BOX, length)))
        for box, boxes in adds:
            field[box] = field[box] + boxes
        return unused

    lax.fori_loop(0, rounds, spread, 0)
    store = pltpu.make_async_copy(
        field.at[:, ZP : ZP + depth, YP : YP + breadth], new_ref, store_sem
    )
    store.start()

    def sample(number, unused):
        results = []
        for at, counts, pair, rank, z, y in members(number):
            wz, wy = near_weights(slots_ref[pair, pl.ds(6 * rank, 6), :], z, y)
            cells = field[box_of(z, y)].reshape(3 * BOX * BOX, length)
            taken = product(split(cells), (wx_high[at], wx_low[at]), 0)
            taken = taken.reshape(3, BOX, BOX, length)
            summed = jnp.sum(taken * wz[None, :, None, :], axis=1)
            results.append((pair, rank, jnp.sum(summed * wy[None], axis=1)))
        for pair, rank, values in results:
            partial_ref[pair, pl.ds(3 * rank, 3), :] = values
        return unused

    lax.fori_loop(0, rounds, sample, 0)
    store.wait()


def return_kernel(
    rows, columns, target_hbm, partial_ref, out_ref,
    side_in, summed, gathered, c_send, c_recv, ab_send, ab_recv, known, target_ref, target_sem,
):
    gz, xy = lax.axis_index("gz"), lax.axis_index("xy")
    near, farther = staged_greeting(gz, xy, rows, columns, known)
    target_load = pltpu.make_async_copy(target_hbm, target_ref, target_sem)
    target_load.start()
    has_low, has_high = xy > 0, xy < columns - 1
    sides = ((has_low, xy - 1), (has_high, xy + 1))

    def side_copy(number, column, landing):
        return pltpu.make_async_remote_copy(
            src_ref=partial_ref.at[number + 1, :, :, 0:KEPT],
            dst_ref=side_in.at[landing, :, :, 0:KEPT],
            send_sem=c_send.at[number],
            recv_sem=c_recv.at[landing],
            device_id=(gz, column),
            device_id_type=MESH,
        )

    near_peers = near()
    for number, (there, column) in enumerate(sides):
        pl.when(there)(
            lambda number=number, column=column: side_copy(number, column, 1 - number).start()
        )

        @pl.when(jnp.logical_not(there))
        def _(number=number):
            side_in[number] = jnp.zeros(side_in.shape[1:], jnp.float32)

    def block_copy(dr, column):
        return pltpu.make_async_remote_copy(
            src_ref=summed.at[dr + 1, column, 0:KEPT],
            dst_ref=gathered.at[1 - dr, xy, 0:KEPT],
            send_sem=ab_send.at[dr + 1],
            recv_sem=ab_recv.at[1 - dr],
            device_id=(gz + dr, column),
            device_id_type=MESH,
        )

    def whole_row(dr):
        span = pl.ds(0, columns - (1 if dr == 0 else 0))
        return pltpu.make_async_remote_copy(
            src_ref=summed.at[dr + 1, span, 0:KEPT],
            dst_ref=gathered.at[dr + 1, span, 0:KEPT],
            send_sem=ab_send.at[dr + 1],
            recv_sem=ab_recv.at[dr + 1],
            device_id=(gz, xy),
            device_id_type=MESH,
        )

    @pl.when(gz == 0)
    def _():
        gathered[0] = jnp.zeros(gathered.shape[1:], jnp.float32)

    @pl.when(gz == rows - 1)
    def _():
        gathered[2] = jnp.zeros(gathered.shape[1:], jnp.float32)

    far_peers = list(farther())
    for number, (there, column) in enumerate(sides):
        pl.when(there)(
            lambda number=number, column=column: side_copy(number, column, number).wait_recv()
        )
    summed[:, :, 0:KEPT] = (
        partial_ref[0, :, :, 0:KEPT] + side_in[0, :, :, 0:KEPT] + side_in[1, :, :, 0:KEPT]
    )
    for group in far_peers[::-1] + [near_peers]:
        group(lambda dr, column: block_copy(dr, column).start())
    gathered[1, xy, 0:KEPT] = summed[1, xy, 0:KEPT]

    target_load.wait()
    count = out_ref.shape[1]
    ranks = []
    for j in range(count):
        rank = jnp.int32(0)
        for earlier in range(j):
            rank = rank + (target_ref[earlier] == target_ref[j]).astype(jnp.int32)
        ranks.append(rank)
    each_row(gz, rows, lambda dr: whole_row(dr).wait_recv())
    for j, rank in enumerate(ranks):
        column = target_ref[j]
        tile = gathered[0, column] + gathered[1, column] + gathered[2, column]
        out_ref[:, j, :] = jnp.where(rank == 0, tile[0:3], tile[3:KEPT])
    each_row(gz, rows, lambda dr: whole_row(dr).wait_send())
    for number, (there, column) in enumerate(sides):
        pl.when(there)(
            lambda number=number, column=column: side_copy(number, column, number).wait_send()
        )


def shards(rows, columns, velocity, viscosity, frac, force, target, z_offset, y_offset):
    parts, depth, breadth, length = velocity.shape
    target = target.reshape(target.shape[0])
    frac, force = jnp.transpose(frac, (1, 0, 2)), jnp.transpose(force, (1, 0, 2))
    held = lambda array: pltpu.with_memory_space_constraint(array, pltpu.HBM)
    velocity, viscosity, frac, force = held(velocity), held(viscosity), held(frac), held(force)
    target, z_offset, y_offset = held(target), held(z_offset), held(y_offset)
    f32 = jnp.float32
    vmem = pl.BlockSpec(memory_space=pltpu.VMEM)
    smem = pl.BlockSpec(memory_space=pltpu.SMEM)
    hbm = pl.BlockSpec(memory_space=pltpu.HBM)
    anyw = pl.BlockSpec(memory_space=pl.ANY)
    dma = pltpu.SemaphoreType.DMA
    pairs = 9 * columns
    listed = pl.cdiv(CAP * pairs, length) * length
    field_shape = (3, depth + 2 * ZP, breadth + 2 * YP, length)
    field, slots, listing = pl.pallas_call(
        functools.partial(exchange_kernel, rows, columns),
        out_shape=(
            jax.ShapeDtypeStruct(field_shape, f32),
            jax.ShapeDtypeStruct((3, 3, columns, PAIR, length), f32),
            jax.ShapeDtypeStruct((8, listed), jnp.int32),
        ),
        in_specs=[hbm] * 7,
        out_specs=(vmem, vmem, vmem),
        scratch_shapes=[
            pltpu.VMEM((4, depth + 4, breadth + 16, length), f32),
            pltpu.VMEM((3, depth + 2, breadth + 16, length), f32),
            pltpu.VMEM((columns, PAIR, length), f32),
            pltpu.VMEM((2, 4, 2 * depth, length), f32),
            pltpu.VMEM((2, 4, 2 * depth, length), f32),
            pltpu.VMEM((4, 8, length), f32),
            pltpu.VMEM((4, 8, length), f32),
            dma((2,)), dma((3,)), dma((3,)), dma((4, 2)), dma((4, 2)),
            dma((4,)), dma((4,)), dma((2, 3)), dma((2, 3)),
            known_shape(columns),
            pltpu.SMEM(target.shape, jnp.int32),
            pltpu.SMEM(target.shape, jnp.int32),
            pltpu.SMEM(target.shape, jnp.int32),
            pltpu.VMEM(frac.shape, f32),
            pltpu.VMEM(force.shape, f32),
            dma((5,)),
        ],
        compiler_params=pltpu.CompilerParams(
            collective_id=0, has_side_effects=True, vmem_limit_bytes=VMEM_LIMIT
        ),
    )(target, z_offset, y_offset, velocity, viscosity, frac, force)

    new_velocity, partial, unused = pl.pallas_call(
        functools.partial(points_kernel, depth, breadth),
        out_shape=(
            jax.ShapeDtypeStruct(velocity.shape, f32),
            jax.ShapeDtypeStruct((pairs, 8, length), f32),
            jax.ShapeDtypeStruct(field_shape, f32),
        ),
        in_specs=[smem, vmem, vmem],
        out_specs=(anyw, vmem, vmem),
        scratch_shapes=[
            pltpu.VMEM((CAP * pairs + TOGETHER, length, length), jnp.bfloat16),
            pltpu.VMEM((CAP * pairs + TOGETHER, length, length), jnp.bfloat16),
            dma(()),
        ],
        input_output_aliases={2: 2},
        compiler_params=pltpu.CompilerParams(vmem_limit_bytes=VMEM_LIMIT),
    )(listing, slots.reshape(pairs, PAIR, length), field)

    point_velocity = pl.pallas_call(
        functools.partial(return_kernel, rows, columns),
        out_shape=jax.ShapeDtypeStruct(frac.shape, f32),
        in_specs=[hbm, vmem],
        out_specs=vmem,
        scratch_shapes=[
            pltpu.VMEM((2, 3, columns, 8, length), f32),
            pltpu.VMEM((3, columns, 8, length), f32),
            pltpu.VMEM((3, columns, 8, length), f32),
            dma((2,)), dma((2,)), dma((3,)), dma((3,)), known_shape(columns),
            pltpu.SMEM(target.shape, jnp.int32), dma(()),
        ],
        compiler_params=pltpu.CompilerParams(
            collective_id=1, has_side_effects=True, vmem_limit_bytes=VMEM_LIMIT
        ),
    )(target, partial.reshape(3, 3, columns, 8, length))
    return new_velocity, jnp.transpose(point_velocity, (1, 0, 2))


def solution(mesh):
    placed = (
        P(None, "gz", "xy", None),
        P("gz", "xy", None),
        P(("gz", "xy"), None, None),
        P(("gz", "xy"), None, None),
        P(("gz", "xy"), None),
        P(("gz", "xy")),
        P(("gz", "xy")),
    )
    return jax.shard_map(
        functools.partial(shards, mesh.shape["gz"], mesh.shape["xy"]),
        mesh=mesh,
        in_specs=placed,
        out_specs=(P(None, "gz", "xy", None), P(("gz", "xy"), None, None)),
        check_vma=False,
    )
```

```python
import functools

import jax
import jax.numpy as jnp
from jax import lax
from jax.experimental import pallas as pl
from jax.experimental.pallas import tpu as pltpu
from jax.sharding import PartitionSpec as P

BOX = 8
CAP = 2
FAR = 4096.0
ZP = 7
YP = 8
PAIR = 16
USED = 13
KEPT = 6
TOGETHER = 8
CORES = 2
MESH = pl.DeviceIdType.MESH
VMEM_LIMIT = 24 * 1024 * 1024


def each_row(gz, rows, body):
    for dr in (-1, 0, 1):
        inside = jnp.logical_and(gz + dr >= 0, gz + dr < rows)
        pl.when(inside)(functools.partial(body, dr))


def chip_peers(gz, xy, rows, columns, steps):
    chip, core = xy // CORES, xy % CORES
    chips = columns // CORES

    def each(body):
        for step in steps:
            for dr in (0, -1, 1):
                there = (gz + dr >= 0) & (gz + dr < rows) & (chip + step >= 0) & (chip + step < chips)
                for turn in range(CORES):
                    if step == 0 and dr == 0 and turn == 0:
                        continue
                    other = core + turn
                    column = (chip + step) * CORES + jnp.where(other >= CORES, other - CORES, other)
                    pl.when(there)(functools.partial(body, dr, column))

    return each


def staged_greeting(gz, xy, rows, columns, known):
    chip, chips = xy // CORES, columns // CORES
    barrier = pltpu.get_barrier_semaphore()
    near_peers = chip_peers(gz, xy, rows, columns, (0, -1, 1))

    def signal_near(dr, column):
        pl.semaphore_signal(barrier, inc=1, device_id=(gz + dr, column), device_id_type=MESH)

    near_peers(signal_near)
    near_rows = 1 + (gz > 0).astype(jnp.int32) + (gz < rows - 1).astype(jnp.int32)
    near_chips = 1 + (chip > 0).astype(jnp.int32) + (chip < chips - 1).astype(jnp.int32)
    chain = ((chip < chips - 1, xy + CORES), (chip > 0, xy - CORES))

    def tell(reach):
        for number, (there, column) in enumerate(chain):
            pl.when(there)(
                lambda number=number, column=column: pl.semaphore_signal(
                    known.at[reach, number], inc=1, device_id=(gz, column), device_id_type=MESH
                )
            )

    def hear(reach):
        for number, (there, column) in enumerate(chain):
            pl.when(there)(lambda number=number: pl.semaphore_wait(known.at[reach, 1 - number], 1))

    def near():
        pl.semaphore_wait(barrier, near_rows * near_chips * CORES - 1)
        if chips > 2:
            tell(0)
        return near_peers

    def farther():
        for reach in range(chips - 2):
            hear(reach)
            if reach < chips - 3:
                tell(reach + 1)
            yield chip_peers(gz, xy, rows, columns, (-2 - reach, 2 + reach))

    return near, farther


def known_shape(columns):
    return pltpu.SemaphoreType.REGULAR((max(columns // CORES - 2, 1), 2))


def matches(target_ref, count, column):
    first, second = jnp.int32(-1), jnp.int32(-1)
    for j in range(count):
        hit = target_ref[j] == column
        second = jnp.where(jnp.logical_and(hit, jnp.logical_and(first >= 0, second < 0)), j, second)
        first = jnp.where(jnp.logical_and(hit, first < 0), j, first)
    return first, second


def laplace(centre, visc, z_low, z_high, y_low, y_high, coeffs, lane):
    length = centre.shape[-1]
    x_high = jnp.where(lane == length - 1, 0.0, pltpu.roll(centre, length - 1, 1))
    x_low = jnp.where(lane == 0, 0.0, pltpu.roll(centre, 1, 1))
    total = coeffs[0] * (z_high - centre) + coeffs[1] * (z_low - centre)
    total = total + coeffs[2] * (y_high - centre) + coeffs[3] * (y_low - centre)
    total = total + coeffs[4] * (x_high - centre) + coeffs[5] * (x_low - centre)
    return centre + 0.08 * total


def x_coeffs(visc, lane):
    length = visc.shape[-1]
    high = jnp.where(lane == length - 1, 0.0, pltpu.roll(visc, length - 1, 1))
    low = jnp.where(lane == 0, 0.0, pltpu.roll(visc, 1, 1))
    return 0.5 * (visc + high), 0.5 * (visc + low)


def make_list(depth, breadth, slots_ref, list_ref):
    columns, length = slots_ref.shape[2], slots_ref.shape[4]
    pairs, listed = 9 * columns, list_ref.shape[1]
    rows = slots_ref[:, :, :, USED - 1 : USED, :].reshape(pairs, length)
    facts = jnp.transpose(rows)[0:8]
    number = lax.broadcasted_iota(jnp.int32, (1, pairs), 1)
    above = (number >= 3 * columns).astype(jnp.int32)
    below = (number >= 6 * columns).astype(jnp.int32)
    place = number - 3 * columns * (above + below)
    level = (place >= columns).astype(jnp.int32) + (place >= 2 * columns).astype(jnp.int32)
    shift_z = ((level - 1) * depth).astype(jnp.float32)
    shift_y = ((2 * below - above) * breadth).astype(jnp.float32)
    earlier = lax.broadcasted_iota(jnp.int32, (pairs, pairs), 0) < lax.broadcasted_iota(
        jnp.int32, (pairs, pairs), 1
    )
    earlier = earlier.astype(jnp.float32).astype(jnp.bfloat16)
    found = []
    for rank in range(CAP):
        z = facts[2 * rank : 2 * rank + 1] + shift_z
        y = facts[2 * rank + 1 : 2 * rank + 2] + shift_y
        meets = (z > -BOX) & (z < depth) & (y > -BOX) & (y < breadth)
        found.append((z, y, meets, jnp.where(meets, 1.0, 0.0)))
    both = found[0][3] + found[1][3]
    spot = jnp.dot(
        jnp.broadcast_to(both, (BOX, pairs)).astype(jnp.bfloat16), earlier,
        preferred_element_type=jnp.float32,
    )[0:1]
    entry = lax.broadcasted_iota(jnp.int32, (listed, pairs), 0).astype(jnp.float32)
    fact = lax.broadcasted_iota(jnp.int32, (BOX, pairs), 0)
    listing = jnp.zeros((BOX, listed), jnp.float32)
    for rank, (z, y, meets, one) in enumerate(found):
        mine = jnp.where(meets, spot + (found[0][3] if rank else 0.0), -1.0)
        chosen = jnp.where(entry == mine, 1.0, 0.0).astype(jnp.bfloat16)
        told = jnp.where(fact == 0, z, jnp.where(fact == 1, y, number.astype(jnp.float32)))
        told = jnp.where(meets, jnp.where(fact == 3, float(rank), told), 0.0).astype(jnp.bfloat16)
        listing = listing + lax.dot_general(
            told, chosen, (((1,), (1,)), ((), ())), preferred_element_type=jnp.float32
        )
    list_ref[0:4, :] = listing[0:4].astype(jnp.int32)
    total = jnp.sum(both, axis=1, keepdims=True)
    list_ref[4:8, :] = jnp.broadcast_to(total, (4, listed)).astype(jnp.int32)


def exchange_kernel(
    rows, columns, target_hbm, zoff_hbm, yoff_hbm, velocity_ref, viscosity_ref, frac_hbm, force_hbm,
    field_ref, slots_ref, list_ref,
    pad, once, staging, layers_out, layers_in, corner_out, corner_in,
    load_sem, ab_send, ab_recv, halo_send, halo_recv, corner_send, corner_recv, c_send, c_recv, known,
    target_ref, zoff_ref, yoff_ref, frac_ref, force_ref, small_sem,
):
    gz, xy = lax.axis_index("gz"), lax.axis_index("xy")
    depth, breadth = velocity_ref.shape[1], velocity_ref.shape[2]
    length = velocity_ref.shape[3]
    near, farther = staged_greeting(gz, xy, rows, columns, known)
    loads = (
        pltpu.make_async_copy(
            velocity_ref, pad.at[0:3, 2 : 2 + depth, 8 : 8 + breadth], load_sem.at[0]
        ),
        pltpu.make_async_copy(
            viscosity_ref, pad.at[3, 2 : 2 + depth, 8 : 8 + breadth], load_sem.at[1]
        ),
    )
    small = [
        pltpu.make_async_copy(source, place, small_sem.at[number])
        for number, (source, place) in enumerate((
            (target_hbm, target_ref), (zoff_hbm, zoff_ref), (yoff_hbm, yoff_ref),
            (frac_hbm, frac_ref), (force_hbm, force_ref),
        ))
    ]
    for load in small:
        load.start()
    for load in loads:
        load.start()

    lanes = lax.broadcasted_iota(jnp.int32, (1, length), 1)
    count = frac_ref.shape[1]

    def stage(column, unused):
        row = jnp.full((1, length), FAR, jnp.float32)
        for rank, block in enumerate(matches(target_ref, count, column)):
            at = jnp.maximum(block, 0)
            there = block >= 0
            z = jnp.where(there, zoff_ref[at].astype(jnp.float32), FAR)
            y = jnp.where(there, yoff_ref[at].astype(jnp.float32), FAR)
            staging[column, 6 * rank : 6 * rank + 3, :] = frac_ref[:, at, :]
            staging[column, 6 * rank + 3 : 6 * rank + 6, :] = force_ref[:, at, :]
            row = jnp.where(lanes == 2 * rank, z, row)
            row = jnp.where(lanes == 2 * rank + 1, y, row)
        staging[column, 12:13, :] = row
        return unused

    def block_copy(dr, column):
        return pltpu.make_async_remote_copy(
            src_ref=staging.at[column, 0:USED],
            dst_ref=slots_ref.at[0, 1 - dr, xy, 0:USED],
            send_sem=ab_send.at[dr + 1],
            recv_sem=ab_recv.at[1 - dr],
            device_id=(gz + dr, column),
            device_id_type=MESH,
        )

    def whole_row(dr):
        span = pl.ds(0, columns - (1 if dr == 0 else 0))
        return pltpu.make_async_remote_copy(
            src_ref=staging.at[span, 0:USED],
            dst_ref=slots_ref.at[0, dr + 1, span, 0:USED],
            send_sem=ab_send.at[dr + 1],
            recv_sem=ab_recv.at[dr + 1],
            device_id=(gz, xy),
            device_id_type=MESH,
        )

    for load in small:
        load.wait()
    lax.fori_loop(0, columns, stage, 0)
    near_peers = near()

    has = (gz > 0, gz < rows - 1, xy > 0, xy < columns - 1)
    device = ((gz - 1, xy), (gz + 1, xy), (gz, xy - 1), (gz, xy + 1))
    own_y = slice(8, 8 + breadth)
    own_z = slice(2, 2 + depth)

    def halo_copies(side):
        if side == 0:
            cut, land = slice(0, 2), (slice(2 + depth, 4 + depth), own_y)
        elif side == 1:
            cut, land = slice(depth - 2, depth), (slice(0, 2), own_y)
        if side < 2:
            sources = (velocity_ref.at[:, cut], viscosity_ref.at[cut])
            lands = (pad.at[(slice(0, 3),) + land], pad.at[(3,) + land])
        else:
            sources, lands = (layers_out.at[side - 2],), (layers_in.at[3 - side],)
        return [
            pltpu.make_async_remote_copy(
                src_ref=source,
                dst_ref=spot,
                send_sem=halo_send.at[side, number],
                recv_sem=halo_recv.at[side, number],
                device_id=device[side],
                device_id_type=MESH,
            )
            for number, (source, spot) in enumerate(zip(sources, lands))
        ]

    def on_side(side, action):
        @pl.when(has[side])
        def _():
            for copy in halo_copies(side):
                action(copy)


    near_peers(lambda dr, column: block_copy(dr, column).start())
    slots_ref[0, 1, xy, 0:USED] = staging[xy, 0:USED]


    wide, high = field_ref.shape[2], field_ref.shape[1]
    field_ref[:, 0:ZP] = jnp.zeros((3, ZP, wide, length), jnp.float32)
    field_ref[:, ZP + depth :] = jnp.zeros((3, high - ZP - depth, wide, length), jnp.float32)
    field_ref[:, ZP : ZP + depth, 0:YP] = jnp.zeros((3, depth, YP, length), jnp.float32)
    field_ref[:, ZP : ZP + depth, YP + breadth :] = jnp.zeros(
        (3, depth, wide - YP - breadth, length), jnp.float32
    )
    zeros_z = jnp.zeros((4, 2, breadth, length), jnp.float32)
    zeros_y = jnp.zeros((4, depth, 8, length), jnp.float32)

    @pl.when(gz == 0)
    def _():
        pad[:, 0:2, 8 : 8 + breadth, :] = zeros_z
        slots_ref[0, 0] = jnp.full(slots_ref.shape[2:], FAR, jnp.float32)

    @pl.when(gz == rows - 1)
    def _():
        pad[:, 2 + depth : 4 + depth, 8 : 8 + breadth, :] = zeros_z
        slots_ref[0, 2] = jnp.full(slots_ref.shape[2:], FAR, jnp.float32)

    @pl.when(xy == 0)
    def _():
        pad[:, 2 : 2 + depth, 0:8, :] = zeros_y
        slots_ref[1] = jnp.full(slots_ref.shape[1:], FAR, jnp.float32)

    @pl.when(xy == columns - 1)
    def _():
        pad[:, 2 : 2 + depth, 8 + breadth : 16 + breadth, :] = zeros_y
        slots_ref[2] = jnp.full(slots_ref.shape[1:], FAR, jnp.float32)

    for load in loads:
        load.wait()
    for side, start in ((2, 8), (3, 6 + breadth)):
        for part in range(4):
            for layer in range(2):
                layers_out[side - 2, part, layer * depth : (layer + 1) * depth, :] = pad[
                    part, 2 : 2 + depth, start + layer, :
                ]
        on_side(side, lambda copy: copy.start())

    corners = []
    for number, (dz, dy) in enumerate(((-1, -1), (-1, 1), (1, -1), (1, 1))):
        z_in = 2 if dz < 0 else 1 + depth
        y_in = 8 if dy < 0 else 7 + breadth
        z_out = 1 if dz < 0 else 2 + depth
        y_out = 7 if dy < 0 else 8 + breadth
        present = jnp.logical_and(has[0 if dz < 0 else 1], has[2 if dy < 0 else 3])
        for part in range(4):
            corner_out[number, part : part + 1, :] = pad[part, z_in, y_in : y_in + 1, :]
        copy = pltpu.make_async_remote_copy(
            src_ref=corner_out.at[number],
            dst_ref=corner_in.at[3 - number],
            send_sem=corner_send.at[number],
            recv_sem=corner_recv.at[3 - number],
            device_id=(gz + dz, xy + dy),
            device_id_type=MESH,
        )
        arrival = pltpu.make_async_remote_copy(
            src_ref=corner_out.at[number],
            dst_ref=corner_in.at[number],
            send_sem=corner_send.at[number],
            recv_sem=corner_recv.at[number],
            device_id=(gz + dz, xy + dy),
            device_id_type=MESH,
        )
        corners.append((present, copy, arrival, number, z_out, y_out))
    for present, copy, arrival, number, z_out, y_out in corners:
        pl.when(present)(lambda copy=copy: copy.start())

    for side in (0, 1):
        on_side(side, lambda copy: copy.start())
    for far_peers in farther():
        far_peers(lambda dr, column: block_copy(dr, column).start())

    lane = lax.broadcasted_iota(jnp.int32, (breadth + 16, length), 1)
    line = lax.broadcasted_iota(jnp.int32, (breadth + 16, length), 0)
    low_y = jnp.where(xy > 0, 0, 8)
    high_y = jnp.where(xy < columns - 1, breadth + 16, breadth + 8)
    in_grid = jnp.logical_and(line >= low_y, line < high_y)
    first_z = jnp.where(gz > 0, 0, 2)
    last_z = jnp.where(gz < rows - 1, depth + 3, depth + 1)

    def first_sweep(z):
        visc = pad[3, z]
        size = visc.shape[0]
        cx_high, cx_low = x_coeffs(visc, lane)
        coeffs = (
            0.5 * (visc + pad[3, z + 1]),
            0.5 * (visc + pad[3, z - 1]),
            0.5 * (visc + pltpu.roll(visc, size - 1, 0)),
            0.5 * (visc + pltpu.roll(visc, 1, 0)),
            cx_high,
            cx_low,
        )
        z_inside = jnp.logical_and(z >= first_z, z <= last_z)
        keep = jnp.logical_and(in_grid, z_inside)
        for part in range(3):
            centre = pad[part, z]
            new = laplace(
                centre, visc, pad[part, z - 1], pad[part, z + 1],
                pltpu.roll(centre, 1, 0), pltpu.roll(centre, size - 1, 0), coeffs, lane,
            )
            once[part, z - 1] = jnp.where(keep, new, 0.0)

    own_lane = lane[:breadth]

    def second_sweep(z):
        visc = pad[3, z, 8 : 8 + breadth, :]
        cx_high, cx_low = x_coeffs(visc, own_lane)
        coeffs = (
            0.5 * (visc + pad[3, z + 1, 8 : 8 + breadth, :]),
            0.5 * (visc + pad[3, z - 1, 8 : 8 + breadth, :]),
            0.5 * (visc + pad[3, z, 9 : 9 + breadth, :]),
            0.5 * (visc + pad[3, z, 7 : 7 + breadth, :]),
            cx_high,
            cx_low,
        )
        for part in range(3):
            field_ref[part, z - 2 + ZP, YP : YP + breadth, :] = laplace(
                once[part, z - 1, 8 : 8 + breadth, :], visc,
                once[part, z - 2, 8 : 8 + breadth, :], once[part, z, 8 : 8 + breadth, :],
                once[part, z - 1, 7 : 7 + breadth, :], once[part, z - 1, 9 : 9 + breadth, :],
                coeffs, own_lane,
            )

    def loop(low, high, body):
        def step(z, unused):
            body(z)
            return unused

        lax.fori_loop(low, high, step, 0)

    arrives = ((1, 0), (0, 1), (3, 2), (2, 3))

    def wait_side(side, neighbour):
        @pl.when(has[neighbour])
        def _():
            for copy in halo_copies(side):
                copy.wait_recv()
            if side >= 2:
                start = 6 if side == 3 else 8 + breadth
                for part in range(4):
                    for layer in range(2):
                        pad[part, 2 : 2 + depth, start + layer, :] = layers_in[
                            3 - side, part, layer * depth : (layer + 1) * depth, :
                        ]

    forwards = []
    for number, (there, column, side) in enumerate(((has[3], xy + 1, 1), (has[2], xy - 1, 2))):
        for dr in (-1, 0, 1):
            copy = pltpu.make_async_remote_copy(
                src_ref=slots_ref.at[0, dr + 1, :, 0:USED],
                dst_ref=slots_ref.at[side, dr + 1, :, 0:USED],
                send_sem=c_send.at[number, dr + 1],
                recv_sem=c_recv.at[number, dr + 1],
                device_id=(gz, column),
                device_id_type=MESH,
            )
            forwards.append((there, copy, dr, has[2 + number]))

    def forward(row):
        for there, copy, dr, unused in forwards:
            if dr == row:
                pl.when(there)(lambda copy=copy: copy.start())

    wait_side(2, 3)
    wait_side(3, 2)
    loop(3, 1 + depth, first_sweep)
    whole_row(0).wait_recv()
    forward(0)
    middle = 4 + (depth - 4) // 2
    loop(4, middle, second_sweep)
    for dr in (-1, 1):
        pl.when(has[0 if dr < 0 else 1])(lambda dr=dr: whole_row(dr).wait_recv())
        forward(dr)
    loop(middle, depth, second_sweep)

    wait_side(0, 1)
    wait_side(1, 0)
    for present, copy, arrival, number, z_out, y_out in corners:

        @pl.when(present)
        def _(arrival=arrival, number=number, z_out=z_out, y_out=y_out):
            arrival.wait_recv()
            for part in range(4):
                pad[part, z_out, y_out : y_out + 1, :] = corner_in[number, part : part + 1, :]

        @pl.when(jnp.logical_not(present))
        def _(z_out=z_out, y_out=y_out):
            for part in range(4):
                pad[part, z_out, y_out : y_out + 1, :] = jnp.zeros((1, length), jnp.float32)

    for z in (1, 2, 1 + depth, 2 + depth):
        first_sweep(z)
    for z in (2, 3, depth, 1 + depth):
        second_sweep(z)

    for unused, copy, dr, comes in forwards:
        pl.when(comes)(lambda copy=copy: copy.wait_recv())
    make_list(depth, breadth, slots_ref, list_ref)
    each_row(gz, rows, lambda dr: whole_row(dr).wait_send())
    for side in range(4):
        on_side(side, lambda copy: copy.wait_send())
    for present, copy, arrival, number, z_out, y_out in corners:
        pl.when(present)(lambda copy=copy: copy.wait_send())
    for there, copy, unused, comes in forwards:
        pl.when(there)(lambda copy=copy: copy.wait_send())


def phi(radius):
    x2 = radius * radius * 0.6168502750680849
    c = 1.0 / 479001600.0
    for factor in (-1.0 / 3628800.0, 1.0 / 40320.0, -1.0 / 720.0, 1.0 / 24.0, -0.5, 1.0):
        c = c * x2 + factor
    return jnp.where(jnp.abs(radius) < 2.0, 0.5 * c * c, 0.0)


def split(value):
    high = value.astype(jnp.bfloat16)
    return high, (value - high.astype(jnp.float32)).astype(jnp.bfloat16)


def product(left, right, contract):
    (left_high, left_low), (right_high, right_low) = left, right
    return lax.dot_general(
        jnp.concatenate([left_high, left_low, left_high], axis=1),
        jnp.concatenate([right_high, right_high, right_low], axis=contract),
        (((1,), (contract,)), ((), ())),
        preferred_element_type=jnp.float32,
    )


def points_kernel(
    depth, breadth, list_ref, slots_ref, field_in, new_ref, partial_ref, field, wx_high, wx_low, store_sem
):
    length = field.shape[3]
    partial_ref[...] = jnp.zeros_like(partial_ref)
    found = list_ref[4, 0]
    rounds = (found + TOGETHER - 1) // TOGETHER

    line = lax.broadcasted_iota(jnp.int32, (BOX, length), 0)
    rel = line.astype(jnp.float32)
    far = lax.broadcasted_iota(jnp.int32, (length, length), 0).astype(jnp.float32)

    def members(number):
        for other in range(TOGETHER):
            at = number * TOGETHER + other
            spot = jnp.minimum(at, found - 1)
            z, y, pair, rank = (list_ref[row, spot] for row in range(4))
            yield at, at < found, pair, rank, z, y

    def near_weights(frac, z, y):
        wz = phi(2.0 + (BOX - 5) * frac[0:1] - rel)
        wy = phi(2.0 + (BOX - 5) * frac[1:2] - rel)
        wz = jnp.where((z + line >= 0) & (z + line < depth), wz, 0.0)
        wy = jnp.where((y + line >= 0) & (y + line < breadth), wy, 0.0)
        return wz, wy

    def far_weights(frac):
        at = 2.0 + (length - 5) * frac
        near = at - rel
        base = phi(near - 4.0 * jnp.floor(0.25 * near + 0.5))
        high = base.astype(jnp.bfloat16).astype(jnp.float32)
        low = base - high
        inside = jnp.abs(at - far) < 2.0

        def spread_out(part):
            whole = jnp.broadcast_to(part[None], (length // BOX, BOX, length)).reshape(length, length)
            return jnp.where(inside, whole, 0.0).astype(jnp.bfloat16)

        return spread_out(high), spread_out(low)

    def box_of(z, y):
        return (slice(None), pl.ds(z + ZP, BOX), pl.ds(y + YP, BOX), slice(None))

    def spread(number, unused):
        adds = []
        for at, counts, pair, rank, z, y in members(number):
            tile = slots_ref[pair, pl.ds(6 * rank, 6), :]
            wz, wy = near_weights(tile, z, y)
            wy = jnp.where(counts, wy, 0.0)
            wx = far_weights(tile[2:3])
            wx_high[at], wx_low[at] = wx
            pulled = tile[3:6][:, None, :] * wz[None]
            coeff = pulled[:, :, None, :] * wy[None, None]
            boxes = product(split(coeff.reshape(3 * BOX * BOX, length)), wx, 1)
            adds.append((box_of(z, y), boxes.reshape(3, BOX, BOX, length)))
        for box, boxes in adds:
            field[box] = field[box] + boxes
        return unused

    lax.fori_loop(0, rounds, spread, 0)
    store = pltpu.make_async_copy(
        field.at[:, ZP : ZP + depth, YP : YP + breadth], new_ref, store_sem
    )
    store.start()

    def sample(number, unused):
        results = []
        for at, counts, pair, rank, z, y in members(number):
            wz, wy = near_weights(slots_ref[pair, pl.ds(6 * rank, 6), :], z, y)
            cells = field[box_of(z, y)].reshape(3 * BOX * BOX, length)
            taken = product(split(cells), (wx_high[at], wx_low[at]), 0)
            taken = taken.reshape(3, BOX, BOX, length)
            summed = jnp.sum(taken * wz[None, :, None, :], axis=1)
            results.append((pair, rank, jnp.sum(summed * wy[None], axis=1)))
        for pair, rank, values in results:
            partial_ref[pair, pl.ds(3 * rank, 3), :] = values
        return unused

    lax.fori_loop(0, rounds, sample, 0)
    store.wait()


def return_kernel(
    rows, columns, target_hbm, partial_ref, out_ref,
    side_in, summed, gathered, c_send, c_recv, ab_send, ab_recv, known, target_ref, target_sem,
):
    gz, xy = lax.axis_index("gz"), lax.axis_index("xy")
    near, farther = staged_greeting(gz, xy, rows, columns, known)
    target_load = pltpu.make_async_copy(target_hbm, target_ref, target_sem)
    target_load.start()
    has_low, has_high = xy > 0, xy < columns - 1
    sides = ((has_low, xy - 1), (has_high, xy + 1))

    def side_copy(number, column, landing):
        return pltpu.make_async_remote_copy(
            src_ref=partial_ref.at[number + 1, :, :, 0:KEPT],
            dst_ref=side_in.at[landing, :, :, 0:KEPT],
            send_sem=c_send.at[number],
            recv_sem=c_recv.at[landing],
            device_id=(gz, column),
            device_id_type=MESH,
        )

    near_peers = near()
    for number, (there, column) in enumerate(sides):
        pl.when(there)(
            lambda number=number, column=column: side_copy(number, column, 1 - number).start()
        )

        @pl.when(jnp.logical_not(there))
        def _(number=number):
            side_in[number] = jnp.zeros(side_in.shape[1:], jnp.float32)

    def block_copy(dr, column):
        return pltpu.make_async_remote_copy(
            src_ref=summed.at[dr + 1, column, 0:KEPT],
            dst_ref=gathered.at[1 - dr, xy, 0:KEPT],
            send_sem=ab_send.at[dr + 1],
            recv_sem=ab_recv.at[1 - dr],
            device_id=(gz + dr, column),
            device_id_type=MESH,
        )

    def whole_row(dr):
        span = pl.ds(0, columns - (1 if dr == 0 else 0))
        return pltpu.make_async_remote_copy(
            src_ref=summed.at[dr + 1, span, 0:KEPT],
            dst_ref=gathered.at[dr + 1, span, 0:KEPT],
            send_sem=ab_send.at[dr + 1],
            recv_sem=ab_recv.at[dr + 1],
            device_id=(gz, xy),
            device_id_type=MESH,
        )

    @pl.when(gz == 0)
    def _():
        gathered[0] = jnp.zeros(gathered.shape[1:], jnp.float32)

    @pl.when(gz == rows - 1)
    def _():
        gathered[2] = jnp.zeros(gathered.shape[1:], jnp.float32)

    far_peers = list(farther())
    for number, (there, column) in enumerate(sides):
        pl.when(there)(
            lambda number=number, column=column: side_copy(number, column, number).wait_recv()
        )
    summed[:, :, 0:KEPT] = (
        partial_ref[0, :, :, 0:KEPT] + side_in[0, :, :, 0:KEPT] + side_in[1, :, :, 0:KEPT]
    )
    for group in far_peers[::-1] + [near_peers]:
        group(lambda dr, column: block_copy(dr, column).start())
    gathered[1, xy, 0:KEPT] = summed[1, xy, 0:KEPT]

    target_load.wait()
    count = out_ref.shape[1]
    ranks = []
    for j in range(count):
        rank = jnp.int32(0)
        for earlier in range(j):
            rank = rank + (target_ref[earlier] == target_ref[j]).astype(jnp.int32)
        ranks.append(rank)
    each_row(gz, rows, lambda dr: whole_row(dr).wait_recv())
    for j, rank in enumerate(ranks):
        column = target_ref[j]
        tile = gathered[0, column] + gathered[1, column] + gathered[2, column]
        out_ref[:, j, :] = jnp.where(rank == 0, tile[0:3], tile[3:KEPT])
    each_row(gz, rows, lambda dr: whole_row(dr).wait_send())
    for number, (there, column) in enumerate(sides):
        pl.when(there)(
            lambda number=number, column=column: side_copy(number, column, number).wait_send()
        )


def shards(rows, columns, velocity, viscosity, frac, force, target, z_offset, y_offset):
    parts, depth, breadth, length = velocity.shape
    target = target.reshape(target.shape[0])
    frac, force = jnp.transpose(frac, (1, 0, 2)), jnp.transpose(force, (1, 0, 2))
    held = lambda array: pltpu.with_memory_space_constraint(array, pltpu.HBM)
    velocity, viscosity, frac, force = held(velocity), held(viscosity), held(frac), held(force)
    target, z_offset, y_offset = held(target), held(z_offset), held(y_offset)
    f32 = jnp.float32
    vmem = pl.BlockSpec(memory_space=pltpu.VMEM)
    smem = pl.BlockSpec(memory_space=pltpu.SMEM)
    hbm = pl.BlockSpec(memory_space=pltpu.HBM)
    anyw = pl.BlockSpec(memory_space=pl.ANY)
    dma = pltpu.SemaphoreType.DMA
    pairs = 9 * columns
    listed = pl.cdiv(CAP * pairs, length) * length
    field_shape = (3, depth + 2 * ZP, breadth + 2 * YP, length)
    field, slots, listing = pl.pallas_call(
        functools.partial(exchange_kernel, rows, columns),
        out_shape=(
            jax.ShapeDtypeStruct(field_shape, f32),
            jax.ShapeDtypeStruct((3, 3, columns, PAIR, length), f32),
            jax.ShapeDtypeStruct((8, listed), jnp.int32),
        ),
        in_specs=[hbm] * 7,
        out_specs=(vmem, vmem, vmem),
        scratch_shapes=[
            pltpu.VMEM((4, depth + 4, breadth + 16, length), f32),
            pltpu.VMEM((3, depth + 2, breadth + 16, length), f32),
            pltpu.VMEM((columns, PAIR, length), f32),
            pltpu.VMEM((2, 4, 2 * depth, length), f32),
            pltpu.VMEM((2, 4, 2 * depth, length), f32),
            pltpu.VMEM((4, 8, length), f32),
            pltpu.VMEM((4, 8, length), f32),
            dma((2,)), dma((3,)), dma((3,)), dma((4, 2)), dma((4, 2)),
            dma((4,)), dma((4,)), dma((2, 3)), dma((2, 3)),
            known_shape(columns),
            pltpu.SMEM(target.shape, jnp.int32),
            pltpu.SMEM(target.shape, jnp.int32),
            pltpu.SMEM(target.shape, jnp.int32),
            pltpu.VMEM(frac.shape, f32),
            pltpu.VMEM(force.shape, f32),
            dma((5,)),
        ],
        compiler_params=pltpu.CompilerParams(
            collective_id=0, has_side_effects=True, vmem_limit_bytes=VMEM_LIMIT
        ),
    )(target, z_offset, y_offset, velocity, viscosity, frac, force)

    new_velocity, partial, unused = pl.pallas_call(
        functools.partial(points_kernel, depth, breadth),
        out_shape=(
            jax.ShapeDtypeStruct(velocity.shape, f32),
            jax.ShapeDtypeStruct((pairs, 8, length), f32),
            jax.ShapeDtypeStruct(field_shape, f32),
        ),
        in_specs=[smem, vmem, vmem],
        out_specs=(anyw, vmem, vmem),
        scratch_shapes=[
            pltpu.VMEM((CAP * pairs + TOGETHER, length, length), jnp.bfloat16),
            pltpu.VMEM((CAP * pairs + TOGETHER, length, length), jnp.bfloat16),
            dma(()),
        ],
        input_output_aliases={2: 2},
        compiler_params=pltpu.CompilerParams(vmem_limit_bytes=VMEM_LIMIT),
    )(listing, slots.reshape(pairs, PAIR, length), field)

    point_velocity = pl.pallas_call(
        functools.partial(return_kernel, rows, columns),
        out_shape=jax.ShapeDtypeStruct(frac.shape, f32),
        in_specs=[hbm, vmem],
        out_specs=vmem,
        scratch_shapes=[
            pltpu.VMEM((2, 3, columns, 8, length), f32),
            pltpu.VMEM((3, columns, 8, length), f32),
            pltpu.VMEM((3, columns, 8, length), f32),
            dma((2,)), dma((2,)), dma((3,)), dma((3,)), known_shape(columns),
            pltpu.SMEM(target.shape, jnp.int32), dma(()),
        ],
        compiler_params=pltpu.CompilerParams(
            collective_id=1, has_side_effects=True, vmem_limit_bytes=VMEM_LIMIT
        ),
    )(target, partial.reshape(3, 3, columns, 8, length))
    return new_velocity, jnp.transpose(point_velocity, (1, 0, 2))


def solution(mesh):
    placed = (
        P(None, "gz", "xy", None),
        P("gz", "xy", None),
        P(("gz", "xy"), None, None),
        P(("gz", "xy"), None, None),
        P(("gz", "xy"), None),
        P(("gz", "xy")),
        P(("gz", "xy")),
    )
    return jax.shard_map(
        functools.partial(shards, mesh.shape["gz"], mesh.shape["xy"]),
        mesh=mesh,
        in_specs=placed,
        out_specs=(P(None, "gz", "xy", None), P(("gz", "xy"), None, None)),
        check_vma=False,
    )
```

```python
import functools

import jax
import jax.numpy as jnp
from jax import lax
from jax.experimental import pallas as pl
from jax.experimental.pallas import tpu as pltpu
from jax.sharding import PartitionSpec as P

BOX = 8
CAP = 2
FAR = 4096.0
ZP = 7
YP = 8
PAIR = 16
USED = 13
KEPT = 6
TOGETHER = 8
FEW = 4
CORES = 2
MESH = pl.DeviceIdType.MESH
VMEM_LIMIT = 24 * 1024 * 1024


def each_row(gz, rows, body):
    for dr in (-1, 0, 1):
        inside = jnp.logical_and(gz + dr >= 0, gz + dr < rows)
        pl.when(inside)(functools.partial(body, dr))


def chip_peers(gz, xy, rows, columns, steps):
    chip, core = xy // CORES, xy % CORES
    chips = columns // CORES

    def each(body):
        for step in steps:
            for dr in (0, -1, 1):
                there = (gz + dr >= 0) & (gz + dr < rows) & (chip + step >= 0) & (chip + step < chips)
                for turn in range(CORES):
                    if step == 0 and dr == 0 and turn == 0:
                        continue
                    other = core + turn
                    column = (chip + step) * CORES + jnp.where(other >= CORES, other - CORES, other)
                    pl.when(there)(functools.partial(body, dr, column))

    return each


def staged_greeting(gz, xy, rows, columns, known):
    chip, chips = xy // CORES, columns // CORES
    barrier = pltpu.get_barrier_semaphore()
    near_peers = chip_peers(gz, xy, rows, columns, (0, -1, 1))

    def signal_near(dr, column):
        pl.semaphore_signal(barrier, inc=1, device_id=(gz + dr, column), device_id_type=MESH)

    near_peers(signal_near)
    near_rows = 1 + (gz > 0).astype(jnp.int32) + (gz < rows - 1).astype(jnp.int32)
    near_chips = 1 + (chip > 0).astype(jnp.int32) + (chip < chips - 1).astype(jnp.int32)
    chain = ((chip < chips - 1, xy + CORES), (chip > 0, xy - CORES))

    def tell(reach):
        for number, (there, column) in enumerate(chain):
            pl.when(there)(
                lambda number=number, column=column: pl.semaphore_signal(
                    known.at[reach, number], inc=1, device_id=(gz, column), device_id_type=MESH
                )
            )

    def hear(reach):
        for number, (there, column) in enumerate(chain):
            pl.when(there)(lambda number=number: pl.semaphore_wait(known.at[reach, 1 - number], 1))

    def near():
        pl.semaphore_wait(barrier, near_rows * near_chips * CORES - 1)
        if chips > 2:
            tell(0)
        return near_peers

    def farther():
        for reach in range(chips - 2):
            hear(reach)
            if reach < chips - 3:
                tell(reach + 1)
            yield chip_peers(gz, xy, rows, columns, (-2 - reach, 2 + reach))

    return near, farther


def known_shape(columns):
    return pltpu.SemaphoreType.REGULAR((max(columns // CORES - 2, 1), 2))


def matches(target_ref, count, column):
    first, second = jnp.int32(-1), jnp.int32(-1)
    for j in range(count):
        hit = target_ref[j] == column
        second = jnp.where(jnp.logical_and(hit, jnp.logical_and(first >= 0, second < 0)), j, second)
        first = jnp.where(jnp.logical_and(hit, first < 0), j, first)
    return first, second


def laplace(centre, visc, z_low, z_high, y_low, y_high, coeffs, lane):
    length = centre.shape[-1]
    x_high = jnp.where(lane == length - 1, 0.0, pltpu.roll(centre, length - 1, 1))
    x_low = jnp.where(lane == 0, 0.0, pltpu.roll(centre, 1, 1))
    total = coeffs[0] * (z_high - centre) + coeffs[1] * (z_low - centre)
    total = total + coeffs[2] * (y_high - centre) + coeffs[3] * (y_low - centre)
    total = total + coeffs[4] * (x_high - centre) + coeffs[5] * (x_low - centre)
    return centre + 0.08 * total


def x_coeffs(visc, lane):
    length = visc.shape[-1]
    high = jnp.where(lane == length - 1, 0.0, pltpu.roll(visc, length - 1, 1))
    low = jnp.where(lane == 0, 0.0, pltpu.roll(visc, 1, 1))
    return 0.5 * (visc + high), 0.5 * (visc + low)


def make_list(depth, breadth, slots_ref, list_ref):
    columns, length = slots_ref.shape[2], slots_ref.shape[4]
    pairs, listed = 9 * columns, list_ref.shape[1]
    rows = slots_ref[:, :, :, USED - 1 : USED, :].reshape(pairs, length)
    facts = jnp.transpose(rows)[0:8]
    number = lax.broadcasted_iota(jnp.int32, (1, pairs), 1)
    above = (number >= 3 * columns).astype(jnp.int32)
    below = (number >= 6 * columns).astype(jnp.int32)
    place = number - 3 * columns * (above + below)
    level = (place >= columns).astype(jnp.int32) + (place >= 2 * columns).astype(jnp.int32)
    shift_z = ((level - 1) * depth).astype(jnp.float32)
    shift_y = ((2 * below - above) * breadth).astype(jnp.float32)
    earlier = lax.broadcasted_iota(jnp.int32, (pairs, pairs), 0) < lax.broadcasted_iota(
        jnp.int32, (pairs, pairs), 1
    )
    earlier = earlier.astype(jnp.float32).astype(jnp.bfloat16)
    found = []
    for rank in range(CAP):
        z = facts[2 * rank : 2 * rank + 1] + shift_z
        y = facts[2 * rank + 1 : 2 * rank + 2] + shift_y
        meets = (z > -BOX) & (z < depth) & (y > -BOX) & (y < breadth)
        found.append((z, y, meets, jnp.where(meets, 1.0, 0.0)))
    both = found[0][3] + found[1][3]
    spot = jnp.dot(
        jnp.broadcast_to(both, (BOX, pairs)).astype(jnp.bfloat16), earlier,
        preferred_element_type=jnp.float32,
    )[0:1]
    entry = lax.broadcasted_iota(jnp.int32, (listed, pairs), 0).astype(jnp.float32)
    fact = lax.broadcasted_iota(jnp.int32, (BOX, pairs), 0)
    listing = jnp.zeros((BOX, listed), jnp.float32)
    for rank, (z, y, meets, one) in enumerate(found):
        mine = jnp.where(meets, spot + (found[0][3] if rank else 0.0), -1.0)
        chosen = jnp.where(entry == mine, 1.0, 0.0).astype(jnp.bfloat16)
        told = jnp.where(fact == 0, z, jnp.where(fact == 1, y, number.astype(jnp.float32)))
        told = jnp.where(meets, jnp.where(fact == 3, float(rank), told), 0.0).astype(jnp.bfloat16)
        listing = listing + lax.dot_general(
            told, chosen, (((1,), (1,)), ((), ())), preferred_element_type=jnp.float32
        )
    list_ref[0:4, :] = listing[0:4].astype(jnp.int32)
    total = jnp.sum(both, axis=1, keepdims=True)
    list_ref[4:8, :] = jnp.broadcast_to(total, (4, listed)).astype(jnp.int32)


def exchange_kernel(
    rows, columns, target_hbm, zoff_hbm, yoff_hbm, velocity_ref, viscosity_ref, frac_hbm, force_hbm,
    field_ref, slots_ref, list_ref,
    pad, once, staging, layers_out, layers_in, corner_out, corner_in,
    load_sem, ab_send, ab_recv, halo_send, halo_recv, corner_send, corner_recv, c_send, c_recv, known,
    target_ref, zoff_ref, yoff_ref, frac_ref, force_ref, small_sem,
):
    gz, xy = lax.axis_index("gz"), lax.axis_index("xy")
    depth, breadth = velocity_ref.shape[1], velocity_ref.shape[2]
    length = velocity_ref.shape[3]
    near, farther = staged_greeting(gz, xy, rows, columns, known)
    loads = (
        pltpu.make_async_copy(
            velocity_ref, pad.at[0:3, 2 : 2 + depth, 8 : 8 + breadth], load_sem.at[0]
        ),
        pltpu.make_async_copy(
            viscosity_ref, pad.at[3, 2 : 2 + depth, 8 : 8 + breadth], load_sem.at[1]
        ),
    )
    small = [
        pltpu.make_async_copy(source, place, small_sem.at[number])
        for number, (source, place) in enumerate((
            (target_hbm, target_ref), (zoff_hbm, zoff_ref), (yoff_hbm, yoff_ref),
            (frac_hbm, frac_ref), (force_hbm, force_ref),
        ))
    ]
    for load in small:
        load.start()
    for load in loads:
        load.start()

    lanes = lax.broadcasted_iota(jnp.int32, (1, length), 1)
    count = frac_ref.shape[1]

    def stage(column, unused):
        row = jnp.full((1, length), FAR, jnp.float32)
        for rank, block in enumerate(matches(target_ref, count, column)):
            at = jnp.maximum(block, 0)
            there = block >= 0
            z = jnp.where(there, zoff_ref[at].astype(jnp.float32), FAR)
            y = jnp.where(there, yoff_ref[at].astype(jnp.float32), FAR)
            staging[column, 6 * rank : 6 * rank + 3, :] = frac_ref[:, at, :]
            staging[column, 6 * rank + 3 : 6 * rank + 6, :] = force_ref[:, at, :]
            row = jnp.where(lanes == 2 * rank, z, row)
            row = jnp.where(lanes == 2 * rank + 1, y, row)
        staging[column, 12:13, :] = row
        return unused

    def block_copy(dr, column):
        return pltpu.make_async_remote_copy(
            src_ref=staging.at[column, 0:USED],
            dst_ref=slots_ref.at[0, 1 - dr, xy, 0:USED],
            send_sem=ab_send.at[dr + 1],
            recv_sem=ab_recv.at[1 - dr],
            device_id=(gz + dr, column),
            device_id_type=MESH,
        )

    def whole_row(dr):
        span = pl.ds(0, columns - (1 if dr == 0 else 0))
        return pltpu.make_async_remote_copy(
            src_ref=staging.at[span, 0:USED],
            dst_ref=slots_ref.at[0, dr + 1, span, 0:USED],
            send_sem=ab_send.at[dr + 1],
            recv_sem=ab_recv.at[dr + 1],
            device_id=(gz, xy),
            device_id_type=MESH,
        )

    for load in small:
        load.wait()
    lax.fori_loop(0, columns, stage, 0)
    near_peers = near()

    has = (gz > 0, gz < rows - 1, xy > 0, xy < columns - 1)
    device = ((gz - 1, xy), (gz + 1, xy), (gz, xy - 1), (gz, xy + 1))
    own_y = slice(8, 8 + breadth)
    own_z = slice(2, 2 + depth)

    def halo_copies(side):
        if side == 0:
            cut, land = slice(0, 2), (slice(2 + depth, 4 + depth), own_y)
        elif side == 1:
            cut, land = slice(depth - 2, depth), (slice(0, 2), own_y)
        if side < 2:
            sources = (velocity_ref.at[:, cut], viscosity_ref.at[cut])
            lands = (pad.at[(slice(0, 3),) + land], pad.at[(3,) + land])
        else:
            sources, lands = (layers_out.at[side - 2],), (layers_in.at[3 - side],)
        return [
            pltpu.make_async_remote_copy(
                src_ref=source,
                dst_ref=spot,
                send_sem=halo_send.at[side, number],
                recv_sem=halo_recv.at[side, number],
                device_id=device[side],
                device_id_type=MESH,
            )
            for number, (source, spot) in enumerate(zip(sources, lands))
        ]

    def on_side(side, action):
        @pl.when(has[side])
        def _():
            for copy in halo_copies(side):
                action(copy)


    near_peers(lambda dr, column: block_copy(dr, column).start())
    slots_ref[0, 1, xy, 0:USED] = staging[xy, 0:USED]


    wide, high = field_ref.shape[2], field_ref.shape[1]
    field_ref[:, 0:ZP] = jnp.zeros((3, ZP, wide, length), jnp.float32)
    field_ref[:, ZP + depth :] = jnp.zeros((3, high - ZP - depth, wide, length), jnp.float32)
    field_ref[:, ZP : ZP + depth, 0:YP] = jnp.zeros((3, depth, YP, length), jnp.float32)
    field_ref[:, ZP : ZP + depth, YP + breadth :] = jnp.zeros(
        (3, depth, wide - YP - breadth, length), jnp.float32
    )
    zeros_z = jnp.zeros((4, 2, breadth, length), jnp.float32)
    zeros_y = jnp.zeros((4, depth, 8, length), jnp.float32)

    @pl.when(gz == 0)
    def _():
        pad[:, 0:2, 8 : 8 + breadth, :] = zeros_z
        slots_ref[0, 0] = jnp.full(slots_ref.shape[2:], FAR, jnp.float32)

    @pl.when(gz == rows - 1)
    def _():
        pad[:, 2 + depth : 4 + depth, 8 : 8 + breadth, :] = zeros_z
        slots_ref[0, 2] = jnp.full(slots_ref.shape[2:], FAR, jnp.float32)

    @pl.when(xy == 0)
    def _():
        pad[:, 2 : 2 + depth, 0:8, :] = zeros_y
        slots_ref[1] = jnp.full(slots_ref.shape[1:], FAR, jnp.float32)

    @pl.when(xy == columns - 1)
    def _():
        pad[:, 2 : 2 + depth, 8 + breadth : 16 + breadth, :] = zeros_y
        slots_ref[2] = jnp.full(slots_ref.shape[1:], FAR, jnp.float32)

    for load in loads:
        load.wait()
    for side, start in ((2, 8), (3, 6 + breadth)):
        for part in range(4):
            for layer in range(2):
                layers_out[side - 2, part, layer * depth : (layer + 1) * depth, :] = pad[
                    part, 2 : 2 + depth, start + layer, :
                ]
        on_side(side, lambda copy: copy.start())

    corners = []
    for number, (dz, dy) in enumerate(((-1, -1), (-1, 1), (1, -1), (1, 1))):
        z_in = 2 if dz < 0 else 1 + depth
        y_in = 8 if dy < 0 else 7 + breadth
        z_out = 1 if dz < 0 else 2 + depth
        y_out = 7 if dy < 0 else 8 + breadth
        present = jnp.logical_and(has[0 if dz < 0 else 1], has[2 if dy < 0 else 3])
        for part in range(4):
            corner_out[number, part : part + 1, :] = pad[part, z_in, y_in : y_in + 1, :]
        copy = pltpu.make_async_remote_copy(
            src_ref=corner_out.at[number],
            dst_ref=corner_in.at[3 - number],
            send_sem=corner_send.at[number],
            recv_sem=corner_recv.at[3 - number],
            device_id=(gz + dz, xy + dy),
            device_id_type=MESH,
        )
        arrival = pltpu.make_async_remote_copy(
            src_ref=corner_out.at[number],
            dst_ref=corner_in.at[number],
            send_sem=corner_send.at[number],
            recv_sem=corner_recv.at[number],
            device_id=(gz + dz, xy + dy),
            device_id_type=MESH,
        )
        corners.append((present, copy, arrival, number, z_out, y_out))
    for present, copy, arrival, number, z_out, y_out in corners:
        pl.when(present)(lambda copy=copy: copy.start())

    for side in (0, 1):
        on_side(side, lambda copy: copy.start())
    for far_peers in farther():
        far_peers(lambda dr, column: block_copy(dr, column).start())

    lane = lax.broadcasted_iota(jnp.int32, (breadth + 16, length), 1)
    line = lax.broadcasted_iota(jnp.int32, (breadth + 16, length), 0)
    low_y = jnp.where(xy > 0, 0, 8)
    high_y = jnp.where(xy < columns - 1, breadth + 16, breadth + 8)
    in_grid = jnp.logical_and(line >= low_y, line < high_y)
    first_z = jnp.where(gz > 0, 0, 2)
    last_z = jnp.where(gz < rows - 1, depth + 3, depth + 1)

    def first_sweep(z):
        visc = pad[3, z]
        size = visc.shape[0]
        cx_high, cx_low = x_coeffs(visc, lane)
        coeffs = (
            0.5 * (visc + pad[3, z + 1]),
            0.5 * (visc + pad[3, z - 1]),
            0.5 * (visc + pltpu.roll(visc, size - 1, 0)),
            0.5 * (visc + pltpu.roll(visc, 1, 0)),
            cx_high,
            cx_low,
        )
        z_inside = jnp.logical_and(z >= first_z, z <= last_z)
        keep = jnp.logical_and(in_grid, z_inside)
        for part in range(3):
            centre = pad[part, z]
            new = laplace(
                centre, visc, pad[part, z - 1], pad[part, z + 1],
                pltpu.roll(centre, 1, 0), pltpu.roll(centre, size - 1, 0), coeffs, lane,
            )
            once[part, z - 1] = jnp.where(keep, new, 0.0)

    own_lane = lane[:breadth]

    def second_sweep(z):
        visc = pad[3, z, 8 : 8 + breadth, :]
        cx_high, cx_low = x_coeffs(visc, own_lane)
        coeffs = (
            0.5 * (visc + pad[3, z + 1, 8 : 8 + breadth, :]),
            0.5 * (visc + pad[3, z - 1, 8 : 8 + breadth, :]),
            0.5 * (visc + pad[3, z, 9 : 9 + breadth, :]),
            0.5 * (visc + pad[3, z, 7 : 7 + breadth, :]),
            cx_high,
            cx_low,
        )
        for part in range(3):
            field_ref[part, z - 2 + ZP, YP : YP + breadth, :] = laplace(
                once[part, z - 1, 8 : 8 + breadth, :], visc,
                once[part, z - 2, 8 : 8 + breadth, :], once[part, z, 8 : 8 + breadth, :],
                once[part, z - 1, 7 : 7 + breadth, :], once[part, z - 1, 9 : 9 + breadth, :],
                coeffs, own_lane,
            )

    def loop(low, high, body):
        def step(z, unused):
            body(z)
            return unused

        lax.fori_loop(low, high, step, 0)

    arrives = ((1, 0), (0, 1), (3, 2), (2, 3))

    def wait_side(side, neighbour):
        @pl.when(has[neighbour])
        def _():
            for copy in halo_copies(side):
                copy.wait_recv()
            if side >= 2:
                start = 6 if side == 3 else 8 + breadth
                for part in range(4):
                    for layer in range(2):
                        pad[part, 2 : 2 + depth, start + layer, :] = layers_in[
                            3 - side, part, layer * depth : (layer + 1) * depth, :
                        ]

    forwards = []
    for number, (there, column, side) in enumerate(((has[3], xy + 1, 1), (has[2], xy - 1, 2))):
        for dr in (-1, 0, 1):
            copy = pltpu.make_async_remote_copy(
                src_ref=slots_ref.at[0, dr + 1, :, 0:USED],
                dst_ref=slots_ref.at[side, dr + 1, :, 0:USED],
                send_sem=c_send.at[number, dr + 1],
                recv_sem=c_recv.at[number, dr + 1],
                device_id=(gz, column),
                device_id_type=MESH,
            )
            forwards.append((there, copy, dr, has[2 + number]))

    def forward(row):
        for there, copy, dr, unused in forwards:
            if dr == row:
                pl.when(there)(lambda copy=copy: copy.start())

    wait_side(2, 3)
    wait_side(3, 2)
    loop(3, 1 + depth, first_sweep)
    whole_row(0).wait_recv()
    forward(0)
    middle = 4 + (depth - 4) // 2
    loop(4, middle, second_sweep)
    for dr in (-1, 1):
        pl.when(has[0 if dr < 0 else 1])(lambda dr=dr: whole_row(dr).wait_recv())
        forward(dr)
    loop(middle, depth, second_sweep)

    wait_side(0, 1)
    wait_side(1, 0)
    for present, copy, arrival, number, z_out, y_out in corners:

        @pl.when(present)
        def _(arrival=arrival, number=number, z_out=z_out, y_out=y_out):
            arrival.wait_recv()
            for part in range(4):
                pad[part, z_out, y_out : y_out + 1, :] = corner_in[number, part : part + 1, :]

        @pl.when(jnp.logical_not(present))
        def _(z_out=z_out, y_out=y_out):
            for part in range(4):
                pad[part, z_out, y_out : y_out + 1, :] = jnp.zeros((1, length), jnp.float32)

    for z in (1, 2, 1 + depth, 2 + depth):
        first_sweep(z)
    for z in (2, 3, depth, 1 + depth):
        second_sweep(z)

    for unused, copy, dr, comes in forwards:
        pl.when(comes)(lambda copy=copy: copy.wait_recv())
    make_list(depth, breadth, slots_ref, list_ref)
    each_row(gz, rows, lambda dr: whole_row(dr).wait_send())
    for side in range(4):
        on_side(side, lambda copy: copy.wait_send())
    for present, copy, arrival, number, z_out, y_out in corners:
        pl.when(present)(lambda copy=copy: copy.wait_send())
    for there, copy, unused, comes in forwards:
        pl.when(there)(lambda copy=copy: copy.wait_send())


def phi(radius):
    x2 = radius * radius * 0.6168502750680849
    c = 1.0 / 479001600.0
    for factor in (-1.0 / 3628800.0, 1.0 / 40320.0, -1.0 / 720.0, 1.0 / 24.0, -0.5, 1.0):
        c = c * x2 + factor
    return jnp.where(jnp.abs(radius) < 2.0, 0.5 * c * c, 0.0)


def split(value):
    high = value.astype(jnp.bfloat16)
    return high, (value - high.astype(jnp.float32)).astype(jnp.bfloat16)


def product(left, right, contract):
    (left_high, left_low), (right_high, right_low) = left, right
    return lax.dot_general(
        jnp.concatenate([left_high, left_low, left_high], axis=1),
        jnp.concatenate([right_high, right_high, right_low], axis=contract),
        (((1,), (contract,)), ((), ())),
        preferred_element_type=jnp.float32,
    )


def points_kernel(
    depth, breadth, list_ref, slots_ref, field_in, new_ref, partial_ref, field, wx_high, wx_low, store_sem
):
    length = field.shape[3]
    partial_ref[...] = jnp.zeros_like(partial_ref)
    found = list_ref[4, 0]
    whole = found // TOGETHER
    rest = found - whole * TOGETHER

    line = lax.broadcasted_iota(jnp.int32, (BOX, length), 0)
    rel = line.astype(jnp.float32)
    far = lax.broadcasted_iota(jnp.int32, (length, length), 0).astype(jnp.float32)

    def in_rounds(work):
        def some(number, unused):
            work(TOGETHER, number * TOGETHER)
            return unused

        def last(number, unused):
            work(FEW, whole * TOGETHER + number * FEW)
            return unused

        lax.fori_loop(0, whole, some, 0)
        lax.fori_loop(0, (rest + FEW - 1) // FEW, last, 0)

    def members(first, size):
        for other in range(size):
            at = first + other
            spot = jnp.minimum(at, found - 1)
            z, y, pair, rank = (list_ref[row, spot] for row in range(4))
            yield at, at < found, pair, rank, z, y

    def near_weights(frac, z, y):
        wz = phi(2.0 + (BOX - 5) * frac[0:1] - rel)
        wy = phi(2.0 + (BOX - 5) * frac[1:2] - rel)
        wz = jnp.where((z + line >= 0) & (z + line < depth), wz, 0.0)
        wy = jnp.where((y + line >= 0) & (y + line < breadth), wy, 0.0)
        return wz, wy

    def far_weights(frac):
        at = 2.0 + (length - 5) * frac
        near = at - rel
        base = phi(near - 4.0 * jnp.floor(0.25 * near + 0.5))
        high = base.astype(jnp.bfloat16).astype(jnp.float32)
        low = base - high
        inside = jnp.abs(at - far) < 2.0

        def spread_out(part):
            whole = jnp.broadcast_to(part[None], (length // BOX, BOX, length)).reshape(length, length)
            return jnp.where(inside, whole, 0.0).astype(jnp.bfloat16)

        return spread_out(high), spread_out(low)

    def box_of(z, y):
        return (slice(None), pl.ds(z + ZP, BOX), pl.ds(y + YP, BOX), slice(None))

    def spread(size, first):
        adds = []
        for at, counts, pair, rank, z, y in members(first, size):
            tile = slots_ref[pair, pl.ds(6 * rank, 6), :]
            wz, wy = near_weights(tile, z, y)
            wy = jnp.where(counts, wy, 0.0)
            wx = far_weights(tile[2:3])
            wx_high[at], wx_low[at] = wx
            pulled = tile[3:6][:, None, :] * wz[None]
            coeff = pulled[:, :, None, :] * wy[None, None]
            boxes = product(split(coeff.reshape(3 * BOX * BOX, length)), wx, 1)
            adds.append((box_of(z, y), boxes.reshape(3, BOX, BOX, length)))
        for box, boxes in adds:
            field[box] = field[box] + boxes

    in_rounds(spread)
    store = pltpu.make_async_copy(
        field.at[:, ZP : ZP + depth, YP : YP + breadth], new_ref, store_sem
    )
    store.start()

    def sample(size, first):
        results = []
        for at, counts, pair, rank, z, y in members(first, size):
            wz, wy = near_weights(slots_ref[pair, pl.ds(6 * rank, 6), :], z, y)
            cells = field[box_of(z, y)].reshape(3 * BOX * BOX, length)
            taken = product(split(cells), (wx_high[at], wx_low[at]), 0)
            taken = taken.reshape(3, BOX, BOX, length)
            summed = jnp.sum(taken * wz[None, :, None, :], axis=1)
            results.append((pair, rank, jnp.sum(summed * wy[None], axis=1)))
        for pair, rank, values in results:
            partial_ref[pair, pl.ds(3 * rank, 3), :] = values

    in_rounds(sample)
    store.wait()


def return_kernel(
    rows, columns, target_hbm, partial_ref, out_ref,
    side_in, summed, gathered, c_send, c_recv, ab_send, ab_recv, known, target_ref, target_sem,
):
    gz, xy = lax.axis_index("gz"), lax.axis_index("xy")
    near, farther = staged_greeting(gz, xy, rows, columns, known)
    target_load = pltpu.make_async_copy(target_hbm, target_ref, target_sem)
    target_load.start()
    has_low, has_high = xy > 0, xy < columns - 1
    sides = ((has_low, xy - 1), (has_high, xy + 1))

    def side_copy(number, column, landing):
        return pltpu.make_async_remote_copy(
            src_ref=partial_ref.at[number + 1, :, :, 0:KEPT],
            dst_ref=side_in.at[landing, :, :, 0:KEPT],
            send_sem=c_send.at[number],
            recv_sem=c_recv.at[landing],
            device_id=(gz, column),
            device_id_type=MESH,
        )

    near_peers = near()
    for number, (there, column) in enumerate(sides):
        pl.when(there)(
            lambda number=number, column=column: side_copy(number, column, 1 - number).start()
        )

        @pl.when(jnp.logical_not(there))
        def _(number=number):
            side_in[number] = jnp.zeros(side_in.shape[1:], jnp.float32)

    def block_copy(dr, column):
        return pltpu.make_async_remote_copy(
            src_ref=summed.at[dr + 1, column, 0:KEPT],
            dst_ref=gathered.at[1 - dr, xy, 0:KEPT],
            send_sem=ab_send.at[dr + 1],
            recv_sem=ab_recv.at[1 - dr],
            device_id=(gz + dr, column),
            device_id_type=MESH,
        )

    def whole_row(dr):
        span = pl.ds(0, columns - (1 if dr == 0 else 0))
        return pltpu.make_async_remote_copy(
            src_ref=summed.at[dr + 1, span, 0:KEPT],
            dst_ref=gathered.at[dr + 1, span, 0:KEPT],
            send_sem=ab_send.at[dr + 1],
            recv_sem=ab_recv.at[dr + 1],
            device_id=(gz, xy),
            device_id_type=MESH,
        )

    @pl.when(gz == 0)
    def _():
        gathered[0] = jnp.zeros(gathered.shape[1:], jnp.float32)

    @pl.when(gz == rows - 1)
    def _():
        gathered[2] = jnp.zeros(gathered.shape[1:], jnp.float32)

    far_peers = list(farther())
    for number, (there, column) in enumerate(sides):
        pl.when(there)(
            lambda number=number, column=column: side_copy(number, column, number).wait_recv()
        )
    summed[:, :, 0:KEPT] = (
        partial_ref[0, :, :, 0:KEPT] + side_in[0, :, :, 0:KEPT] + side_in[1, :, :, 0:KEPT]
    )
    groups = far_peers[::-1] + [near_peers]
    for group in groups:
        group(lambda dr, column: block_copy(dr, column).start() if dr else None)
    for group in groups:
        group(lambda dr, column: None if dr else block_copy(dr, column).start())
    gathered[1, xy, 0:KEPT] = summed[1, xy, 0:KEPT]

    target_load.wait()
    count = out_ref.shape[1]
    ranks = []
    for j in range(count):
        rank = jnp.int32(0)
        for earlier in range(j):
            rank = rank + (target_ref[earlier] == target_ref[j]).astype(jnp.int32)
        ranks.append(rank)
    each_row(gz, rows, lambda dr: whole_row(dr).wait_recv())
    for j, rank in enumerate(ranks):
        column = target_ref[j]
        tile = gathered[0, column] + gathered[1, column] + gathered[2, column]
        out_ref[:, j, :] = jnp.where(rank == 0, tile[0:3], tile[3:KEPT])
    each_row(gz, rows, lambda dr: whole_row(dr).wait_send())
    for number, (there, column) in enumerate(sides):
        pl.when(there)(
            lambda number=number, column=column: side_copy(number, column, number).wait_send()
        )


def shards(rows, columns, velocity, viscosity, frac, force, target, z_offset, y_offset):
    parts, depth, breadth, length = velocity.shape
    target = target.reshape(target.shape[0])
    frac, force = jnp.transpose(frac, (1, 0, 2)), jnp.transpose(force, (1, 0, 2))
    held = lambda array: pltpu.with_memory_space_constraint(array, pltpu.HBM)
    velocity, viscosity, frac, force = held(velocity), held(viscosity), held(frac), held(force)
    target, z_offset, y_offset = held(target), held(z_offset), held(y_offset)
    f32 = jnp.float32
    vmem = pl.BlockSpec(memory_space=pltpu.VMEM)
    smem = pl.BlockSpec(memory_space=pltpu.SMEM)
    hbm = pl.BlockSpec(memory_space=pltpu.HBM)
    anyw = pl.BlockSpec(memory_space=pl.ANY)
    dma = pltpu.SemaphoreType.DMA
    pairs = 9 * columns
    listed = pl.cdiv(CAP * pairs, length) * length
    field_shape = (3, depth + 2 * ZP, breadth + 2 * YP, length)
    field, slots, listing = pl.pallas_call(
        functools.partial(exchange_kernel, rows, columns),
        out_shape=(
            jax.ShapeDtypeStruct(field_shape, f32),
            jax.ShapeDtypeStruct((3, 3, columns, PAIR, length), f32),
            jax.ShapeDtypeStruct((8, listed), jnp.int32),
        ),
        in_specs=[hbm] * 7,
        out_specs=(vmem, vmem, vmem),
        scratch_shapes=[
            pltpu.VMEM((4, depth + 4, breadth + 16, length), f32),
            pltpu.VMEM((3, depth + 2, breadth + 16, length), f32),
            pltpu.VMEM((columns, PAIR, length), f32),
            pltpu.VMEM((2, 4, 2 * depth, length), f32),
            pltpu.VMEM((2, 4, 2 * depth, length), f32),
            pltpu.VMEM((4, 8, length), f32),
            pltpu.VMEM((4, 8, length), f32),
            dma((2,)), dma((3,)), dma((3,)), dma((4, 2)), dma((4, 2)),
            dma((4,)), dma((4,)), dma((2, 3)), dma((2, 3)),
            known_shape(columns),
            pltpu.SMEM(target.shape, jnp.int32),
            pltpu.SMEM(target.shape, jnp.int32),
            pltpu.SMEM(target.shape, jnp.int32),
            pltpu.VMEM(frac.shape, f32),
            pltpu.VMEM(force.shape, f32),
            dma((5,)),
        ],
        compiler_params=pltpu.CompilerParams(
            collective_id=0, has_side_effects=True, vmem_limit_bytes=VMEM_LIMIT
        ),
    )(target, z_offset, y_offset, velocity, viscosity, frac, force)

    new_velocity, partial, unused = pl.pallas_call(
        functools.partial(points_kernel, depth, breadth),
        out_shape=(
            jax.ShapeDtypeStruct(velocity.shape, f32),
            jax.ShapeDtypeStruct((pairs, 8, length), f32),
            jax.ShapeDtypeStruct(field_shape, f32),
        ),
        in_specs=[smem, vmem, vmem],
        out_specs=(anyw, vmem, vmem),
        scratch_shapes=[
            pltpu.VMEM((CAP * pairs + TOGETHER, length, length), jnp.bfloat16),
            pltpu.VMEM((CAP * pairs + TOGETHER, length, length), jnp.bfloat16),
            dma(()),
        ],
        input_output_aliases={2: 2},
        compiler_params=pltpu.CompilerParams(vmem_limit_bytes=VMEM_LIMIT),
    )(listing, slots.reshape(pairs, PAIR, length), field)

    point_velocity = pl.pallas_call(
        functools.partial(return_kernel, rows, columns),
        out_shape=jax.ShapeDtypeStruct(frac.shape, f32),
        in_specs=[hbm, vmem],
        out_specs=vmem,
        scratch_shapes=[
            pltpu.VMEM((2, 3, columns, 8, length), f32),
            pltpu.VMEM((3, columns, 8, length), f32),
            pltpu.VMEM((3, columns, 8, length), f32),
            dma((2,)), dma((2,)), dma((3,)), dma((3,)), known_shape(columns),
            pltpu.SMEM(target.shape, jnp.int32), dma(()),
        ],
        compiler_params=pltpu.CompilerParams(
            collective_id=1, has_side_effects=True, vmem_limit_bytes=VMEM_LIMIT
        ),
    )(target, partial.reshape(3, 3, columns, 8, length))
    return new_velocity, jnp.transpose(point_velocity, (1, 0, 2))


def solution(mesh):
    placed = (
        P(None, "gz", "xy", None),
        P("gz", "xy", None),
        P(("gz", "xy"), None, None),
        P(("gz", "xy"), None, None),
        P(("gz", "xy"), None),
        P(("gz", "xy")),
        P(("gz", "xy")),
    )
    return jax.shard_map(
        functools.partial(shards, mesh.shape["gz"], mesh.shape["xy"]),
        mesh=mesh,
        in_specs=placed,
        out_specs=(P(None, "gz", "xy", None), P(("gz", "xy"), None, None)),
        check_vma=False,
    )
```

```python
import functools

import jax
import jax.numpy as jnp
from jax import lax
from jax.experimental import pallas as pl
from jax.experimental.pallas import tpu as pltpu
from jax.sharding import PartitionSpec as P

BOX = 8
CAP = 2
FAR = 4096.0
ZP = 7
YP = 8
PAIR = 16
USED = 13
KEPT = 6
TOGETHER = 8
FEW = 4
CORES = 2
MESH = pl.DeviceIdType.MESH
VMEM_LIMIT = 24 * 1024 * 1024


def each_row(gz, rows, body):
    for dr in (-1, 0, 1):
        inside = jnp.logical_and(gz + dr >= 0, gz + dr < rows)
        pl.when(inside)(functools.partial(body, dr))


def chip_peers(gz, xy, rows, columns, steps):
    chip, core = xy // CORES, xy % CORES
    chips = columns // CORES

    def each(body):
        for step in steps:
            for dr in (0, -1, 1):
                there = (gz + dr >= 0) & (gz + dr < rows) & (chip + step >= 0) & (chip + step < chips)
                for turn in range(CORES):
                    if step == 0 and dr == 0 and turn == 0:
                        continue
                    other = core + turn
                    column = (chip + step) * CORES + jnp.where(other >= CORES, other - CORES, other)
                    pl.when(there)(functools.partial(body, dr, column))

    return each


def staged_greeting(gz, xy, rows, columns, known):
    chip, chips = xy // CORES, columns // CORES
    barrier = pltpu.get_barrier_semaphore()
    near_peers = chip_peers(gz, xy, rows, columns, (0, -1, 1))

    def signal_near(dr, column):
        pl.semaphore_signal(barrier, inc=1, device_id=(gz + dr, column), device_id_type=MESH)

    near_peers(signal_near)
    near_rows = 1 + (gz > 0).astype(jnp.int32) + (gz < rows - 1).astype(jnp.int32)
    near_chips = 1 + (chip > 0).astype(jnp.int32) + (chip < chips - 1).astype(jnp.int32)
    chain = ((chip < chips - 1, xy + CORES), (chip > 0, xy - CORES))

    def tell(reach):
        for number, (there, column) in enumerate(chain):
            pl.when(there)(
                lambda number=number, column=column: pl.semaphore_signal(
                    known.at[reach, number], inc=1, device_id=(gz, column), device_id_type=MESH
                )
            )

    def hear(reach):
        for number, (there, column) in enumerate(chain):
            pl.when(there)(lambda number=number: pl.semaphore_wait(known.at[reach, 1 - number], 1))

    def near():
        pl.semaphore_wait(barrier, near_rows * near_chips * CORES - 1)
        if chips > 2:
            tell(0)
        return near_peers

    def farther():
        for reach in range(chips - 2):
            hear(reach)
            if reach < chips - 3:
                tell(reach + 1)
            yield chip_peers(gz, xy, rows, columns, (-2 - reach, 2 + reach))

    return near, farther


def known_shape(columns):
    return pltpu.SemaphoreType.REGULAR((max(columns // CORES - 2, 1), 2))


def matches(target_ref, count, column):
    first, second = jnp.int32(-1), jnp.int32(-1)
    for j in range(count):
        hit = target_ref[j] == column
        second = jnp.where(jnp.logical_and(hit, jnp.logical_and(first >= 0, second < 0)), j, second)
        first = jnp.where(jnp.logical_and(hit, first < 0), j, first)
    return first, second


def laplace(centre, visc, z_low, z_high, y_low, y_high, coeffs, lane):
    length = centre.shape[-1]
    x_high = jnp.where(lane == length - 1, 0.0, pltpu.roll(centre, length - 1, 1))
    x_low = jnp.where(lane == 0, 0.0, pltpu.roll(centre, 1, 1))
    total = coeffs[0] * (z_high - centre) + coeffs[1] * (z_low - centre)
    total = total + coeffs[2] * (y_high - centre) + coeffs[3] * (y_low - centre)
    total = total + coeffs[4] * (x_high - centre) + coeffs[5] * (x_low - centre)
    return centre + 0.08 * total


def x_coeffs(visc, lane):
    length = visc.shape[-1]
    high = jnp.where(lane == length - 1, 0.0, pltpu.roll(visc, length - 1, 1))
    low = jnp.where(lane == 0, 0.0, pltpu.roll(visc, 1, 1))
    return 0.5 * (visc + high), 0.5 * (visc + low)


def make_list(depth, breadth, slots_ref, list_ref):
    columns, length = slots_ref.shape[2], slots_ref.shape[4]
    pairs, listed = 9 * columns, list_ref.shape[1]
    rows = slots_ref[:, :, :, USED - 1 : USED, :].reshape(pairs, length)
    facts = jnp.transpose(rows)[0:8]
    number = lax.broadcasted_iota(jnp.int32, (1, pairs), 1)
    above = (number >= 3 * columns).astype(jnp.int32)
    below = (number >= 6 * columns).astype(jnp.int32)
    place = number - 3 * columns * (above + below)
    level = (place >= columns).astype(jnp.int32) + (place >= 2 * columns).astype(jnp.int32)
    shift_z = ((level - 1) * depth).astype(jnp.float32)
    shift_y = ((2 * below - above) * breadth).astype(jnp.float32)
    earlier = lax.broadcasted_iota(jnp.int32, (pairs, pairs), 0) < lax.broadcasted_iota(
        jnp.int32, (pairs, pairs), 1
    )
    earlier = earlier.astype(jnp.float32).astype(jnp.bfloat16)
    found = []
    for rank in range(CAP):
        z = facts[2 * rank : 2 * rank + 1] + shift_z
        y = facts[2 * rank + 1 : 2 * rank + 2] + shift_y
        meets = (z > -BOX) & (z < depth) & (y > -BOX) & (y < breadth)
        found.append((z, y, meets, jnp.where(meets, 1.0, 0.0)))
    both = found[0][3] + found[1][3]
    spot = jnp.dot(
        jnp.broadcast_to(both, (BOX, pairs)).astype(jnp.bfloat16), earlier,
        preferred_element_type=jnp.float32,
    )[0:1]
    entry = lax.broadcasted_iota(jnp.int32, (listed, pairs), 0).astype(jnp.float32)
    fact = lax.broadcasted_iota(jnp.int32, (BOX, pairs), 0)
    listing = jnp.zeros((BOX, listed), jnp.float32)
    for rank, (z, y, meets, one) in enumerate(found):
        mine = jnp.where(meets, spot + (found[0][3] if rank else 0.0), -1.0)
        chosen = jnp.where(entry == mine, 1.0, 0.0).astype(jnp.bfloat16)
        told = jnp.where(fact == 0, z, jnp.where(fact == 1, y, number.astype(jnp.float32)))
        told = jnp.where(meets, jnp.where(fact == 3, float(rank), told), 0.0).astype(jnp.bfloat16)
        listing = listing + lax.dot_general(
            told, chosen, (((1,), (1,)), ((), ())), preferred_element_type=jnp.float32
        )
    list_ref[0:4, :] = listing[0:4].astype(jnp.int32)
    total = jnp.sum(both, axis=1, keepdims=True)
    list_ref[4:8, :] = jnp.broadcast_to(total, (4, listed)).astype(jnp.int32)


def exchange_kernel(
    rows, columns, target_hbm, zoff_hbm, yoff_hbm, velocity_ref, viscosity_ref, frac_hbm, force_hbm,
    field_ref, slots_ref, list_ref,
    pad, once, staging, layers_out, layers_in, corner_out, corner_in,
    load_sem, ab_send, ab_recv, halo_send, halo_recv, corner_send, corner_recv, c_send, c_recv, known,
    target_ref, zoff_ref, yoff_ref, frac_ref, force_ref, small_sem,
):
    gz, xy = lax.axis_index("gz"), lax.axis_index("xy")
    depth, breadth = velocity_ref.shape[1], velocity_ref.shape[2]
    length = velocity_ref.shape[3]
    near, farther = staged_greeting(gz, xy, rows, columns, known)
    loads = (
        pltpu.make_async_copy(
            velocity_ref, pad.at[0:3, 2 : 2 + depth, 8 : 8 + breadth], load_sem.at[0]
        ),
        pltpu.make_async_copy(
            viscosity_ref, pad.at[3, 2 : 2 + depth, 8 : 8 + breadth], load_sem.at[1]
        ),
    )
    small = [
        pltpu.make_async_copy(source, place, small_sem.at[number])
        for number, (source, place) in enumerate((
            (target_hbm, target_ref), (zoff_hbm, zoff_ref), (yoff_hbm, yoff_ref),
            (frac_hbm, frac_ref), (force_hbm, force_ref),
        ))
    ]
    for load in small:
        load.start()
    for load in loads:
        load.start()

    lanes = lax.broadcasted_iota(jnp.int32, (1, length), 1)
    count = frac_ref.shape[1]

    def stage(column, unused):
        row = jnp.full((1, length), FAR, jnp.float32)
        for rank, block in enumerate(matches(target_ref, count, column)):
            at = jnp.maximum(block, 0)
            there = block >= 0
            z = jnp.where(there, zoff_ref[at].astype(jnp.float32), FAR)
            y = jnp.where(there, yoff_ref[at].astype(jnp.float32), FAR)
            staging[column, 6 * rank : 6 * rank + 3, :] = frac_ref[:, at, :]
            staging[column, 6 * rank + 3 : 6 * rank + 6, :] = force_ref[:, at, :]
            row = jnp.where(lanes == 2 * rank, z, row)
            row = jnp.where(lanes == 2 * rank + 1, y, row)
        staging[column, 12:13, :] = row
        return unused

    def block_copy(dr, column):
        return pltpu.make_async_remote_copy(
            src_ref=staging.at[column, 0:USED],
            dst_ref=slots_ref.at[0, 1 - dr, xy, 0:USED],
            send_sem=ab_send.at[dr + 1],
            recv_sem=ab_recv.at[1 - dr],
            device_id=(gz + dr, column),
            device_id_type=MESH,
        )

    def whole_row(dr):
        span = pl.ds(0, columns - (1 if dr == 0 else 0))
        return pltpu.make_async_remote_copy(
            src_ref=staging.at[span, 0:USED],
            dst_ref=slots_ref.at[0, dr + 1, span, 0:USED],
            send_sem=ab_send.at[dr + 1],
            recv_sem=ab_recv.at[dr + 1],
            device_id=(gz, xy),
            device_id_type=MESH,
        )

    for load in small:
        load.wait()
    lax.fori_loop(0, columns, stage, 0)
    near_peers = near()

    has = (gz > 0, gz < rows - 1, xy > 0, xy < columns - 1)
    device = ((gz - 1, xy), (gz + 1, xy), (gz, xy - 1), (gz, xy + 1))
    own_y = slice(8, 8 + breadth)
    own_z = slice(2, 2 + depth)

    def halo_copies(side):
        if side == 0:
            cut, land = slice(0, 2), (slice(2 + depth, 4 + depth), own_y)
        elif side == 1:
            cut, land = slice(depth - 2, depth), (slice(0, 2), own_y)
        if side < 2:
            sources = (velocity_ref.at[:, cut], viscosity_ref.at[cut])
            lands = (pad.at[(slice(0, 3),) + land], pad.at[(3,) + land])
        else:
            sources, lands = (layers_out.at[side - 2],), (layers_in.at[3 - side],)
        return [
            pltpu.make_async_remote_copy(
                src_ref=source,
                dst_ref=spot,
                send_sem=halo_send.at[side, number],
                recv_sem=halo_recv.at[side, number],
                device_id=device[side],
                device_id_type=MESH,
            )
            for number, (source, spot) in enumerate(zip(sources, lands))
        ]

    def on_side(side, action):
        @pl.when(has[side])
        def _():
            for copy in halo_copies(side):
                action(copy)


    near_peers(lambda dr, column: block_copy(dr, column).start())
    slots_ref[0, 1, xy, 0:USED] = staging[xy, 0:USED]


    wide, high = field_ref.shape[2], field_ref.shape[1]
    field_ref[:, 0:ZP] = jnp.zeros((3, ZP, wide, length), jnp.float32)
    field_ref[:, ZP + depth :] = jnp.zeros((3, high - ZP - depth, wide, length), jnp.float32)
    field_ref[:, ZP : ZP + depth, 0:YP] = jnp.zeros((3, depth, YP, length), jnp.float32)
    field_ref[:, ZP : ZP + depth, YP + breadth :] = jnp.zeros(
        (3, depth, wide - YP - breadth, length), jnp.float32
    )
    zeros_z = jnp.zeros((4, 2, breadth, length), jnp.float32)
    zeros_y = jnp.zeros((4, depth, 8, length), jnp.float32)

    @pl.when(gz == 0)
    def _():
        pad[:, 0:2, 8 : 8 + breadth, :] = zeros_z
        slots_ref[0, 0] = jnp.full(slots_ref.shape[2:], FAR, jnp.float32)

    @pl.when(gz == rows - 1)
    def _():
        pad[:, 2 + depth : 4 + depth, 8 : 8 + breadth, :] = zeros_z
        slots_ref[0, 2] = jnp.full(slots_ref.shape[2:], FAR, jnp.float32)

    @pl.when(xy == 0)
    def _():
        pad[:, 2 : 2 + depth, 0:8, :] = zeros_y
        slots_ref[1] = jnp.full(slots_ref.shape[1:], FAR, jnp.float32)

    @pl.when(xy == columns - 1)
    def _():
        pad[:, 2 : 2 + depth, 8 + breadth : 16 + breadth, :] = zeros_y
        slots_ref[2] = jnp.full(slots_ref.shape[1:], FAR, jnp.float32)

    for load in loads:
        load.wait()
    for side, start in ((2, 8), (3, 6 + breadth)):
        for part in range(4):
            for layer in range(2):
                layers_out[side - 2, part, layer * depth : (layer + 1) * depth, :] = pad[
                    part, 2 : 2 + depth, start + layer, :
                ]
        on_side(side, lambda copy: copy.start())

    corners = []
    for number, (dz, dy) in enumerate(((-1, -1), (-1, 1), (1, -1), (1, 1))):
        z_in = 2 if dz < 0 else 1 + depth
        y_in = 8 if dy < 0 else 7 + breadth
        z_out = 1 if dz < 0 else 2 + depth
        y_out = 7 if dy < 0 else 8 + breadth
        present = jnp.logical_and(has[0 if dz < 0 else 1], has[2 if dy < 0 else 3])
        for part in range(4):
            corner_out[number, part : part + 1, :] = pad[part, z_in, y_in : y_in + 1, :]
        copy = pltpu.make_async_remote_copy(
            src_ref=corner_out.at[number],
            dst_ref=corner_in.at[3 - number],
            send_sem=corner_send.at[number],
            recv_sem=corner_recv.at[3 - number],
            device_id=(gz + dz, xy + dy),
            device_id_type=MESH,
        )
        arrival = pltpu.make_async_remote_copy(
            src_ref=corner_out.at[number],
            dst_ref=corner_in.at[number],
            send_sem=corner_send.at[number],
            recv_sem=corner_recv.at[number],
            device_id=(gz + dz, xy + dy),
            device_id_type=MESH,
        )
        corners.append((present, copy, arrival, number, z_out, y_out))
    for present, copy, arrival, number, z_out, y_out in corners:
        pl.when(present)(lambda copy=copy: copy.start())

    @pl.when(gz % 2 == 1)
    def _():
        on_side(1, lambda copy: copy.start())

    on_side(0, lambda copy: copy.start())

    @pl.when(gz % 2 == 0)
    def _():
        on_side(1, lambda copy: copy.start())

    for far_peers in farther():
        far_peers(lambda dr, column: block_copy(dr, column).start())

    lane = lax.broadcasted_iota(jnp.int32, (breadth + 16, length), 1)
    line = lax.broadcasted_iota(jnp.int32, (breadth + 16, length), 0)
    low_y = jnp.where(xy > 0, 0, 8)
    high_y = jnp.where(xy < columns - 1, breadth + 16, breadth + 8)
    in_grid = jnp.logical_and(line >= low_y, line < high_y)
    first_z = jnp.where(gz > 0, 0, 2)
    last_z = jnp.where(gz < rows - 1, depth + 3, depth + 1)

    def first_sweep(z):
        visc = pad[3, z]
        size = visc.shape[0]
        cx_high, cx_low = x_coeffs(visc, lane)
        coeffs = (
            0.5 * (visc + pad[3, z + 1]),
            0.5 * (visc + pad[3, z - 1]),
            0.5 * (visc + pltpu.roll(visc, size - 1, 0)),
            0.5 * (visc + pltpu.roll(visc, 1, 0)),
            cx_high,
            cx_low,
        )
        z_inside = jnp.logical_and(z >= first_z, z <= last_z)
        keep = jnp.logical_and(in_grid, z_inside)
        for part in range(3):
            centre = pad[part, z]
            new = laplace(
                centre, visc, pad[part, z - 1], pad[part, z + 1],
                pltpu.roll(centre, 1, 0), pltpu.roll(centre, size - 1, 0), coeffs, lane,
            )
            once[part, z - 1] = jnp.where(keep, new, 0.0)

    own_lane = lane[:breadth]

    def second_sweep(z):
        visc = pad[3, z, 8 : 8 + breadth, :]
        cx_high, cx_low = x_coeffs(visc, own_lane)
        coeffs = (
            0.5 * (visc + pad[3, z + 1, 8 : 8 + breadth, :]),
            0.5 * (visc + pad[3, z - 1, 8 : 8 + breadth, :]),
            0.5 * (visc + pad[3, z, 9 : 9 + breadth, :]),
            0.5 * (visc + pad[3, z, 7 : 7 + breadth, :]),
            cx_high,
            cx_low,
        )
        for part in range(3):
            field_ref[part, z - 2 + ZP, YP : YP + breadth, :] = laplace(
                once[part, z - 1, 8 : 8 + breadth, :], visc,
                once[part, z - 2, 8 : 8 + breadth, :], once[part, z, 8 : 8 + breadth, :],
                once[part, z - 1, 7 : 7 + breadth, :], once[part, z - 1, 9 : 9 + breadth, :],
                coeffs, own_lane,
            )

    def loop(low, high, body):
        def step(z, unused):
            body(z)
            return unused

        lax.fori_loop(low, high, step, 0)

    arrives = ((1, 0), (0, 1), (3, 2), (2, 3))

    def wait_side(side, neighbour):
        @pl.when(has[neighbour])
        def _():
            for copy in halo_copies(side):
                copy.wait_recv()
            if side >= 2:
                start = 6 if side == 3 else 8 + breadth
                for part in range(4):
                    for layer in range(2):
                        pad[part, 2 : 2 + depth, start + layer, :] = layers_in[
                            3 - side, part, layer * depth : (layer + 1) * depth, :
                        ]

    forwards = []
    for number, (there, column, side) in enumerate(((has[3], xy + 1, 1), (has[2], xy - 1, 2))):
        for dr in (-1, 0, 1):
            copy = pltpu.make_async_remote_copy(
                src_ref=slots_ref.at[0, dr + 1, :, 0:USED],
                dst_ref=slots_ref.at[side, dr + 1, :, 0:USED],
                send_sem=c_send.at[number, dr + 1],
                recv_sem=c_recv.at[number, dr + 1],
                device_id=(gz, column),
                device_id_type=MESH,
            )
            forwards.append((there, copy, dr, has[2 + number]))

    def forward(row):
        for there, copy, dr, unused in forwards:
            if dr == row:
                pl.when(there)(lambda copy=copy: copy.start())

    wait_side(2, 3)
    wait_side(3, 2)
    loop(3, 1 + depth, first_sweep)
    whole_row(0).wait_recv()
    forward(0)
    middle = 4 + (depth - 4) // 2
    loop(4, middle, second_sweep)
    for dr in (-1, 1):
        pl.when(has[0 if dr < 0 else 1])(lambda dr=dr: whole_row(dr).wait_recv())
        forward(dr)
    loop(middle, depth, second_sweep)

    wait_side(0, 1)
    wait_side(1, 0)
    for present, copy, arrival, number, z_out, y_out in corners:

        @pl.when(present)
        def _(arrival=arrival, number=number, z_out=z_out, y_out=y_out):
            arrival.wait_recv()
            for part in range(4):
                pad[part, z_out, y_out : y_out + 1, :] = corner_in[number, part : part + 1, :]

        @pl.when(jnp.logical_not(present))
        def _(z_out=z_out, y_out=y_out):
            for part in range(4):
                pad[part, z_out, y_out : y_out + 1, :] = jnp.zeros((1, length), jnp.float32)

    for z in (1, 2, 1 + depth, 2 + depth):
        first_sweep(z)
    for z in (2, 3, depth, 1 + depth):
        second_sweep(z)

    for unused, copy, dr, comes in forwards:
        pl.when(comes)(lambda copy=copy: copy.wait_recv())
    make_list(depth, breadth, slots_ref, list_ref)
    each_row(gz, rows, lambda dr: whole_row(dr).wait_send())
    for side in range(4):
        on_side(side, lambda copy: copy.wait_send())
    for present, copy, arrival, number, z_out, y_out in corners:
        pl.when(present)(lambda copy=copy: copy.wait_send())
    for there, copy, unused, comes in forwards:
        pl.when(there)(lambda copy=copy: copy.wait_send())


def phi(radius):
    x2 = radius * radius * 0.6168502750680849
    c = 1.0 / 479001600.0
    for factor in (-1.0 / 3628800.0, 1.0 / 40320.0, -1.0 / 720.0, 1.0 / 24.0, -0.5, 1.0):
        c = c * x2 + factor
    return jnp.where(jnp.abs(radius) < 2.0, 0.5 * c * c, 0.0)


def split(value):
    high = value.astype(jnp.bfloat16)
    return high, (value - high.astype(jnp.float32)).astype(jnp.bfloat16)


def product(left, right, contract):
    (left_high, left_low), (right_high, right_low) = left, right
    return lax.dot_general(
        jnp.concatenate([left_high, left_low, left_high], axis=1),
        jnp.concatenate([right_high, right_high, right_low], axis=contract),
        (((1,), (contract,)), ((), ())),
        preferred_element_type=jnp.float32,
    )


def points_kernel(
    depth, breadth, list_ref, slots_ref, field_in, new_ref, partial_ref, field, wx_high, wx_low, near_held, store_sem
):
    length = field.shape[3]
    partial_ref[...] = jnp.zeros_like(partial_ref)
    found = list_ref[4, 0]
    whole = found // TOGETHER
    rest = found - whole * TOGETHER

    line = lax.broadcasted_iota(jnp.int32, (BOX, length), 0)
    rel = line.astype(jnp.float32)
    far = lax.broadcasted_iota(jnp.int32, (length, length), 0).astype(jnp.float32)

    def in_rounds(work):
        def some(number, unused):
            work(TOGETHER, number * TOGETHER)
            return unused

        def last(number, unused):
            work(FEW, whole * TOGETHER + number * FEW)
            return unused

        lax.fori_loop(0, whole, some, 0)
        lax.fori_loop(0, (rest + FEW - 1) // FEW, last, 0)

    def members(first, size):
        for other in range(size):
            at = first + other
            spot = jnp.minimum(at, found - 1)
            z, y, pair, rank = (list_ref[row, spot] for row in range(4))
            yield at, at < found, pair, rank, z, y

    def near_weights(frac, z, y):
        wz = phi(2.0 + (BOX - 5) * frac[0:1] - rel)
        wy = phi(2.0 + (BOX - 5) * frac[1:2] - rel)
        wz = jnp.where((z + line >= 0) & (z + line < depth), wz, 0.0)
        wy = jnp.where((y + line >= 0) & (y + line < breadth), wy, 0.0)
        return wz, wy

    def far_weights(frac):
        at = 2.0 + (length - 5) * frac
        near = at - rel
        base = phi(near - 4.0 * jnp.floor(0.25 * near + 0.5))
        high = base.astype(jnp.bfloat16).astype(jnp.float32)
        low = base - high
        inside = jnp.abs(at - far) < 2.0

        def spread_out(part):
            whole = jnp.broadcast_to(part[None], (length // BOX, BOX, length)).reshape(length, length)
            return jnp.where(inside, whole, 0.0).astype(jnp.bfloat16)

        return spread_out(high), spread_out(low)

    def box_of(z, y):
        return (slice(None), pl.ds(z + ZP, BOX), pl.ds(y + YP, BOX), slice(None))

    def spread(size, first):
        adds = []
        for at, counts, pair, rank, z, y in members(first, size):
            tile = slots_ref[pair, pl.ds(6 * rank, 6), :]
            wz, wy = near_weights(tile, z, y)
            near_held[at, 0], near_held[at, 1] = wz, wy
            wy = jnp.where(counts, wy, 0.0)
            wx = far_weights(tile[2:3])
            wx_high[at], wx_low[at] = wx
            pulled = tile[3:6][:, None, :] * wz[None]
            coeff = pulled[:, :, None, :] * wy[None, None]
            boxes = product(split(coeff.reshape(3 * BOX * BOX, length)), wx, 1)
            adds.append((box_of(z, y), boxes.reshape(3, BOX, BOX, length)))
        for box, boxes in adds:
            field[box] = field[box] + boxes

    in_rounds(spread)
    store = pltpu.make_async_copy(
        field.at[:, ZP : ZP + depth, YP : YP + breadth], new_ref, store_sem
    )
    store.start()

    def sample(size, first):
        results = []
        for at, counts, pair, rank, z, y in members(first, size):
            wz, wy = near_held[at, 0], near_held[at, 1]
            cells = field[box_of(z, y)].reshape(3 * BOX * BOX, length)
            taken = product(split(cells), (wx_high[at], wx_low[at]), 0)
            taken = taken.reshape(3, BOX, BOX, length)
            summed = jnp.sum(taken * wz[None, :, None, :], axis=1)
            results.append((pair, rank, jnp.sum(summed * wy[None], axis=1)))
        for pair, rank, values in results:
            partial_ref[pair, pl.ds(3 * rank, 3), :] = values

    in_rounds(sample)
    store.wait()


def return_kernel(
    rows, columns, target_hbm, partial_ref, out_ref,
    side_in, summed, gathered, c_send, c_recv, ab_send, ab_recv, known, target_ref, target_sem,
):
    gz, xy = lax.axis_index("gz"), lax.axis_index("xy")
    near, farther = staged_greeting(gz, xy, rows, columns, known)
    target_load = pltpu.make_async_copy(target_hbm, target_ref, target_sem)
    target_load.start()
    has_low, has_high = xy > 0, xy < columns - 1
    sides = ((has_low, xy - 1), (has_high, xy + 1))

    def side_copy(number, column, landing):
        return pltpu.make_async_remote_copy(
            src_ref=partial_ref.at[number + 1, :, :, 0:KEPT],
            dst_ref=side_in.at[landing, :, :, 0:KEPT],
            send_sem=c_send.at[number],
            recv_sem=c_recv.at[landing],
            device_id=(gz, column),
            device_id_type=MESH,
        )

    near_peers = near()
    for number, (there, column) in enumerate(sides):
        pl.when(there)(
            lambda number=number, column=column: side_copy(number, column, 1 - number).start()
        )

        @pl.when(jnp.logical_not(there))
        def _(number=number):
            side_in[number] = jnp.zeros(side_in.shape[1:], jnp.float32)

    def block_copy(dr, column):
        return pltpu.make_async_remote_copy(
            src_ref=summed.at[dr + 1, column, 0:KEPT],
            dst_ref=gathered.at[1 - dr, xy, 0:KEPT],
            send_sem=ab_send.at[dr + 1],
            recv_sem=ab_recv.at[1 - dr],
            device_id=(gz + dr, column),
            device_id_type=MESH,
        )

    def whole_row(dr):
        span = pl.ds(0, columns - (1 if dr == 0 else 0))
        return pltpu.make_async_remote_copy(
            src_ref=summed.at[dr + 1, span, 0:KEPT],
            dst_ref=gathered.at[dr + 1, span, 0:KEPT],
            send_sem=ab_send.at[dr + 1],
            recv_sem=ab_recv.at[dr + 1],
            device_id=(gz, xy),
            device_id_type=MESH,
        )

    @pl.when(gz == 0)
    def _():
        gathered[0] = jnp.zeros(gathered.shape[1:], jnp.float32)

    @pl.when(gz == rows - 1)
    def _():
        gathered[2] = jnp.zeros(gathered.shape[1:], jnp.float32)

    far_peers = list(farther())
    for number, (there, column) in enumerate(sides):
        pl.when(there)(
            lambda number=number, column=column: side_copy(number, column, number).wait_recv()
        )
    summed[:, :, 0:KEPT] = (
        partial_ref[0, :, :, 0:KEPT] + side_in[0, :, :, 0:KEPT] + side_in[1, :, :, 0:KEPT]
    )
    groups = far_peers[::-1] + [near_peers]
    for group in groups:
        group(lambda dr, column: block_copy(dr, column).start() if dr else None)
    for group in groups:
        group(lambda dr, column: None if dr else block_copy(dr, column).start())
    gathered[1, xy, 0:KEPT] = summed[1, xy, 0:KEPT]

    target_load.wait()
    count = out_ref.shape[1]
    ranks = []
    for j in range(count):
        rank = jnp.int32(0)
        for earlier in range(j):
            rank = rank + (target_ref[earlier] == target_ref[j]).astype(jnp.int32)
        ranks.append(rank)
    each_row(gz, rows, lambda dr: whole_row(dr).wait_recv())
    for j, rank in enumerate(ranks):
        column = target_ref[j]
        tile = gathered[0, column] + gathered[1, column] + gathered[2, column]
        out_ref[:, j, :] = jnp.where(rank == 0, tile[0:3], tile[3:KEPT])
    each_row(gz, rows, lambda dr: whole_row(dr).wait_send())
    for number, (there, column) in enumerate(sides):
        pl.when(there)(
            lambda number=number, column=column: side_copy(number, column, number).wait_send()
        )


def shards(rows, columns, velocity, viscosity, frac, force, target, z_offset, y_offset):
    parts, depth, breadth, length = velocity.shape
    target = target.reshape(target.shape[0])
    frac, force = jnp.transpose(frac, (1, 0, 2)), jnp.transpose(force, (1, 0, 2))
    held = lambda array: pltpu.with_memory_space_constraint(array, pltpu.HBM)
    velocity, viscosity, frac, force = held(velocity), held(viscosity), held(frac), held(force)
    target, z_offset, y_offset = held(target), held(z_offset), held(y_offset)
    f32 = jnp.float32
    vmem = pl.BlockSpec(memory_space=pltpu.VMEM)
    smem = pl.BlockSpec(memory_space=pltpu.SMEM)
    hbm = pl.BlockSpec(memory_space=pltpu.HBM)
    anyw = pl.BlockSpec(memory_space=pl.ANY)
    dma = pltpu.SemaphoreType.DMA
    pairs = 9 * columns
    listed = pl.cdiv(CAP * pairs, length) * length
    field_shape = (3, depth + 2 * ZP, breadth + 2 * YP, length)
    field, slots, listing = pl.pallas_call(
        functools.partial(exchange_kernel, rows, columns),
        out_shape=(
            jax.ShapeDtypeStruct(field_shape, f32),
            jax.ShapeDtypeStruct((3, 3, columns, PAIR, length), f32),
            jax.ShapeDtypeStruct((8, listed), jnp.int32),
        ),
        in_specs=[hbm] * 7,
        out_specs=(vmem, vmem, vmem),
        scratch_shapes=[
            pltpu.VMEM((4, depth + 4, breadth + 16, length), f32),
            pltpu.VMEM((3, depth + 2, breadth + 16, length), f32),
            pltpu.VMEM((columns, PAIR, length), f32),
            pltpu.VMEM((2, 4, 2 * depth, length), f32),
            pltpu.VMEM((2, 4, 2 * depth, length), f32),
            pltpu.VMEM((4, 8, length), f32),
            pltpu.VMEM((4, 8, length), f32),
            dma((2,)), dma((3,)), dma((3,)), dma((4, 2)), dma((4, 2)),
            dma((4,)), dma((4,)), dma((2, 3)), dma((2, 3)),
            known_shape(columns),
            pltpu.SMEM(target.shape, jnp.int32),
            pltpu.SMEM(target.shape, jnp.int32),
            pltpu.SMEM(target.shape, jnp.int32),
            pltpu.VMEM(frac.shape, f32),
            pltpu.VMEM(force.shape, f32),
            dma((5,)),
        ],
        compiler_params=pltpu.CompilerParams(
            collective_id=0, has_side_effects=True, vmem_limit_bytes=VMEM_LIMIT
        ),
    )(target, z_offset, y_offset, velocity, viscosity, frac, force)

    new_velocity, partial, unused = pl.pallas_call(
        functools.partial(points_kernel, depth, breadth),
        out_shape=(
            jax.ShapeDtypeStruct(velocity.shape, f32),
            jax.ShapeDtypeStruct((pairs, 8, length), f32),
            jax.ShapeDtypeStruct(field_shape, f32),
        ),
        in_specs=[smem, vmem, vmem],
        out_specs=(anyw, vmem, vmem),
        scratch_shapes=[
            pltpu.VMEM((CAP * pairs + TOGETHER, length, length), jnp.bfloat16),
            pltpu.VMEM((CAP * pairs + TOGETHER, length, length), jnp.bfloat16),
            pltpu.VMEM((CAP * pairs + TOGETHER, 2, BOX, length), f32),
            dma(()),
        ],
        input_output_aliases={2: 2},
        compiler_params=pltpu.CompilerParams(vmem_limit_bytes=VMEM_LIMIT),
    )(listing, slots.reshape(pairs, PAIR, length), field)

    point_velocity = pl.pallas_call(
        functools.partial(return_kernel, rows, columns),
        out_shape=jax.ShapeDtypeStruct(frac.shape, f32),
        in_specs=[hbm, vmem],
        out_specs=vmem,
        scratch_shapes=[
            pltpu.VMEM((2, 3, columns, 8, length), f32),
            pltpu.VMEM((3, columns, 8, length), f32),
            pltpu.VMEM((3, columns, 8, length), f32),
            dma((2,)), dma((2,)), dma((3,)), dma((3,)), known_shape(columns),
            pltpu.SMEM(target.shape, jnp.int32), dma(()),
        ],
        compiler_params=pltpu.CompilerParams(
            collective_id=1, has_side_effects=True, vmem_limit_bytes=VMEM_LIMIT
        ),
    )(target, partial.reshape(3, 3, columns, 8, length))
    return new_velocity, jnp.transpose(point_velocity, (1, 0, 2))


def solution(mesh):
    placed = (
        P(None, "gz", "xy", None),
        P("gz", "xy", None),
        P(("gz", "xy"), None, None),
        P(("gz", "xy"), None, None),
        P(("gz", "xy"), None),
        P(("gz", "xy")),
        P(("gz", "xy")),
    )
    return jax.shard_map(
        functools.partial(shards, mesh.shape["gz"], mesh.shape["xy"]),
        mesh=mesh,
        in_specs=placed,
        out_specs=(P(None, "gz", "xy", None), P(("gz", "xy"), None, None)),
        check_vma=False,
    )
```

```python
import functools

import jax
import jax.numpy as jnp
from jax import lax
from jax.experimental import pallas as pl
from jax.experimental.pallas import tpu as pltpu
from jax.sharding import PartitionSpec as P

BOX = 8
CAP = 2
FAR = 4096.0
ZP = 7
YP = 8
PAIR = 16
USED = 13
KEPT = 6
TOGETHER = 8
FEW = 4
CORES = 2
MESH = pl.DeviceIdType.MESH
VMEM_LIMIT = 24 * 1024 * 1024


def each_row(gz, rows, body):
    for dr in (-1, 0, 1):
        inside = jnp.logical_and(gz + dr >= 0, gz + dr < rows)
        pl.when(inside)(functools.partial(body, dr))


def chip_peers(gz, xy, rows, columns, steps):
    chip, core = xy // CORES, xy % CORES
    chips = columns // CORES

    def each(body):
        for step in steps:
            for dr in (0, -1, 1):
                there = (gz + dr >= 0) & (gz + dr < rows) & (chip + step >= 0) & (chip + step < chips)
                for turn in range(CORES):
                    if step == 0 and dr == 0 and turn == 0:
                        continue
                    other = core + turn
                    column = (chip + step) * CORES + jnp.where(other >= CORES, other - CORES, other)
                    pl.when(there)(functools.partial(body, dr, column))

    return each


def staged_greeting(gz, xy, rows, columns, known):
    chip, chips = xy // CORES, columns // CORES
    barrier = pltpu.get_barrier_semaphore()
    near_peers = chip_peers(gz, xy, rows, columns, (0, -1, 1))

    def signal_near(dr, column):
        pl.semaphore_signal(barrier, inc=1, device_id=(gz + dr, column), device_id_type=MESH)

    near_peers(signal_near)
    near_rows = 1 + (gz > 0).astype(jnp.int32) + (gz < rows - 1).astype(jnp.int32)
    near_chips = 1 + (chip > 0).astype(jnp.int32) + (chip < chips - 1).astype(jnp.int32)
    chain = ((chip < chips - 1, xy + CORES), (chip > 0, xy - CORES))

    def tell(reach):
        for number, (there, column) in enumerate(chain):
            pl.when(there)(
                lambda number=number, column=column: pl.semaphore_signal(
                    known.at[reach, number], inc=1, device_id=(gz, column), device_id_type=MESH
                )
            )

    def hear(reach):
        for number, (there, column) in enumerate(chain):
            pl.when(there)(lambda number=number: pl.semaphore_wait(known.at[reach, 1 - number], 1))

    def near():
        pl.semaphore_wait(barrier, near_rows * near_chips * CORES - 1)
        if chips > 2:
            tell(0)
        return near_peers

    def farther():
        for reach in range(chips - 2):
            hear(reach)
            if reach < chips - 3:
                tell(reach + 1)
            yield chip_peers(gz, xy, rows, columns, (-2 - reach, 2 + reach))

    return near, farther


def known_shape(columns):
    return pltpu.SemaphoreType.REGULAR((max(columns // CORES - 2, 1), 2))


def matches(target_ref, count, column):
    first, second = jnp.int32(-1), jnp.int32(-1)
    for j in range(count):
        hit = target_ref[j] == column
        second = jnp.where(jnp.logical_and(hit, jnp.logical_and(first >= 0, second < 0)), j, second)
        first = jnp.where(jnp.logical_and(hit, first < 0), j, first)
    return first, second


def laplace(centre, visc, z_low, z_high, y_low, y_high, coeffs, lane):
    length = centre.shape[-1]
    x_high = jnp.where(lane == length - 1, 0.0, pltpu.roll(centre, length - 1, 1))
    x_low = jnp.where(lane == 0, 0.0, pltpu.roll(centre, 1, 1))
    total = coeffs[0] * (z_high - centre) + coeffs[1] * (z_low - centre)
    total = total + coeffs[2] * (y_high - centre) + coeffs[3] * (y_low - centre)
    total = total + coeffs[4] * (x_high - centre) + coeffs[5] * (x_low - centre)
    return centre + 0.08 * total


def x_coeffs(visc, lane):
    length = visc.shape[-1]
    high = jnp.where(lane == length - 1, 0.0, pltpu.roll(visc, length - 1, 1))
    low = jnp.where(lane == 0, 0.0, pltpu.roll(visc, 1, 1))
    return 0.5 * (visc + high), 0.5 * (visc + low)


def make_list(depth, breadth, slots_ref, list_ref):
    columns, length = slots_ref.shape[2], slots_ref.shape[4]
    pairs, listed = 9 * columns, list_ref.shape[1]
    rows = slots_ref[:, :, :, USED - 1 : USED, :].reshape(pairs, length)
    facts = jnp.transpose(rows)[0:8]
    number = lax.broadcasted_iota(jnp.int32, (1, pairs), 1)
    above = (number >= 3 * columns).astype(jnp.int32)
    below = (number >= 6 * columns).astype(jnp.int32)
    place = number - 3 * columns * (above + below)
    level = (place >= columns).astype(jnp.int32) + (place >= 2 * columns).astype(jnp.int32)
    shift_z = ((level - 1) * depth).astype(jnp.float32)
    shift_y = ((2 * below - above) * breadth).astype(jnp.float32)
    earlier = lax.broadcasted_iota(jnp.int32, (pairs, pairs), 0) < lax.broadcasted_iota(
        jnp.int32, (pairs, pairs), 1
    )
    earlier = earlier.astype(jnp.float32).astype(jnp.bfloat16)
    found = []
    for rank in range(CAP):
        z = facts[2 * rank : 2 * rank + 1] + shift_z
        y = facts[2 * rank + 1 : 2 * rank + 2] + shift_y
        meets = (z > -BOX) & (z < depth) & (y > -BOX) & (y < breadth)
        found.append((z, y, meets, jnp.where(meets, 1.0, 0.0)))
    both = found[0][3] + found[1][3]
    spot = jnp.dot(
        jnp.broadcast_to(both, (BOX, pairs)).astype(jnp.bfloat16), earlier,
        preferred_element_type=jnp.float32,
    )[0:1]
    entry = lax.broadcasted_iota(jnp.int32, (listed, pairs), 0).astype(jnp.float32)
    fact = lax.broadcasted_iota(jnp.int32, (BOX, pairs), 0)
    listing = jnp.zeros((BOX, listed), jnp.float32)
    for rank, (z, y, meets, one) in enumerate(found):
        mine = jnp.where(meets, spot + (found[0][3] if rank else 0.0), -1.0)
        chosen = jnp.where(entry == mine, 1.0, 0.0).astype(jnp.bfloat16)
        told = jnp.where(fact == 0, z, jnp.where(fact == 1, y, number.astype(jnp.float32)))
        told = jnp.where(meets, jnp.where(fact == 3, float(rank), told), 0.0).astype(jnp.bfloat16)
        listing = listing + lax.dot_general(
            told, chosen, (((1,), (1,)), ((), ())), preferred_element_type=jnp.float32
        )
    list_ref[0:4, :] = listing[0:4].astype(jnp.int32)
    total = jnp.sum(both, axis=1, keepdims=True)
    list_ref[4:8, :] = jnp.broadcast_to(total, (4, listed)).astype(jnp.int32)


def exchange_kernel(
    rows, columns, target_hbm, zoff_hbm, yoff_hbm, velocity_ref, viscosity_ref, frac_hbm, force_hbm,
    field_ref, slots_ref, list_ref,
    pad, once, staging, layers_out, layers_in, corner_out, corner_in,
    load_sem, ab_send, ab_recv, halo_send, halo_recv, corner_send, corner_recv, c_send, c_recv, known,
    target_ref, zoff_ref, yoff_ref, frac_ref, force_ref, small_sem,
):
    gz, xy = lax.axis_index("gz"), lax.axis_index("xy")
    depth, breadth = velocity_ref.shape[1], velocity_ref.shape[2]
    length = velocity_ref.shape[3]
    near, farther = staged_greeting(gz, xy, rows, columns, known)
    loads = (
        pltpu.make_async_copy(
            velocity_ref, pad.at[0:3, 2 : 2 + depth, 8 : 8 + breadth], load_sem.at[0]
        ),
        pltpu.make_async_copy(
            viscosity_ref, pad.at[3, 2 : 2 + depth, 8 : 8 + breadth], load_sem.at[1]
        ),
    )
    small = [
        pltpu.make_async_copy(source, place, small_sem.at[number])
        for number, (source, place) in enumerate((
            (target_hbm, target_ref), (zoff_hbm, zoff_ref), (yoff_hbm, yoff_ref),
            (frac_hbm, frac_ref), (force_hbm, force_ref),
        ))
    ]
    for load in small:
        load.start()
    for load in loads:
        load.start()

    lanes = lax.broadcasted_iota(jnp.int32, (1, length), 1)
    count = frac_ref.shape[1]

    def stage(column, unused):
        row = jnp.full((1, length), FAR, jnp.float32)
        for rank, block in enumerate(matches(target_ref, count, column)):
            at = jnp.maximum(block, 0)
            there = block >= 0
            z = jnp.where(there, zoff_ref[at].astype(jnp.float32), FAR)
            y = jnp.where(there, yoff_ref[at].astype(jnp.float32), FAR)
            staging[column, 6 * rank : 6 * rank + 3, :] = frac_ref[:, at, :]
            staging[column, 6 * rank + 3 : 6 * rank + 6, :] = force_ref[:, at, :]
            row = jnp.where(lanes == 2 * rank, z, row)
            row = jnp.where(lanes == 2 * rank + 1, y, row)
        staging[column, 12:13, :] = row
        return unused

    def block_copy(dr, column):
        return pltpu.make_async_remote_copy(
            src_ref=staging.at[column, 0:USED],
            dst_ref=slots_ref.at[0, 1 - dr, xy, 0:USED],
            send_sem=ab_send.at[dr + 1],
            recv_sem=ab_recv.at[1 - dr],
            device_id=(gz + dr, column),
            device_id_type=MESH,
        )

    def whole_row(dr):
        span = pl.ds(0, columns - (1 if dr == 0 else 0))
        return pltpu.make_async_remote_copy(
            src_ref=staging.at[span, 0:USED],
            dst_ref=slots_ref.at[0, dr + 1, span, 0:USED],
            send_sem=ab_send.at[dr + 1],
            recv_sem=ab_recv.at[dr + 1],
            device_id=(gz, xy),
            device_id_type=MESH,
        )

    for load in small:
        load.wait()
    lax.fori_loop(0, columns, stage, 0)
    near_peers = near()

    has = (gz > 0, gz < rows - 1, xy > 0, xy < columns - 1)
    device = ((gz - 1, xy), (gz + 1, xy), (gz, xy - 1), (gz, xy + 1))
    own_y = slice(8, 8 + breadth)
    own_z = slice(2, 2 + depth)

    def halo_copies(side):
        if side == 0:
            cut, land = slice(0, 2), (slice(2 + depth, 4 + depth), own_y)
        elif side == 1:
            cut, land = slice(depth - 2, depth), (slice(0, 2), own_y)
        if side < 2:
            sources = (velocity_ref.at[:, cut], viscosity_ref.at[cut])
            lands = (pad.at[(slice(0, 3),) + land], pad.at[(3,) + land])
        else:
            sources, lands = (layers_out.at[side - 2],), (layers_in.at[3 - side],)
        return [
            pltpu.make_async_remote_copy(
                src_ref=source,
                dst_ref=spot,
                send_sem=halo_send.at[side, number],
                recv_sem=halo_recv.at[side, number],
                device_id=device[side],
                device_id_type=MESH,
            )
            for number, (source, spot) in enumerate(zip(sources, lands))
        ]

    def on_side(side, action):
        @pl.when(has[side])
        def _():
            for copy in halo_copies(side):
                action(copy)


    near_peers(lambda dr, column: block_copy(dr, column).start())
    slots_ref[0, 1, xy, 0:USED] = staging[xy, 0:USED]


    wide, high = field_ref.shape[2], field_ref.shape[1]
    field_ref[:, 0:ZP] = jnp.zeros((3, ZP, wide, length), jnp.float32)
    field_ref[:, ZP + depth :] = jnp.zeros((3, high - ZP - depth, wide, length), jnp.float32)
    field_ref[:, ZP : ZP + depth, 0:YP] = jnp.zeros((3, depth, YP, length), jnp.float32)
    field_ref[:, ZP : ZP + depth, YP + breadth :] = jnp.zeros(
        (3, depth, wide - YP - breadth, length), jnp.float32
    )
    zeros_z = jnp.zeros((4, 2, breadth, length), jnp.float32)
    zeros_y = jnp.zeros((4, depth, 8, length), jnp.float32)

    @pl.when(gz == 0)
    def _():
        pad[:, 0:2, 8 : 8 + breadth, :] = zeros_z
        slots_ref[0, 0] = jnp.full(slots_ref.shape[2:], FAR, jnp.float32)

    @pl.when(gz == rows - 1)
    def _():
        pad[:, 2 + depth : 4 + depth, 8 : 8 + breadth, :] = zeros_z
        slots_ref[0, 2] = jnp.full(slots_ref.shape[2:], FAR, jnp.float32)

    @pl.when(xy == 0)
    def _():
        pad[:, 2 : 2 + depth, 0:8, :] = zeros_y
        slots_ref[1] = jnp.full(slots_ref.shape[1:], FAR, jnp.float32)

    @pl.when(xy == columns - 1)
    def _():
        pad[:, 2 : 2 + depth, 8 + breadth : 16 + breadth, :] = zeros_y
        slots_ref[2] = jnp.full(slots_ref.shape[1:], FAR, jnp.float32)

    for load in loads:
        load.wait()
    for side, start in ((2, 8), (3, 6 + breadth)):
        for part in range(4):
            for layer in range(2):
                layers_out[side - 2, part, layer * depth : (layer + 1) * depth, :] = pad[
                    part, 2 : 2 + depth, start + layer, :
                ]
        on_side(side, lambda copy: copy.start())

    corners = []
    for number, (dz, dy) in enumerate(((-1, -1), (-1, 1), (1, -1), (1, 1))):
        z_in = 2 if dz < 0 else 1 + depth
        y_in = 8 if dy < 0 else 7 + breadth
        z_out = 1 if dz < 0 else 2 + depth
        y_out = 7 if dy < 0 else 8 + breadth
        present = jnp.logical_and(has[0 if dz < 0 else 1], has[2 if dy < 0 else 3])
        for part in range(4):
            corner_out[number, part : part + 1, :] = pad[part, z_in, y_in : y_in + 1, :]
        copy = pltpu.make_async_remote_copy(
            src_ref=corner_out.at[number],
            dst_ref=corner_in.at[3 - number],
            send_sem=corner_send.at[number],
            recv_sem=corner_recv.at[3 - number],
            device_id=(gz + dz, xy + dy),
            device_id_type=MESH,
        )
        arrival = pltpu.make_async_remote_copy(
            src_ref=corner_out.at[number],
            dst_ref=corner_in.at[number],
            send_sem=corner_send.at[number],
            recv_sem=corner_recv.at[number],
            device_id=(gz + dz, xy + dy),
            device_id_type=MESH,
        )
        corners.append((present, copy, arrival, number, z_out, y_out))
    for present, copy, arrival, number, z_out, y_out in corners:
        pl.when(present)(lambda copy=copy: copy.start())

    @pl.when((gz % 2 == 1) & has[0] & has[1])
    def _():
        for number in (0, 1):
            for side in (1, 0):
                halo_copies(side)[number].start()

    @pl.when((gz % 2 == 0) | jnp.logical_not(has[0] & has[1]))
    def _():
        for side in (0, 1):
            on_side(side, lambda copy: copy.start())

    for far_peers in farther():
        far_peers(lambda dr, column: block_copy(dr, column).start())

    lane = lax.broadcasted_iota(jnp.int32, (breadth + 16, length), 1)
    line = lax.broadcasted_iota(jnp.int32, (breadth + 16, length), 0)
    low_y = jnp.where(xy > 0, 0, 8)
    high_y = jnp.where(xy < columns - 1, breadth + 16, breadth + 8)
    in_grid = jnp.logical_and(line >= low_y, line < high_y)
    first_z = jnp.where(gz > 0, 0, 2)
    last_z = jnp.where(gz < rows - 1, depth + 3, depth + 1)

    def first_sweep(z):
        visc = pad[3, z]
        size = visc.shape[0]
        cx_high, cx_low = x_coeffs(visc, lane)
        coeffs = (
            0.5 * (visc + pad[3, z + 1]),
            0.5 * (visc + pad[3, z - 1]),
            0.5 * (visc + pltpu.roll(visc, size - 1, 0)),
            0.5 * (visc + pltpu.roll(visc, 1, 0)),
            cx_high,
            cx_low,
        )
        z_inside = jnp.logical_and(z >= first_z, z <= last_z)
        keep = jnp.logical_and(in_grid, z_inside)
        for part in range(3):
            centre = pad[part, z]
            new = laplace(
                centre, visc, pad[part, z - 1], pad[part, z + 1],
                pltpu.roll(centre, 1, 0), pltpu.roll(centre, size - 1, 0), coeffs, lane,
            )
            once[part, z - 1] = jnp.where(keep, new, 0.0)

    own_lane = lane[:breadth]

    def second_sweep(z):
        visc = pad[3, z, 8 : 8 + breadth, :]
        cx_high, cx_low = x_coeffs(visc, own_lane)
        coeffs = (
            0.5 * (visc + pad[3, z + 1, 8 : 8 + breadth, :]),
            0.5 * (visc + pad[3, z - 1, 8 : 8 + breadth, :]),
            0.5 * (visc + pad[3, z, 9 : 9 + breadth, :]),
            0.5 * (visc + pad[3, z, 7 : 7 + breadth, :]),
            cx_high,
            cx_low,
        )
        for part in range(3):
            field_ref[part, z - 2 + ZP, YP : YP + breadth, :] = laplace(
                once[part, z - 1, 8 : 8 + breadth, :], visc,
                once[part, z - 2, 8 : 8 + breadth, :], once[part, z, 8 : 8 + breadth, :],
                once[part, z - 1, 7 : 7 + breadth, :], once[part, z - 1, 9 : 9 + breadth, :],
                coeffs, own_lane,
            )

    def loop(low, high, body):
        def step(z, unused):
            body(z)
            return unused

        lax.fori_loop(low, high, step, 0)

    arrives = ((1, 0), (0, 1), (3, 2), (2, 3))

    def wait_side(side, neighbour):
        @pl.when(has[neighbour])
        def _():
            for copy in halo_copies(side):
                copy.wait_recv()
            if side >= 2:
                start = 6 if side == 3 else 8 + breadth
                for part in range(4):
                    for layer in range(2):
                        pad[part, 2 : 2 + depth, start + layer, :] = layers_in[
                            3 - side, part, layer * depth : (layer + 1) * depth, :
                        ]

    forwards = []
    for number, (there, column, side) in enumerate(((has[3], xy + 1, 1), (has[2], xy - 1, 2))):
        for dr in (-1, 0, 1):
            copy = pltpu.make_async_remote_copy(
                src_ref=slots_ref.at[0, dr + 1, :, 0:USED],
                dst_ref=slots_ref.at[side, dr + 1, :, 0:USED],
                send_sem=c_send.at[number, dr + 1],
                recv_sem=c_recv.at[number, dr + 1],
                device_id=(gz, column),
                device_id_type=MESH,
            )
            forwards.append((there, copy, dr, has[2 + number]))

    def forward(row):
        for there, copy, dr, unused in forwards:
            if dr == row:
                pl.when(there)(lambda copy=copy: copy.start())

    wait_side(2, 3)
    wait_side(3, 2)
    loop(3, 1 + depth, first_sweep)
    whole_row(0).wait_recv()
    forward(0)
    middle = 4 + (depth - 4) // 2
    loop(4, middle, second_sweep)
    for dr in (-1, 1):
        pl.when(has[0 if dr < 0 else 1])(lambda dr=dr: whole_row(dr).wait_recv())
        forward(dr)
    loop(middle, depth, second_sweep)

    wait_side(0, 1)
    wait_side(1, 0)
    for present, copy, arrival, number, z_out, y_out in corners:

        @pl.when(present)
        def _(arrival=arrival, number=number, z_out=z_out, y_out=y_out):
            arrival.wait_recv()
            for part in range(4):
                pad[part, z_out, y_out : y_out + 1, :] = corner_in[number, part : part + 1, :]

        @pl.when(jnp.logical_not(present))
        def _(z_out=z_out, y_out=y_out):
            for part in range(4):
                pad[part, z_out, y_out : y_out + 1, :] = jnp.zeros((1, length), jnp.float32)

    for z in (1, 2, 1 + depth, 2 + depth):
        first_sweep(z)
    for z in (2, 3, depth, 1 + depth):
        second_sweep(z)

    for unused, copy, dr, comes in forwards:
        pl.when(comes)(lambda copy=copy: copy.wait_recv())
    make_list(depth, breadth, slots_ref, list_ref)
    each_row(gz, rows, lambda dr: whole_row(dr).wait_send())
    for side in range(4):
        on_side(side, lambda copy: copy.wait_send())
    for present, copy, arrival, number, z_out, y_out in corners:
        pl.when(present)(lambda copy=copy: copy.wait_send())
    for there, copy, unused, comes in forwards:
        pl.when(there)(lambda copy=copy: copy.wait_send())


def phi(radius):
    x2 = radius * radius * 0.6168502750680849
    c = 1.0 / 479001600.0
    for factor in (-1.0 / 3628800.0, 1.0 / 40320.0, -1.0 / 720.0, 1.0 / 24.0, -0.5, 1.0):
        c = c * x2 + factor
    return jnp.where(jnp.abs(radius) < 2.0, 0.5 * c * c, 0.0)


def split(value):
    high = value.astype(jnp.bfloat16)
    return high, (value - high.astype(jnp.float32)).astype(jnp.bfloat16)


def product(left, right, contract):
    (left_high, left_low), (right_high, right_low) = left, right
    return lax.dot_general(
        jnp.concatenate([left_high, left_low, left_high], axis=1),
        jnp.concatenate([right_high, right_high, right_low], axis=contract),
        (((1,), (contract,)), ((), ())),
        preferred_element_type=jnp.float32,
    )


def points_kernel(
    depth, breadth, list_ref, slots_ref, field_in, new_ref, partial_ref, field, wx_high, wx_low, near_held, store_sem
):
    length = field.shape[3]
    partial_ref[...] = jnp.zeros_like(partial_ref)
    found = list_ref[4, 0]
    whole = found // TOGETHER
    rest = found - whole * TOGETHER

    line = lax.broadcasted_iota(jnp.int32, (BOX, length), 0)
    rel = line.astype(jnp.float32)
    far = lax.broadcasted_iota(jnp.int32, (length, length), 0).astype(jnp.float32)

    def in_rounds(work):
        def some(number, unused):
            work(TOGETHER, number * TOGETHER)
            return unused

        def last(number, unused):
            work(FEW, whole * TOGETHER + number * FEW)
            return unused

        lax.fori_loop(0, whole, some, 0)
        lax.fori_loop(0, (rest + FEW - 1) // FEW, last, 0)

    def members(first, size):
        for other in range(size):
            at = first + other
            spot = jnp.minimum(at, found - 1)
            z, y, pair, rank = (list_ref[row, spot] for row in range(4))
            yield at, at < found, pair, rank, z, y

    def near_weights(frac, z, y):
        wz = phi(2.0 + (BOX - 5) * frac[0:1] - rel)
        wy = phi(2.0 + (BOX - 5) * frac[1:2] - rel)
        wz = jnp.where((z + line >= 0) & (z + line < depth), wz, 0.0)
        wy = jnp.where((y + line >= 0) & (y + line < breadth), wy, 0.0)
        return wz, wy

    def far_weights(frac):
        at = 2.0 + (length - 5) * frac
        near = at - rel
        base = phi(near - 4.0 * jnp.floor(0.25 * near + 0.5))
        high = base.astype(jnp.bfloat16).astype(jnp.float32)
        low = base - high
        inside = jnp.abs(at - far) < 2.0

        def spread_out(part):
            whole = jnp.broadcast_to(part[None], (length // BOX, BOX, length)).reshape(length, length)
            return jnp.where(inside, whole, 0.0).astype(jnp.bfloat16)

        return spread_out(high), spread_out(low)

    def box_of(z, y):
        return (slice(None), pl.ds(z + ZP, BOX), pl.ds(y + YP, BOX), slice(None))

    def spread(size, first):
        adds = []
        for at, counts, pair, rank, z, y in members(first, size):
            tile = slots_ref[pair, pl.ds(6 * rank, 6), :]
            wz, wy = near_weights(tile, z, y)
            near_held[at, 0], near_held[at, 1] = wz, wy
            wy = jnp.where(counts, wy, 0.0)
            wx = far_weights(tile[2:3])
            wx_high[at], wx_low[at] = wx
            pulled = tile[3:6][:, None, :] * wz[None]
            coeff = pulled[:, :, None, :] * wy[None, None]
            boxes = product(split(coeff.reshape(3 * BOX * BOX, length)), wx, 1)
            adds.append((box_of(z, y), boxes.reshape(3, BOX, BOX, length)))
        for box, boxes in adds:
            field[box] = field[box] + boxes

    in_rounds(spread)
    store = pltpu.make_async_copy(
        field.at[:, ZP : ZP + depth, YP : YP + breadth], new_ref, store_sem
    )
    store.start()

    def sample(size, first):
        results = []
        for at, counts, pair, rank, z, y in members(first, size):
            wz, wy = near_held[at, 0], near_held[at, 1]
            cells = field[box_of(z, y)].reshape(3 * BOX * BOX, length)
            taken = product(split(cells), (wx_high[at], wx_low[at]), 0)
            taken = taken.reshape(3, BOX, BOX, length)
            summed = jnp.sum(taken * wz[None, :, None, :], axis=1)
            results.append((pair, rank, jnp.sum(summed * wy[None], axis=1)))
        for pair, rank, values in results:
            partial_ref[pair, pl.ds(3 * rank, 3), :] = values

    in_rounds(sample)
    store.wait()


def return_kernel(
    rows, columns, target_hbm, partial_ref, out_ref,
    side_in, summed, gathered, c_send, c_recv, ab_send, ab_recv, known, target_ref, target_sem,
):
    gz, xy = lax.axis_index("gz"), lax.axis_index("xy")
    near, farther = staged_greeting(gz, xy, rows, columns, known)
    target_load = pltpu.make_async_copy(target_hbm, target_ref, target_sem)
    target_load.start()
    has_low, has_high = xy > 0, xy < columns - 1
    sides = ((has_low, xy - 1), (has_high, xy + 1))

    def side_copy(number, column, landing):
        return pltpu.make_async_remote_copy(
            src_ref=partial_ref.at[number + 1, :, :, 0:KEPT],
            dst_ref=side_in.at[landing, :, :, 0:KEPT],
            send_sem=c_send.at[number],
            recv_sem=c_recv.at[landing],
            device_id=(gz, column),
            device_id_type=MESH,
        )

    near_peers = near()
    for number, (there, column) in enumerate(sides):
        pl.when(there)(
            lambda number=number, column=column: side_copy(number, column, 1 - number).start()
        )

        @pl.when(jnp.logical_not(there))
        def _(number=number):
            side_in[number] = jnp.zeros(side_in.shape[1:], jnp.float32)

    def block_copy(dr, column):
        return pltpu.make_async_remote_copy(
            src_ref=summed.at[dr + 1, column, 0:KEPT],
            dst_ref=gathered.at[1 - dr, xy, 0:KEPT],
            send_sem=ab_send.at[dr + 1],
            recv_sem=ab_recv.at[1 - dr],
            device_id=(gz + dr, column),
            device_id_type=MESH,
        )

    def whole_row(dr):
        span = pl.ds(0, columns - (1 if dr == 0 else 0))
        return pltpu.make_async_remote_copy(
            src_ref=summed.at[dr + 1, span, 0:KEPT],
            dst_ref=gathered.at[dr + 1, span, 0:KEPT],
            send_sem=ab_send.at[dr + 1],
            recv_sem=ab_recv.at[dr + 1],
            device_id=(gz, xy),
            device_id_type=MESH,
        )

    @pl.when(gz == 0)
    def _():
        gathered[0] = jnp.zeros(gathered.shape[1:], jnp.float32)

    @pl.when(gz == rows - 1)
    def _():
        gathered[2] = jnp.zeros(gathered.shape[1:], jnp.float32)

    far_peers = list(farther())
    for number, (there, column) in enumerate(sides):
        pl.when(there)(
            lambda number=number, column=column: side_copy(number, column, number).wait_recv()
        )
    summed[:, :, 0:KEPT] = (
        partial_ref[0, :, :, 0:KEPT] + side_in[0, :, :, 0:KEPT] + side_in[1, :, :, 0:KEPT]
    )
    groups = far_peers[::-1] + [near_peers]
    for group in groups:
        group(lambda dr, column: block_copy(dr, column).start() if dr else None)
    for group in groups:
        group(lambda dr, column: None if dr else block_copy(dr, column).start())
    gathered[1, xy, 0:KEPT] = summed[1, xy, 0:KEPT]

    target_load.wait()
    count = out_ref.shape[1]
    ranks = []
    for j in range(count):
        rank = jnp.int32(0)
        for earlier in range(j):
            rank = rank + (target_ref[earlier] == target_ref[j]).astype(jnp.int32)
        ranks.append(rank)
    each_row(gz, rows, lambda dr: whole_row(dr).wait_recv())
    for j, rank in enumerate(ranks):
        column = target_ref[j]
        tile = gathered[0, column] + gathered[1, column] + gathered[2, column]
        out_ref[:, j, :] = jnp.where(rank == 0, tile[0:3], tile[3:KEPT])
    each_row(gz, rows, lambda dr: whole_row(dr).wait_send())
    for number, (there, column) in enumerate(sides):
        pl.when(there)(
            lambda number=number, column=column: side_copy(number, column, number).wait_send()
        )


def shards(rows, columns, velocity, viscosity, frac, force, target, z_offset, y_offset):
    parts, depth, breadth, length = velocity.shape
    target = target.reshape(target.shape[0])
    frac, force = jnp.transpose(frac, (1, 0, 2)), jnp.transpose(force, (1, 0, 2))
    held = lambda array: pltpu.with_memory_space_constraint(array, pltpu.HBM)
    velocity, viscosity, frac, force = held(velocity), held(viscosity), held(frac), held(force)
    target, z_offset, y_offset = held(target), held(z_offset), held(y_offset)
    f32 = jnp.float32
    vmem = pl.BlockSpec(memory_space=pltpu.VMEM)
    smem = pl.BlockSpec(memory_space=pltpu.SMEM)
    hbm = pl.BlockSpec(memory_space=pltpu.HBM)
    anyw = pl.BlockSpec(memory_space=pl.ANY)
    dma = pltpu.SemaphoreType.DMA
    pairs = 9 * columns
    listed = pl.cdiv(CAP * pairs, length) * length
    field_shape = (3, depth + 2 * ZP, breadth + 2 * YP, length)
    field, slots, listing = pl.pallas_call(
        functools.partial(exchange_kernel, rows, columns),
        out_shape=(
            jax.ShapeDtypeStruct(field_shape, f32),
            jax.ShapeDtypeStruct((3, 3, columns, PAIR, length), f32),
            jax.ShapeDtypeStruct((8, listed), jnp.int32),
        ),
        in_specs=[hbm] * 7,
        out_specs=(vmem, vmem, vmem),
        scratch_shapes=[
            pltpu.VMEM((4, depth + 4, breadth + 16, length), f32),
            pltpu.VMEM((3, depth + 2, breadth + 16, length), f32),
            pltpu.VMEM((columns, PAIR, length), f32),
            pltpu.VMEM((2, 4, 2 * depth, length), f32),
            pltpu.VMEM((2, 4, 2 * depth, length), f32),
            pltpu.VMEM((4, 8, length), f32),
            pltpu.VMEM((4, 8, length), f32),
            dma((2,)), dma((3,)), dma((3,)), dma((4, 2)), dma((4, 2)),
            dma((4,)), dma((4,)), dma((2, 3)), dma((2, 3)),
            known_shape(columns),
            pltpu.SMEM(target.shape, jnp.int32),
            pltpu.SMEM(target.shape, jnp.int32),
            pltpu.SMEM(target.shape, jnp.int32),
            pltpu.VMEM(frac.shape, f32),
            pltpu.VMEM(force.shape, f32),
            dma((5,)),
        ],
        compiler_params=pltpu.CompilerParams(
            collective_id=0, has_side_effects=True, vmem_limit_bytes=VMEM_LIMIT
        ),
    )(target, z_offset, y_offset, velocity, viscosity, frac, force)

    new_velocity, partial, unused = pl.pallas_call(
        functools.partial(points_kernel, depth, breadth),
        out_shape=(
            jax.ShapeDtypeStruct(velocity.shape, f32),
            jax.ShapeDtypeStruct((pairs, 8, length), f32),
            jax.ShapeDtypeStruct(field_shape, f32),
        ),
        in_specs=[smem, vmem, vmem],
        out_specs=(anyw, vmem, vmem),
        scratch_shapes=[
            pltpu.VMEM((CAP * pairs + TOGETHER, length, length), jnp.bfloat16),
            pltpu.VMEM((CAP * pairs + TOGETHER, length, length), jnp.bfloat16),
            pltpu.VMEM((CAP * pairs + TOGETHER, 2, BOX, length), f32),
            dma(()),
        ],
        input_output_aliases={2: 2},
        compiler_params=pltpu.CompilerParams(vmem_limit_bytes=VMEM_LIMIT),
    )(listing, slots.reshape(pairs, PAIR, length), field)

    point_velocity = pl.pallas_call(
        functools.partial(return_kernel, rows, columns),
        out_shape=jax.ShapeDtypeStruct(frac.shape, f32),
        in_specs=[hbm, vmem],
        out_specs=vmem,
        scratch_shapes=[
            pltpu.VMEM((2, 3, columns, 8, length), f32),
            pltpu.VMEM((3, columns, 8, length), f32),
            pltpu.VMEM((3, columns, 8, length), f32),
            dma((2,)), dma((2,)), dma((3,)), dma((3,)), known_shape(columns),
            pltpu.SMEM(target.shape, jnp.int32), dma(()),
        ],
        compiler_params=pltpu.CompilerParams(
            collective_id=1, has_side_effects=True, vmem_limit_bytes=VMEM_LIMIT
        ),
    )(target, partial.reshape(3, 3, columns, 8, length))
    return new_velocity, jnp.transpose(point_velocity, (1, 0, 2))


def solution(mesh):
    placed = (
        P(None, "gz", "xy", None),
        P("gz", "xy", None),
        P(("gz", "xy"), None, None),
        P(("gz", "xy"), None, None),
        P(("gz", "xy"), None),
        P(("gz", "xy")),
        P(("gz", "xy")),
    )
    return jax.shard_map(
        functools.partial(shards, mesh.shape["gz"], mesh.shape["xy"]),
        mesh=mesh,
        in_specs=placed,
        out_specs=(P(None, "gz", "xy", None), P(("gz", "xy"), None, None)),
        check_vma=False,
    )
```
